128 devices in a mesh: row: 8 (over y, x_hi), col: 16 (over x_lo, z, core).
Axes of the slice: x: 4 (x_hi: 2, x_lo: 2; x = x_hi * 2 + x_lo), y: 4, z: 4, core: 2. Of those that a mesh axis runs over, the one named last changes fastest.
Arguments:
- tokens: bfloat16 [1024, 6144], P('row', 'col'), may hold values from -6 to 6
- cotangent: bfloat16 [1024, 6144], P('row', 'col'), may hold values from -6 to 6
- w_in: bfloat16 [6144, 24576], P('col', 'row'), may hold values from -0.078125 to 0.078125
- w_out: bfloat16 [24576, 6144], P('row', 'col'), may hold values from -0.0390625 to 0.0390625
Outputs:
- input_grad: bfloat16 [1024, 6144], P('row', 'col')
- w_in_grad: bfloat16 [6144, 24576], P('col', 'row')
- w_out_grad: bfloat16 [24576, 6144], P('row', 'col')
The draws below stay inside these ranges and needn't reach their ends.
All inputs are finite; a program needn't handle non-finite values.
Results may differ from the reference program's by a relative error of at most 0.0049.
Values may be sent and summed in bfloat16 or wider, within the bound.
No kernel may reach another device: no remote copies, remote signals or barrier semaphores. Data moves between devices by JAX's collectives and lax.ppermute only.
A program may use at most 128 MiB of HBM per device.

```python
import jax
import jax.numpy as jnp
from jax import lax

D = 6144
FF = 24576
TOKENS = 1024


def block_levels(stream_key, extent, split, low, high):
    factor_of, own = 1.0, jax.random.fold_in(stream_key, 6)
    for dim, parts in split:
        draws = jnp.exp(jax.random.uniform(jax.random.fold_in(own, dim), (parts,), jnp.float32, low / len(split), high / len(split)))
        factor_of = factor_of * jnp.repeat(draws, extent[dim] // parts).reshape([-1 if axis == dim else 1 for axis in range(len(extent))])
    return factor_of


def normal_values(own_key, extent, width, limit, pieces=(), kind=jnp.bfloat16):
    values = width * jax.random.normal(own_key, extent, jnp.float32)
    if pieces:
        values = values * block_levels(own_key, extent, pieces, -0.22, 0.18)
    return jnp.clip(values, -limit, limit).astype(kind)


def setup_inputs(seed: int = 0) -> dict:
    keys = jax.random.split(jax.random.key(seed), 5)
    tokens = normal_values(keys[0], (TOKENS, D), 1.0, 6.0, ((0, 8), (1, 16)))
    cotangent = normal_values(keys[1], (TOKENS, D), 1.0, 6.0, ((0, 8), (1, 16)))
    w_in = normal_values(keys[2], (D, FF), D ** -0.5, 0.078125, ((0, 16), (1, 8)))
    w_out = normal_values(keys[3], (FF, D), FF ** -0.5, 0.0390625, ((0, 8), (1, 16)))
    return {"tokens": tokens, "cotangent": cotangent, "w_in": w_in, "w_out": w_out}


def reference(tokens, cotangent, w_in, w_out):
    pre = jnp.dot(tokens, w_in, preferred_element_type=jnp.float32)
    cdf = 0.5 * (1.0 + lax.erf(pre * 0.7071067811865476))
    pdf = jnp.exp(-0.5 * pre * pre) * 0.3989422804014327
    act = (pre * cdf).astype(jnp.bfloat16)
    act_grad = jnp.dot(cotangent, w_out.T, preferred_element_type=jnp.float32)
    pre_grad = (act_grad * (cdf + pre * pdf)).astype(jnp.bfloat16)
    input_grad = jnp.dot(pre_grad, w_in.T, preferred_element_type=jnp.float32).astype(jnp.bfloat16)
    w_in_grad = jnp.dot(tokens.T, pre_grad, preferred_element_type=jnp.float32).astype(jnp.bfloat16)
    w_out_grad = jnp.dot(act.T, cotangent, preferred_element_type=jnp.float32).astype(jnp.bfloat16)
    return input_grad, w_in_grad, w_out_grad
```

```python
import jax
import jax.numpy as jnp
from jax import lax
from jax.sharding import Mesh
from jax.sharding import PartitionSpec as P

AXES = ("y", "xh", "xl", "z", "core")
SIZES = (4, 2, 2, 4, 2)
ROWS = ("y", "xh")
COLS = ("xl", "z", "core")
F32 = jnp.float32
BF16 = jnp.bfloat16


def gelu_parts(pre):
    cdf = 0.5 * (1.0 + lax.erf(pre * 0.7071067811865476))
    pdf = jnp.exp(-0.5 * pre * pre) * 0.3989422804014327
    return (cdf, pdf)


def shift(x, axis, by):
    n = SIZES[AXES.index(axis)]
    return lax.ppermute(x, axis, [(i, (i + by) % n) for i in range(n)])


def dot(a, b, da, db):
    return lax.dot_general(a, b, (((da,), (db,)), ((), ())), preferred_element_type=F32)


def swap_halves(first, second, flag, axis):
    return jnp.concatenate([jnp.where(flag == 0, first, second), jnp.where(flag == 0, second, first)], axis)


def local(tokens, cotangent, w_in, w_out):
    z, xl, core = lax.axis_index("z"), lax.axis_index("xl"), lax.axis_index("core")
    rows, feat = tokens.shape
    hid = w_in.shape[1] // 2
    piece = rows // 8

    def relative(a, sign):
        a = a.reshape(4, 2, piece, a.shape[-1])
        return jnp.roll(jnp.roll(a, sign * z, 0), sign * xl, 1)

    own = relative(jnp.concatenate([tokens, cotangent], 1), -1)

    near = jnp.stack([own, shift(own, "y", -1), shift(own, "y", -2), shift(own, "y", -3)])
    near = near.transpose(1, 2, 0, 3, 4).reshape(rows * 4, 2 * feat)
    far = shift(near, "xh", 1)

    def core_weights(w, axis):
        keep = lax.dynamic_slice_in_dim(w, core * hid, hid, axis)
        send = lax.dynamic_slice_in_dim(w, (1 - core) * hid, hid, axis)
        return jnp.concatenate([keep, shift(send, "core", 1)], 1 - axis)

    wi = core_weights(w_in, 1)
    wo = core_weights(w_out, 0)

    def chip_features(a):
        b = shift(a, "core", 1)
        return (
            jnp.concatenate([a[:, :feat], b[:, :feat]], 1),
            jnp.concatenate([a[:, feat:], b[:, feat:]], 1),
        )

    def hidden(tok, cot):
        tok4, cot4 = tok.reshape(4, rows, -1), cot.reshape(4, rows, -1)
        pre = lambda k: dot(tok4[k], wi, 1, 0)
        grad = lambda k: dot(cot4[k], wo, 1, 1)
        cat = lambda p, g: jnp.concatenate([p.astype(BF16), g.astype(BF16)], 1)
        up = shift(pre(2).astype(BF16), "z", 1)
        down = shift(grad(2).astype(BF16), "z", -1)
        up = shift(cat(pre(1) + up.astype(F32), grad(1)), "z", 1)
        down = shift(cat(pre(3), grad(3) + down.astype(F32)), "z", -1)
        p = pre(0) + up[:, :hid].astype(F32) + down[:, :hid].astype(F32)
        g = grad(0) + up[:, hid:].astype(F32) + down[:, hid:].astype(F32)
        half = rows // 2
        other = shift(cat(p[half:], g[half:]), "xl", 1)
        p = p[:half] + other[:, :hid].astype(F32)
        g = g[:half] + other[:, hid:].astype(F32)
        cdf, pdf = gelu_parts(p)
        act = (p * cdf).astype(BF16)
        pre_grad = (g * (cdf + p * pdf)).astype(BF16)
        return jnp.concatenate([act, pre_grad], 1)

    def spread(mine):
        mine = jnp.concatenate([mine, shift(mine, "xl", 1)], 0)
        above = shift(mine, "z", -1)
        below = shift(mine, "z", 1)
        act2 = shift(above[:, :hid], "z", -1)
        grad2 = shift(below[:, hid:], "z", 1)
        act = jnp.concatenate([mine[:, :hid], above[:, :hid], act2, below[:, :hid]], 0)
        grad = jnp.concatenate([mine[:, hid:], above[:, hid:], grad2, below[:, hid:]], 0)
        return act, grad

    def input_part(grad):
        part = dot(grad, wi, 1, 1)
        return part[:, :feat] + shift(part[:, feat:], "core", 1)

    tok_a, cot_a = chip_features(near)
    tok_b, cot_b = chip_features(far)
    mine_a = hidden(tok_a, cot_a)
    mine_b = hidden(tok_b, cot_b)
    act_b, grad_b = spread(mine_b)
    act_a, grad_a = spread(mine_a)
    in_b = shift(input_part(grad_b).astype(BF16), "xh", 1)
    in_a = input_part(grad_a) + in_b.astype(F32)
    in_a = in_a.reshape(4, 2, 4, piece, feat).transpose(2, 0, 1, 3, 4)
    total = in_a[0]
    for d in (1, 2, 3):
        total = total + shift(in_a[d].astype(BF16), "y", d).astype(F32)
    input_grad = relative(total, 1).reshape(rows, feat).astype(BF16)

    wi_grad = (dot(tok_b, grad_b, 0, 0) + dot(tok_a, grad_a, 0, 0)).astype(BF16)
    wo_grad = (dot(act_b, cot_b, 0, 0) + dot(act_a, cot_a, 0, 0)).astype(BF16)
    w_in_grad = swap_halves(wi_grad[:feat], shift(wi_grad[feat:], "core", 1), core, 1)
    w_out_grad = swap_halves(wo_grad[:, :feat], shift(wo_grad[:, feat:], "core", 1), core, 0)
    return (input_grad, w_in_grad, w_out_grad)


def solution(mesh):
    fine = Mesh(mesh.devices.reshape(SIZES), AXES)
    return jax.shard_map(
        local,
        mesh=fine,
        in_specs=(P(ROWS, COLS), P(ROWS, COLS), P(COLS, ROWS), P(ROWS, COLS)),
        out_specs=(P(ROWS, COLS), P(COLS, ROWS), P(ROWS, COLS)),
        check_vma=False,
    )
```

```python
import jax
import jax.numpy as jnp
from jax import lax
from jax.sharding import Mesh
from jax.sharding import PartitionSpec as P

AXES = ("y", "xh", "xl", "z", "core")
SIZES = (4, 2, 2, 4, 2)
ROWS = ("y", "xh")
COLS = ("xl", "z", "core")
F32 = jnp.float32
BF16 = jnp.bfloat16


def gelu_parts(pre):
    cdf = 0.5 * (1.0 + lax.erf(pre * 0.7071067811865476))
    pdf = jnp.exp(-0.5 * pre * pre) * 0.3989422804014327
    return (cdf, pdf)


def shift(x, axis, by):
    n = SIZES[AXES.index(axis)]
    return lax.ppermute(x, axis, [(i, (i + by) % n) for i in range(n)])


def dot(a, b, da, db):
    return lax.dot_general(a, b, (((da,), (db,)), ((), ())), preferred_element_type=F32)


def swap_halves(first, second, flag, axis):
    return jnp.concatenate([jnp.where(flag == 0, first, second), jnp.where(flag == 0, second, first)], axis)


def local(tokens, cotangent, w_in, w_out):
    z, core = lax.axis_index("z"), lax.axis_index("core")
    rows, feat = tokens.shape
    hid = w_in.shape[1] // 2
    piece = rows // 4

    def relative(a, sign):
        return jnp.roll(a.reshape(4, piece, a.shape[-1]), sign * z, 0)

    own = relative(jnp.concatenate([tokens, cotangent], 1), -1)
    near = [shift(own, "y", -d) for d in (1, 2, 3)]
    across = shift(own, "xh", 1)
    far = [across] + [shift(across, "y", -d) for d in (1, 2, 3)]

    def core_weights(w, axis):
        keep = lax.dynamic_slice_in_dim(w, core * hid, hid, axis)
        send = lax.dynamic_slice_in_dim(w, (1 - core) * hid, hid, axis)
        return jnp.concatenate([keep, shift(send, "core", 1)], 1 - axis)

    wi = core_weights(w_in, 1)
    wo = core_weights(w_out, 0)

    def chip_features(parts):
        a = jnp.concatenate(parts, 1) if len(parts) > 1 else parts[0]
        b = shift(a, "core", 1)
        return (
            jnp.concatenate([a[..., :feat], b[..., :feat]], -1),
            jnp.concatenate([a[..., feat:], b[..., feat:]], -1),
        )

    def hidden(tok, cot):
        pre = lambda k: dot(tok[k], wi, 1, 0)
        grad = lambda k: dot(cot[k], wo, 1, 1)
        cat = lambda p, g: jnp.concatenate([p.astype(BF16), g.astype(BF16)], 1)
        up = shift(pre(2).astype(BF16), "z", 1)
        down = shift(grad(2).astype(BF16), "z", -1)
        up = shift(cat(pre(1) + up.astype(F32), grad(1)), "z", 1)
        down = shift(cat(pre(3), grad(3) + down.astype(F32)), "z", -1)
        p = pre(0) + up[:, :hid].astype(F32) + down[:, :hid].astype(F32)
        g = grad(0) + up[:, hid:].astype(F32) + down[:, hid:].astype(F32)
        other = shift(cat(p, g), "xl", 1)
        p = p + other[:, :hid].astype(F32)
        g = g + other[:, hid:].astype(F32)
        cdf, pdf = gelu_parts(p)
        act = (p * cdf).astype(BF16)
        pre_grad = (g * (cdf + p * pdf)).astype(BF16)
        return jnp.concatenate([act, pre_grad], 1)

    def spread(mine):
        above = shift(mine, "z", -1)
        below = shift(mine, "z", 1)
        act2 = shift(above[:, :hid], "z", -1)
        grad2 = shift(below[:, hid:], "z", 1)
        act = jnp.concatenate([mine[:, :hid], above[:, :hid], act2, below[:, :hid]], 0)
        grad = jnp.concatenate([mine[:, hid:], above[:, hid:], grad2, below[:, hid:]], 0)
        return act, grad

    def input_part(grad):
        part = dot(grad, wi, 1, 1)
        part = part[:, :feat] + shift(part[:, feat:], "core", 1)
        return part.reshape(4, -1, piece, feat)

    flat = lambda a: a.reshape(-1, a.shape[-1])
    chunks = [chip_features([own]), chip_features(near), chip_features(far)]
    mine = [hidden(*c) for c in chunks]
    (act_n, grad_n), (act_f, grad_f), (act_o, grad_o) = spread(mine[1]), spread(mine[2]), spread(mine[0])

    in_f = input_part(grad_f)
    total = in_f[:, 0]
    for d in (1, 2, 3):
        total = total + shift(in_f[:, d].astype(BF16), "y", d).astype(F32)
    total = shift(total.astype(BF16), "xh", 1).astype(F32)
    in_n = input_part(grad_n)
    for d in (1, 2, 3):
        total = total + shift(in_n[:, d - 1].astype(BF16), "y", d).astype(F32)
    total = total + input_part(grad_o)[:, 0]
    input_grad = relative(total, 1).reshape(rows, feat).astype(BF16)

    def token_sum(left, right):
        out = dot(left[0], right[0], 0, 0)
        for a, b in zip(left[1:], right[1:]):
            out = out + dot(a, b, 0, 0)
        return out.astype(BF16)

    toks = [flat(chunks[i][0]) for i in (1, 2, 0)]
    cots = [flat(chunks[i][1]) for i in (1, 2, 0)]
    grads, acts = [grad_n, grad_f, grad_o], [act_n, act_f, act_o]
    wi_other = shift(token_sum([t[:, feat:] for t in toks], grads), "core", 1)
    wo_other = shift(token_sum(acts, [c[:, feat:] for c in cots]), "core", 1)
    wi_own = token_sum([t[:, :feat] for t in toks], grads)
    wo_own = token_sum(acts, [c[:, :feat] for c in cots])
    w_in_grad = swap_halves(wi_own, wi_other, core, 1)
    w_out_grad = swap_halves(wo_own, wo_other, core, 0)
    return (input_grad, w_in_grad, w_out_grad)


def solution(mesh):
    fine = Mesh(mesh.devices.reshape(SIZES), AXES)
    return jax.shard_map(
        local,
        mesh=fine,
        in_specs=(P(ROWS, COLS), P(ROWS, COLS), P(COLS, ROWS), P(ROWS, COLS)),
        out_specs=(P(ROWS, COLS), P(COLS, ROWS), P(ROWS, COLS)),
        check_vma=False,
    )
```

```python
import jax
import jax.numpy as jnp
from jax import lax
from jax.sharding import Mesh
from jax.sharding import PartitionSpec as P

AXES = ("y", "xh", "xl", "z", "core")
SIZES = (4, 2, 2, 4, 2)
ROWS = ("y", "xh")
COLS = ("xl", "z", "core")
F32 = jnp.float32
BF16 = jnp.bfloat16


def gelu_parts(pre):
    cdf = 0.5 * (1.0 + lax.erf(pre * 0.7071067811865476))
    pdf = jnp.exp(-0.5 * pre * pre) * 0.3989422804014327
    return (cdf, pdf)


def shift(x, axis, by):
    n = SIZES[AXES.index(axis)]
    return lax.ppermute(x, axis, [(i, (i + by) % n) for i in range(n)])


def dot(a, b, da, db):
    return lax.dot_general(a, b, (((da,), (db,)), ((), ())), preferred_element_type=F32)


def swap_halves(first, second, flag, axis):
    return jnp.concatenate([jnp.where(flag == 0, first, second), jnp.where(flag == 0, second, first)], axis)


def gate(value, *after):
    return lax.optimization_barrier((value, after))[0]


def local(tokens, cotangent, w_in, w_out):
    z, core = lax.axis_index("z"), lax.axis_index("core")
    rows, feat = tokens.shape
    hid = w_in.shape[1] // 2
    piece = rows // 4

    def relative(a, sign):
        return jnp.roll(a.reshape(4, piece, a.shape[-1]), sign * z, 0)

    def halves(w, axis):
        keep = lax.dynamic_slice_in_dim(w, core * hid, hid, axis)
        return keep, lax.dynamic_slice_in_dim(w, (1 - core) * hid, hid, axis)

    def features(a, b):
        return (
            jnp.concatenate([a[..., :feat], b[..., :feat]], -1),
            jnp.concatenate([a[..., feat:], b[..., feat:]], -1),
        )

    def cat(p, g):
        return jnp.concatenate([p.astype(BF16), g.astype(BF16)], 1)

    def up_down(up, down):
        return shift(up, "z", 1), shift(down, "z", -1)

    def step1(tok, cot):
        return dot(tok[2], wi, 1, 0).astype(BF16), dot(cot[2], wo, 1, 1).astype(BF16)

    def step2(tok, cot, up, down):
        return (
            cat(dot(tok[1], wi, 1, 0) + up.astype(F32), dot(cot[1], wo, 1, 1)),
            cat(dot(tok[3], wi, 1, 0), dot(cot[3], wo, 1, 1) + down.astype(F32)),
        )

    def step3(tok, cot, up, down):
        p = dot(tok[0], wi, 1, 0) + up[:, :hid].astype(F32) + down[:, :hid].astype(F32)
        g = dot(cot[0], wo, 1, 1) + up[:, hid:].astype(F32) + down[:, hid:].astype(F32)
        return p, g, cat(p, g)

    def step4(p, g, other):
        p = p + other[:, :hid].astype(F32)
        g = g + other[:, hid:].astype(F32)
        cdf, pdf = gelu_parts(p)
        return cat(p * cdf, g * (cdf + p * pdf))

    def send_mine(mine):
        return shift(mine, "z", -1), shift(mine, "z", 1)

    def send_on(above, below):
        return shift(above[:, :hid], "z", -1), shift(below[:, hid:], "z", 1)

    def gathered(mine, above, below, act2, grad2):
        act = jnp.concatenate([mine[:, :hid], above[:, :hid], act2, below[:, :hid]], 0)
        grad = jnp.concatenate([mine[:, hid:], above[:, hid:], grad2, below[:, hid:]], 0)
        return act, grad

    def input_part(grad):
        part = dot(grad, wi, 1, 1)
        return part[:, :feat], part[:, feat:]

    def by_row(mine, other):
        return (mine + other).reshape(4, -1, piece, feat)

    own = relative(jnp.concatenate([tokens, cotangent], 1), -1)
    own_other = shift(own, "core", 1)
    wi_keep, wi_send = halves(w_in, 1)
    wo_keep, wo_send = halves(w_out, 0)
    wi_got, wo_got = shift(wi_send, "core", 1), shift(wo_send, "core", 1)
    own_y = gate(own, wi_send, wo_send)
    near = [shift(own_y, "y", -d) for d in (1, 2, 3)]
    across = shift(own_y, "xh", 1)
    wi = jnp.concatenate([wi_keep, wi_got], 0)
    wo = jnp.concatenate([wo_keep, wo_got], 1)

    tok_o, cot_o = features(own, own_other)
    m_o = step1(tok_o, cot_o)
    r_o = up_down(*m_o)

    across = gate(across, m_o)
    far = [across] + [shift(across, "y", -d) for d in (1, 2, 3)]
    near = jnp.concatenate(gate(near, across), 1)
    near_other = shift(near, "core", 1)
    tok_n, cot_n = features(near, near_other)
    m_n = step1(tok_n, cot_n)
    r_n = up_down(*m_n)

    m_o = step2(tok_o, cot_o, *gate(r_o, m_n))
    r_o = up_down(*m_o)

    far = jnp.concatenate(gate(far, m_o), 1)
    far_other = shift(far, "core", 1)
    tok_f, cot_f = features(far, far_other)
    m_f = step1(tok_f, cot_f)
    r_f = up_down(*m_f)

    m_n = step2(tok_n, cot_n, *gate(r_n, m_f))
    r_n = up_down(*m_n)

    p_o, g_o, m_o = step3(tok_o, cot_o, *gate(r_o, m_n))
    x_o = shift(m_o, "xl", 1)

    m_f = step2(tok_f, cot_f, *gate(r_f, m_o))
    r_f = up_down(*m_f)

    p_n, g_n, m_n = step3(tok_n, cot_n, *gate(r_n, m_f))
    x_n = shift(m_n, "xl", 1)

    mine_o = step4(p_o, g_o, gate(x_o, m_n))
    mine_n = step4(p_n, g_n, gate(x_n, mine_o))
    s_n = send_mine(mine_n)

    p_f, g_f, m_f = step3(tok_f, cot_f, *gate(r_f, mine_n))
    x_f = shift(m_f, "xl", 1)

    s_n = gate(s_n, m_f)
    t_n = send_on(*s_n)
    s_o = send_mine(gate(mine_o, s_n))

    mine_f = step4(p_f, g_f, gate(x_f, s_n))
    s_f = send_mine(mine_f)

    act_n, grad_n = gathered(mine_n, *s_n, *gate(t_n, mine_f))
    in_n, in_n_other = input_part(grad_n)
    in_n_got = shift(in_n_other, "core", 1)

    s_f = gate(s_f, in_n_other)
    t_f = send_on(*s_f)
    s_o = gate(s_o, s_f)
    t_o = send_on(*s_o)

    back_n = by_row(in_n, gate(in_n_got, s_o)).astype(BF16)
    back_n = [shift(back_n[:, d - 1], "y", d) for d in (1, 2, 3)]

    act_f, grad_f = gathered(mine_f, *s_f, *gate(t_f, s_o))
    in_f, in_f_other = input_part(grad_f)
    in_f_got = shift(in_f_other, "core", 1)

    act_o, grad_o = gathered(mine_o, *s_o, *gate(t_o, in_f_other))
    in_o, in_o_other = input_part(grad_o)
    in_o_got = shift(in_o_other, "core", 1)

    back_f = by_row(in_f, gate(in_f_got, in_o_other)).astype(BF16)
    back_f = [
        lax.ppermute(back_f[:, d], ROWS, [(i, ((i // 2 + d) % 4) * 2 + (i + 1) % 2) for i in range(8)])
        for d in (0, 1, 2, 3)
    ]

    def token_sum(left, right):
        out = dot(left[0], right[0], 0, 0)
        for a, b in zip(left[1:], right[1:]):
            out = out + dot(a, b, 0, 0)
        return out.astype(BF16)

    flat = lambda a: a.reshape(-1, a.shape[-1])
    toks = [flat(a) for a in (tok_n, tok_f, tok_o)]
    cots = [flat(a) for a in (cot_n, cot_f, cot_o)]
    grads, acts = [grad_n, grad_f, grad_o], [act_n, act_f, act_o]
    wi_other = shift(token_sum([t[:, feat:] for t in toks], grads), "core", 1)
    wo_other = shift(token_sum(acts, [c[:, feat:] for c in cots]), "core", 1)
    wi_own = token_sum([t[:, :feat] for t in toks], grads)
    wo_own = token_sum(acts, [c[:, :feat] for c in cots])
    w_in_grad = swap_halves(wi_own, wi_other, core, 1)
    w_out_grad = swap_halves(wo_own, wo_other, core, 0)

    total = by_row(in_o, in_o_got)[:, 0]
    for part in back_n + back_f:
        total = total + part.astype(F32)
    input_grad = relative(total, 1).reshape(rows, feat).astype(BF16)
    return (input_grad, w_in_grad, w_out_grad)


def solution(mesh):
    fine = Mesh(mesh.devices.reshape(SIZES), AXES)
    return jax.shard_map(
        local,
        mesh=fine,
        in_specs=(P(ROWS, COLS), P(ROWS, COLS), P(COLS, ROWS), P(ROWS, COLS)),
        out_specs=(P(ROWS, COLS), P(COLS, ROWS), P(ROWS, COLS)),
        check_vma=False,
    )
```

```python
import jax
import jax.numpy as jnp
from jax import lax
from jax.sharding import Mesh
from jax.sharding import PartitionSpec as P

AXES = ("y", "xh", "xl", "z", "core")
SIZES = (4, 2, 2, 4, 2)
ROWS = ("y", "xh")
COLS = ("xl", "z", "core")
F32 = jnp.float32
BF16 = jnp.bfloat16


def gelu_parts(pre):
    cdf = 0.5 * (1.0 + lax.erf(pre * 0.7071067811865476))
    pdf = jnp.exp(-0.5 * pre * pre) * 0.3989422804014327
    return (cdf, pdf)


def shift(x, axis, by):
    n = SIZES[AXES.index(axis)]
    return lax.ppermute(x, axis, [(i, (i + by) % n) for i in range(n)])


def dot(a, b, da, db):
    return lax.dot_general(a, b, (((da,), (db,)), ((), ())), preferred_element_type=F32)


def swap_halves(first, second, flag, axis):
    return jnp.concatenate([jnp.where(flag == 0, first, second), jnp.where(flag == 0, second, first)], axis)


def gate(value, *after):
    return lax.optimization_barrier((value, after))[0]


def local(tokens, cotangent, w_in, w_out):
    z, core = lax.axis_index("z"), lax.axis_index("core")
    rows, feat = tokens.shape
    hid = w_in.shape[1] // 2
    piece = rows // 4

    def relative(a, sign):
        return jnp.roll(a.reshape(4, piece, a.shape[-1]), sign * z, 0)

    def halves(w, axis):
        keep = lax.dynamic_slice_in_dim(w, core * hid, hid, axis)
        return keep, lax.dynamic_slice_in_dim(w, (1 - core) * hid, hid, axis)

    def features(a, b):
        return (
            jnp.concatenate([a[..., :feat], b[..., :feat]], -1),
            jnp.concatenate([a[..., feat:], b[..., feat:]], -1),
        )

    def cat(p, g):
        return jnp.concatenate([p.astype(BF16), g.astype(BF16)], 1)

    def up_down(up, down):
        return shift(up, "z", 1), shift(down, "z", -1)

    def step1(tok, cot):
        return dot(tok[2], wi, 1, 0).astype(BF16), dot(cot[2], wo, 1, 1).astype(BF16)

    def step2(tok, cot, up, down):
        return (
            cat(dot(tok[1], wi, 1, 0) + up.astype(F32), dot(cot[1], wo, 1, 1)),
            cat(dot(tok[3], wi, 1, 0), dot(cot[3], wo, 1, 1) + down.astype(F32)),
        )

    def step3(tok, cot, up, down):
        p = dot(tok[0], wi, 1, 0) + up[:, :hid].astype(F32) + down[:, :hid].astype(F32)
        g = dot(cot[0], wo, 1, 1) + up[:, hid:].astype(F32) + down[:, hid:].astype(F32)
        return p, g, cat(p, g)

    def step4(p, g, other):
        p = p + other[:, :hid].astype(F32)
        g = g + other[:, hid:].astype(F32)
        cdf, pdf = gelu_parts(p)
        return cat(p * cdf, g * (cdf + p * pdf))

    def send_mine(mine):
        return shift(mine, "z", -1), shift(mine, "z", 1)

    def send_on(above, below):
        return shift(above[:, :hid], "z", -1), shift(below[:, hid:], "z", 1)

    def gathered(mine, above, below, act2, grad2):
        act = jnp.concatenate([mine[:, :hid], above[:, :hid], act2, below[:, :hid]], 0)
        grad = jnp.concatenate([mine[:, hid:], above[:, hid:], grad2, below[:, hid:]], 0)
        return act, grad

    def input_part(grad):
        part = dot(grad, wi, 1, 1)
        return part[:, :feat], part[:, feat:]

    def by_row(mine, other):
        return (mine + other).reshape(4, -1, piece, feat)

    own = relative(jnp.concatenate([tokens, cotangent], 1), -1)
    near = [own] + [shift(own, "y", -d) for d in (1, 2, 3)]
    wi_keep, wi_send = halves(w_in, 1)
    wo_keep, wo_send = halves(w_out, 0)
    wi_got, wo_got = shift(wi_send, "core", 1), shift(wo_send, "core", 1)
    across = shift(own, "xh", 1)
    near = jnp.concatenate(near, 1)
    near_other = shift(near, "core", 1)
    wi = jnp.concatenate([wi_keep, wi_got], 0)
    wo = jnp.concatenate([wo_keep, wo_got], 1)
    wi, wo = lax.optimization_barrier((wi, wo))

    tok_a, cot_a = features(near, near_other)
    m_a = step1(tok_a, cot_a)
    r_a = up_down(*m_a)

    across = gate(across, m_a)
    far = [across] + [shift(across, "y", -d) for d in (1, 2, 3)]

    m_a = step2(tok_a, cot_a, *gate(r_a, across))
    r_a = up_down(*m_a)

    far = jnp.concatenate(gate(far, m_a), 1)
    far_other = shift(far, "core", 1)
    tok_b, cot_b = features(far, far_other)
    m_b = step1(tok_b, cot_b)
    r_b = up_down(*m_b)

    p_a, g_a, m_a = step3(tok_a, cot_a, *gate(r_a, m_b))
    x_a = shift(m_a, "xl", 1)

    m_b = step2(tok_b, cot_b, *gate(r_b, m_a))
    r_b = up_down(*m_b)

    mine_a = step4(p_a, g_a, gate(x_a, m_b))
    s_a = send_mine(mine_a)

    p_b, g_b, m_b = step3(tok_b, cot_b, *gate(r_b, mine_a))
    x_b = shift(m_b, "xl", 1)

    s_a = gate(s_a, m_b)
    t_a = send_on(*s_a)

    mine_b = step4(p_b, g_b, gate(x_b, s_a))
    s_b = send_mine(mine_b)

    act_a, grad_a = gathered(mine_a, *s_a, *gate(t_a, mine_b))
    in_a, in_a_other = input_part(grad_a)
    in_a_got = shift(in_a_other, "core", 1)

    s_b = gate(s_b, in_a_other)
    t_b = send_on(*s_b)

    back_a = by_row(in_a, gate(in_a_got, s_b))
    back = [shift(back_a[:, d].astype(BF16), "y", d) for d in (1, 2, 3)]

    act_b, grad_b = gathered(mine_b, *s_b, *gate(t_b, back_a))
    in_b, in_b_other = input_part(grad_b)
    in_b_got = shift(in_b_other, "core", 1)
    back_b = by_row(in_b, in_b_got).astype(BF16)
    back += [
        lax.ppermute(back_b[:, d], ROWS, [(i, ((i // 2 + d) % 4) * 2 + (i + 1) % 2) for i in range(8)])
        for d in (0, 1, 2, 3)
    ]

    def token_sum(left, right):
        return (dot(left[0], right[0], 0, 0) + dot(left[1], right[1], 0, 0)).astype(BF16)

    flat = lambda a: a.reshape(-1, a.shape[-1])
    toks = [flat(a) for a in (tok_a, tok_b)]
    cots = [flat(a) for a in (cot_a, cot_b)]
    grads, acts = [grad_a, grad_b], [act_a, act_b]
    wi_other = shift(token_sum([t[:, feat:] for t in toks], grads), "core", 1)
    wo_other = shift(token_sum(acts, [c[:, feat:] for c in cots]), "core", 1)
    wi_own = token_sum([t[:, :feat] for t in toks], grads)
    wo_own = token_sum(acts, [c[:, :feat] for c in cots])
    w_in_grad = swap_halves(wi_own, wi_other, core, 1)
    w_out_grad = swap_halves(wo_own, wo_other, core, 0)

    total = back_a[:, 0]
    for part in back:
        total = total + part.astype(F32)
    input_grad = relative(total, 1).reshape(rows, feat).astype(BF16)
    return (input_grad, w_in_grad, w_out_grad)


def solution(mesh):
    fine = Mesh(mesh.devices.reshape(SIZES), AXES)
    return jax.shard_map(
        local,
        mesh=fine,
        in_specs=(P(ROWS, COLS), P(ROWS, COLS), P(COLS, ROWS), P(ROWS, COLS)),
        out_specs=(P(ROWS, COLS), P(COLS, ROWS), P(ROWS, COLS)),
        check_vma=False,
    )
```

```python
import jax
import jax.numpy as jnp
from jax import lax
from jax.experimental import pallas as pl
from jax.experimental.pallas import tpu as pltpu
from jax.sharding import Mesh
from jax.sharding import PartitionSpec as P

AXES = ("y", "xh", "xl", "z", "core")
SIZES = (4, 2, 2, 4, 2)
ROWS = ("y", "xh")
COLS = ("xl", "z", "core")
F32 = jnp.float32
BF16 = jnp.bfloat16


def gelu_parts(pre):
    cdf = 0.5 * (1.0 + lax.erf(pre * 0.7071067811865476))
    pdf = jnp.exp(-0.5 * pre * pre) * 0.3989422804014327
    return (cdf, pdf)


def shift(x, axis, by):
    n = SIZES[AXES.index(axis)]
    return lax.ppermute(x, axis, [(i, (i + by) % n) for i in range(n)])


def dot(a, b, da, db):
    return lax.dot_general(a, b, (((da,), (db,)), ((), ())), preferred_element_type=F32)


def swap_halves(first, second, flag, axis):
    return jnp.concatenate([jnp.where(flag == 0, first, second), jnp.where(flag == 0, second, first)], axis)


CHEAP = dict(
    cost_estimate=pl.CostEstimate(flops=10**6, bytes_accessed=10**5, transcendentals=0),
    compiler_params=pltpu.CompilerParams(vmem_limit_bytes=24 * 2**20),
)


def products(tok, cot, wi, wo):
    rows, feat = tok.shape
    hid = wi.shape[1]
    block = hid // 3

    def body(tok, cot, wi, wo, p, g):
        p[...] = jnp.dot(tok[...], wi[...], preferred_element_type=F32)
        g[...] = dot(cot[...], wo[...], 1, 1)

    whole = pl.BlockSpec((rows, feat), lambda i: (0, 0))
    out = pl.BlockSpec((rows, block), lambda i: (0, i))
    return pl.pallas_call(
        body,
        grid=(3,),
        in_specs=[
            whole,
            whole,
            pl.BlockSpec((feat, block), lambda i: (0, i)),
            pl.BlockSpec((block, feat), lambda i: (i, 0)),
        ],
        out_specs=[out, out],
        out_shape=[jax.ShapeDtypeStruct((rows, hid), F32)] * 2,
        **CHEAP,
    )(tok, cot, wi, wo)


def input_product(grad, wi):
    rows, hid = grad.shape
    feat = wi.shape[0]
    block = rows // 2

    def body(grad, wi, out):
        out[...] = dot(grad[...], wi[...], 1, 1)

    return pl.pallas_call(
        body,
        grid=(2,),
        in_specs=[pl.BlockSpec((block, hid), lambda i: (i, 0)), pl.BlockSpec((feat, hid), lambda i: (0, 0))],
        out_specs=pl.BlockSpec((block, feat), lambda i: (i, 0)),
        out_shape=jax.ShapeDtypeStruct((rows, feat), F32),
        **CHEAP,
    )(grad, wi)


def gate(value, *after):
    return lax.optimization_barrier((value, after))[0]


def local(tokens, cotangent, w_in, w_out):
    z, core = lax.axis_index("z"), lax.axis_index("core")
    rows, feat = tokens.shape
    hid = w_in.shape[1] // 2
    piece = rows // 4

    def relative(a, sign):
        return jnp.roll(a.reshape(4, piece, a.shape[-1]), sign * z, 0)

    def halves(w, axis):
        keep = lax.dynamic_slice_in_dim(w, core * hid, hid, axis)
        return keep, lax.dynamic_slice_in_dim(w, (1 - core) * hid, hid, axis)

    def features(a, b):
        return (
            jnp.concatenate([a[..., :feat], b[..., :feat]], -1),
            jnp.concatenate([a[..., feat:], b[..., feat:]], -1),
        )

    def cat(p, g):
        return jnp.concatenate([p.astype(BF16), g.astype(BF16)], 1)

    def up_down(up, down):
        return shift(up, "z", 1), shift(down, "z", -1)

    def partial_sums(tok, cot):
        p, g = products(tok.reshape(4 * rows, -1), cot.reshape(4 * rows, -1), wi, wo)
        return p.reshape(4, rows, hid), g.reshape(4, rows, hid)

    def step1(p, g):
        return p[2].astype(BF16), g[2].astype(BF16)

    def step2(p, g, up, down):
        return cat(p[1] + up.astype(F32), g[1]), cat(p[3], g[3] + down.astype(F32))

    def step3(p, g, up, down):
        p = p[0] + up[:, :hid].astype(F32) + down[:, :hid].astype(F32)
        g = g[0] + up[:, hid:].astype(F32) + down[:, hid:].astype(F32)
        return p, g, cat(p, g)

    def step4(p, g, other):
        p = p + other[:, :hid].astype(F32)
        g = g + other[:, hid:].astype(F32)
        cdf, pdf = gelu_parts(p)
        return cat(p * cdf, g * (cdf + p * pdf))

    def send_mine(mine):
        return shift(mine, "z", -1), shift(mine, "z", 1)

    def send_on(above, below):
        return shift(above[:, :hid], "z", -1), shift(below[:, hid:], "z", 1)

    def gathered(mine, above, below, act2, grad2):
        act = jnp.concatenate([mine[:, :hid], above[:, :hid], act2, below[:, :hid]], 0)
        grad = jnp.concatenate([mine[:, hid:], above[:, hid:], grad2, below[:, hid:]], 0)
        return act, grad

    def input_part(grad):
        part = input_product(grad, wi)
        return part[:, :feat], part[:, feat:]

    def by_row(mine, other):
        return (mine + other).reshape(4, -1, piece, feat)

    own = relative(jnp.concatenate([tokens, cotangent], 1), -1)
    across = shift(own, "xh", 1)
    near = [own] + [shift(own, "y", -d) for d in (1, 2, 3)]
    wi_keep, wi_send = halves(w_in, 1)
    wo_keep, wo_send = halves(w_out, 0)
    wi_got, wo_got = shift(wi_send, "core", 1), shift(wo_send, "core", 1)
    across = gate(across, wi_send, wo_send)
    far = [across] + [shift(across, "y", -d) for d in (1, 2, 3)]
    near = jnp.concatenate(gate(near, across), 1)
    near_other = shift(near, "core", 1)
    wi = jnp.concatenate([wi_keep, wi_got], 0)
    wo = jnp.concatenate([wo_keep, wo_got], 1)
    wi, wo = lax.optimization_barrier((wi, wo))

    tok_a, cot_a = features(near, near_other)
    pg_a = partial_sums(tok_a, cot_a)
    m_a = step1(*pg_a)
    r_a = up_down(*m_a)

    far = jnp.concatenate(gate(far, m_a), 1)
    far_other = shift(far, "core", 1)
    tok_b, cot_b = features(far, far_other)
    pg_b = partial_sums(tok_b, cot_b)
    m_b = step1(*pg_b)
    r_b = up_down(*m_b)

    m_a = step2(*pg_a, *gate(r_a, m_b))
    r_a = up_down(*m_a)

    p_a, g_a, m_a = step3(*pg_a, *r_a)
    x_a = shift(m_a, "xl", 1)

    m_b = step2(*pg_b, *gate(r_b, m_a))
    r_b = up_down(*m_b)

    mine_a = step4(p_a, g_a, gate(x_a, m_b))
    s_a = send_mine(mine_a)

    p_b, g_b, m_b = step3(*pg_b, *gate(r_b, mine_a))
    x_b = shift(m_b, "xl", 1)

    s_a = gate(s_a, m_b)
    t_a = send_on(*s_a)

    mine_b = step4(p_b, g_b, gate(x_b, s_a))
    s_b = send_mine(mine_b)

    act_a, grad_a = gathered(mine_a, *s_a, *gate(t_a, mine_b))
    in_a, in_a_other = input_part(grad_a)
    in_a_got = shift(in_a_other, "core", 1)

    back_a = by_row(in_a, in_a_got)
    back = [shift(back_a[:, d].astype(BF16), "y", d) for d in (1, 2, 3)]

    s_b = gate(s_b, back_a)
    t_b = send_on(*s_b)

    act_b, grad_b = gathered(mine_b, *s_b, *gate(t_b, back))
    in_b, in_b_other = input_part(grad_b)
    in_b_got = shift(in_b_other, "core", 1)
    back_b = by_row(in_b, in_b_got).astype(BF16)
    back_far = [
        lax.ppermute(back_b[:, d], ROWS, [(i, ((i // 2 + d) % 4) * 2 + (i + 1) % 2) for i in range(8)])
        for d in (0, 1, 2, 3)
    ]

    def token_sum(left, right):
        return (dot(left[0], right[0], 0, 0) + dot(left[1], right[1], 0, 0)).astype(BF16)

    flat = lambda a: a.reshape(-1, a.shape[-1])
    grads, acts = gate(([grad_a, grad_b], [act_a, act_b]), in_b_other)
    toks = [flat(a) for a in (tok_a, tok_b)]
    cots = [flat(a) for a in (cot_a, cot_b)]
    wi_other = shift(token_sum([t[:, feat:] for t in toks], grads), "core", 1)
    wo_other = shift(token_sum(acts, [c[:, feat:] for c in cots]), "core", 1)
    wi_own = token_sum([t[:, :feat] for t in toks], grads)
    wo_own = token_sum(acts, [c[:, :feat] for c in cots])
    w_in_grad = swap_halves(wi_own, wi_other, core, 1)
    w_out_grad = swap_halves(wo_own, wo_other, core, 0)

    total = back_a[:, 0]
    for part in back + gate(back_far, w_in_grad, w_out_grad):
        total = total + part.astype(F32)
    input_grad = relative(total, 1).reshape(rows, feat).astype(BF16)
    return (input_grad, w_in_grad, w_out_grad)


def solution(mesh):
    fine = Mesh(mesh.devices.reshape(SIZES), AXES)
    return jax.shard_map(
        local,
        mesh=fine,
        in_specs=(P(ROWS, COLS), P(ROWS, COLS), P(COLS, ROWS), P(ROWS, COLS)),
        out_specs=(P(ROWS, COLS), P(COLS, ROWS), P(ROWS, COLS)),
        check_vma=False,
    )
```

```python
import jax
import jax.numpy as jnp
from jax import lax
from jax.experimental import pallas as pl
from jax.experimental.pallas import tpu as pltpu
from jax.sharding import Mesh
from jax.sharding import PartitionSpec as P

AXES = ("y", "xh", "xl", "z", "core")
SIZES = (4, 2, 2, 4, 2)
ROWS = ("y", "xh")
COLS = ("xl", "z", "core")
F32 = jnp.float32
BF16 = jnp.bfloat16
STEPS = 3


def gelu_parts(pre):
    cdf = 0.5 * (1.0 + lax.erf(pre * 0.7071067811865476))
    pdf = jnp.exp(-0.5 * pre * pre) * 0.3989422804014327
    return (cdf, pdf)


def shift(x, axis, by):
    n = SIZES[AXES.index(axis)]
    return lax.ppermute(x, axis, [(i, (i + by) % n) for i in range(n)])


def dot(a, b, da, db):
    return lax.dot_general(a, b, (((da,), (db,)), ((), ())), preferred_element_type=F32)


def gate(value, *after):
    return lax.optimization_barrier((value, after))[0]


COST = dict(pack=1, weights=1, join=0.1, products=0.1, ring_add=0.1, own_sum=0.1, hidden=0.1, pass_on=0.1, input_part=0.1, return_pieces=0.1, return_far=10, weight_grads=0.1, all_grads=10)


def kernel(name, body, grid, ins, outs, scratch=(), scalar=None):
    def spec(block, index):
        def at(i, *refs):
            return tuple(i if k == "i" else k(i, refs[0][0]) if callable(k) else k for k in index)

        return pl.BlockSpec(block, at)

    def run(*refs):
        body(*(refs if scalar is None else refs[1:]))

    return pl.pallas_call(
        run,
        name=name,
        grid_spec=pltpu.PrefetchScalarGridSpec(
            num_scalar_prefetch=0 if scalar is None else 1,
            grid=(grid,),
            in_specs=[spec(block, index) for _, block, index in ins],
            out_specs=[spec(block, index) for _, _, block, index in outs],
            scratch_shapes=list(scratch),
        ),
        out_shape=[jax.ShapeDtypeStruct(shape, dtype) for shape, dtype, _, _ in outs],
        cost_estimate=pl.CostEstimate(flops=0, bytes_accessed=int(COST[name] * 3.69e6), transcendentals=0),
        compiler_params=pltpu.CompilerParams(vmem_limit_bytes=24 * 2**20),
    )(*([] if scalar is None else [scalar]), *[a for a, _, _ in ins])


def pack(w_in, w_out, core):
    feat = w_in.shape[0]
    half = w_out.shape[0] // feat // 2

    def body(wi, wo, out):
        out[0, 0] = wi[...]
        out[1, 0] = wo[...]

    block = (feat, feat)
    place = lambda i, c: (1 - c) * half + i
    return kernel(
        "pack",
        body,
        half,
        [(w_in, block, (0, place)), (w_out, block, (place, 0))],
        [((2, half, feat, feat), BF16, (2, 1, feat, feat), (0, "i", 0, 0))],
        scalar=core,
    )[0]


def weights(w_in, w_out, got, core):
    feat = w_in.shape[0]
    half = w_out.shape[0] // feat // 2

    def body(wi, wo, got, wi_out, wo_out):
        wi_out[:feat] = wi[...]
        wi_out[feat:] = got[0, 0]
        wo_out[:, :feat] = wo[...]
        wo_out[:, feat:] = got[1, 0]

    block = (feat, feat)
    place = lambda i, c: c * half + i
    return kernel(
        "weights",
        body,
        half,
        [(w_in, block, (0, place)), (w_out, block, (place, 0)), (got, (2, 1, feat, feat), (0, "i", 0, 0))],
        [
            ((2 * feat, half * feat), BF16, (2 * feat, feat), (0, "i")),
            ((half * feat, 2 * feat), BF16, (feat, 2 * feat), ("i", 0)),
        ],
        scalar=core,
    )


def join(pieces, others):
    zs, piece, width = pieces[0].shape
    count = len(pieces)
    per = count * piece

    def body(*refs):
        for out, side in zip(refs[-2:], (refs[:count], refs[count:])):
            for k in range(zs):
                for j in range(count):
                    out[pl.ds(k * per + j * piece, piece), :] = side[j][k]

    return kernel(
        "join",
        body,
        1,
        [(a, (zs, piece, width), (0, 0, 0)) for a in (*pieces, *others)],
        [((zs * per, width), BF16, (zs * per, width), (0, 0))] * 2,
    )


def pass_on(above, below):
    _, per, hid = above.shape

    def body(above, below, act, grad):
        act[...] = above[0]
        grad[...] = below[0]

    return kernel(
        "pass_on",
        body,
        1,
        [(above, (1, per, hid), (0, 0, 0)), (below, (1, per, hid), (1, 0, 0))],
        [((per, hid), BF16, (per, hid), (0, 0))] * 2,
    )


def products(own, other, wi, wo):
    rows, width = own.shape
    feat, hid = wi.shape
    half, per, block = width // 2, rows // 4, hid // STEPS

    def body(own, other, wi, wo, pg, up, down, tok, cot):
        @pl.when(pl.program_id(0) == 0)
        def _():
            for side, ref in enumerate((own, other)):
                tok[:, side * half : (side + 1) * half] = ref[:, :half]
                cot[:, side * half : (side + 1) * half] = ref[:, half:]

        p = jnp.dot(tok[...], wi[...], preferred_element_type=F32)
        g = dot(cot[...], wo[...], 1, 1)
        pg[0] = p
        pg[1] = g
        up[...] = p[2 * per : 3 * per].astype(BF16)
        down[...] = g[2 * per : 3 * per].astype(BF16)

    whole = (rows, width)
    return kernel(
        "products",
        body,
        STEPS,
        [(own, whole, (0, 0)), (other, whole, (0, 0)), (wi, (feat, block), (0, "i")), (wo, (block, feat), ("i", 0))],
        [
            ((2, rows, hid), F32, (2, rows, block), (0, 0, "i")),
            ((per, hid), BF16, (per, block), (0, "i")),
            ((per, hid), BF16, (per, block), (0, "i")),
            ((rows, feat), BF16, (rows, feat), (0, 0)),
            ((rows, feat), BF16, (rows, feat), (0, 0)),
        ],
    )


def ring_add(pg, up, down):
    per, hid = up.shape
    block = hid // STEPS

    def body(one, three, up, down, up_out, down_out):
        up_out[0] = (one[0] + up[...].astype(F32)).astype(BF16)
        up_out[1] = one[1].astype(BF16)
        down_out[0] = three[0].astype(BF16)
        down_out[1] = (three[1] + down[...].astype(F32)).astype(BF16)

    part = (2, per, block)
    return kernel(
        "ring_add",
        body,
        STEPS,
        [(pg, part, (0, 1, "i")), (pg, part, (0, 3, "i")), (up, (per, block), (0, "i")), (down, (per, block), (0, "i"))],
        [((2, per, hid), BF16, part, (0, 0, "i"))] * 2,
    )


def own_sum(pg, up, down):
    _, per, hid = up.shape
    part = (2, per, hid // STEPS)

    def body(zero, up, down, out, sent):
        total = zero[...] + up[...].astype(F32) + down[...].astype(F32)
        out[...] = total
        sent[...] = total.astype(BF16)

    return kernel(
        "own_sum",
        body,
        STEPS,
        [(pg, part, (0, 0, "i")), (up, part, (0, 0, "i")), (down, part, (0, 0, "i"))],
        [((2, per, hid), F32, part, (0, 0, "i")), ((2, per, hid), BF16, part, (0, 0, "i"))],
    )


def hidden(total, other):
    _, per, hid = total.shape
    part = (2, per, hid // STEPS)

    def body(total, other, out):
        pre = total[0] + other[0].astype(F32)
        act_grad = total[1] + other[1].astype(F32)
        cdf, pdf = gelu_parts(pre)
        out[0] = (pre * cdf).astype(BF16)
        out[1] = (act_grad * (cdf + pre * pdf)).astype(BF16)

    return kernel(
        "hidden",
        body,
        STEPS,
        [(total, part, (0, 0, "i")), (other, part, (0, 0, "i"))],
        [((2, per, hid), BF16, part, (0, 0, "i"))],
    )[0]


def input_part(mine, above, grad2, below, wi):
    _, per, hid = mine.shape
    feat = wi.shape[0]
    half = feat // 2

    def body(mine, above, grad2, below, wi, own, other):
        for k, grad in enumerate((mine.at[0], above.at[0], grad2, below.at[0])):
            part = dot(grad[...], wi[...], 1, 1)
            own[k * per : (k + 1) * per] = part[:, :half]
            other[k * per : (k + 1) * per] = part[:, half:]

    second, whole = (1, per, hid), (4 * per, half)
    return kernel(
        "input_part",
        body,
        1,
        [
            (mine, second, (1, 0, 0)),
            (above, second, (1, 0, 0)),
            (grad2, (per, hid), (0, 0)),
            (below, second, (1, 0, 0)),
            (wi, (feat, hid), (0, 0)),
        ],
        [(whole, F32, whole, (0, 0))] * 2,
    )


def return_pieces(name, mine, other, pieces, kinds):
    rows, feat = mine.shape
    piece = rows // 4 // pieces

    def body(mine, other, *outs):
        for k in range(4):
            for j, out in enumerate(outs):
                at = pl.ds((k * pieces + j) * piece, piece)
                out[k] = (mine[at, :] + other[at, :]).astype(out.dtype)

    return kernel(
        name,
        body,
        1,
        [(mine, (rows, feat), (0, 0)), (other, (rows, feat), (0, 0))],
        [((4, piece, feat), kind, (4, piece, feat), (0, 0, 0)) for kind in kinds],
    )


def weight_grads(toks, cots, blocks, side, other=None, core=None):
    rows, feat = toks[0].shape
    _, per, hid = blocks[0][0].shape
    half, block, chunks = feat // 2, hid // STEPS, len(toks)
    both = other is not None

    def body(*refs):
        toks, cots = refs[:chunks], refs[chunks : 2 * chunks]
        parts = refs[2 * chunks : -6]
        wi_out, wo_out, tok, cot, act, grad = refs[-6:]
        step = pl.program_id(0)

        @pl.when(step == 0)
        def _():
            for c in range(chunks):
                tok[c * rows : (c + 1) * rows] = toks[c][...]
                cot[c * rows : (c + 1) * rows] = cots[c][...]

        @pl.when(step < STEPS)
        def _():
            for k in range(4 * chunks):
                a, g = parts[2 * k : 2 * k + 2]
                at = pl.ds(k * per, per)
                act[at, :] = a[0] if len(a.shape) == 3 else a[...]
                grad[at, :] = g[0] if len(g.shape) == 3 else g[...]
            wi_out[...] = dot(tok[...], grad[...], 0, 0).astype(BF16)
            wo_out[...] = dot(act[...], cot[...], 0, 0).astype(BF16)

        if both:

            @pl.when(step >= STEPS)
            def _():
                wi_out[...] = parts[-2][...]
                wo_out[...] = parts[-1][...]

    if both:
        at = lambda i, c: jnp.minimum(i, STEPS - 1)
        late = lambda i, c: jnp.maximum(i - STEPS, 0)
        out = lambda i, c: jnp.where(i < STEPS, c * STEPS + i, (1 - c) * STEPS + i - STEPS)
    else:
        at = out = "i"
    ins = [(a, (rows, half), (0, side)) for a in (*toks, *cots)]
    for mine, above, act2, grad2, below in blocks:
        for pair in (mine, above, (act2, grad2), below):
            if isinstance(pair, tuple):
                ins += [(a, (per, block), (0, at)) for a in pair]
            else:
                ins += [(pair, (1, per, block), (k, 0, at)) for k in (0, 1)]
    if both:
        ins += [(other[0], (half, block), (0, late)), (other[1], (block, half), (late, 0))]
    cols = 2 * hid if both else hid
    return kernel(
        "all_grads" if both else "weight_grads",
        body,
        2 * STEPS if both else STEPS,
        ins,
        [((half, cols), BF16, (half, block), (0, out)), ((cols, half), BF16, (block, half), (out, 0))],
        [pltpu.VMEM((chunks * rows, half), BF16)] * 2 + [pltpu.VMEM((chunks * rows, block), BF16)] * 2,
        core,
    )


def local(tokens, cotangent, w_in, w_out):
    z, core = lax.axis_index("z"), lax.axis_index("core")
    rows, feat = tokens.shape
    hid = w_in.shape[1] // 2
    piece = rows // 4

    def relative(a, sign):
        return jnp.roll(a.reshape(4, piece, a.shape[-1]), sign * z, 0)

    def to_core(parts):
        return [shift(a, "core", 1) for a in parts]

    def up_down(up, down):
        return shift(up, "z", 1), shift(down, "z", -1)

    def send_mine(mine):
        return shift(mine, "z", -1), shift(mine, "z", 1)

    def send_on(above, below):
        act, grad = pass_on(above, below)
        return shift(act, "z", -1), shift(grad, "z", 1)

    place = jnp.reshape(core, (1,)).astype(jnp.int32)
    packed = pack(w_in, w_out, place)
    got = shift(packed, "core", 1)
    own = relative(jnp.concatenate([tokens, cotangent], 1), -1)
    across = shift(own, "xh", 1)
    near = [shift(own, "y", -d) for d in (1, 2, 3)]
    across = gate(across, packed)
    far = [shift(across, "y", -d) for d in (1, 2, 3)]
    near = [own, *gate(near, across)]
    near = join(near, to_core(near))
    wi, wo = weights(w_in, w_out, got, place)

    pg_a, up_a, down_a, tok_a, cot_a = products(*near, wi, wo)
    r_a = up_down(up_a, down_a)

    far = [across, *gate(far, up_a)]
    far = join(far, to_core(far))
    pg_b, up_b, down_b, tok_b, cot_b = products(*far, wi, wo)
    r_b = up_down(up_b, down_b)

    m_a = ring_add(pg_a, *gate(r_a, up_b))
    r_a = up_down(*m_a)
    m_b = ring_add(pg_b, *gate(r_b, m_a))
    r_b = up_down(*m_b)

    t_a, m_a = own_sum(pg_a, *gate(r_a, m_b))
    x_a = shift(m_a, "xl", 1)
    t_b, m_b = own_sum(pg_b, *gate(r_b, m_a))
    x_b = shift(m_b, "xl", 1)

    mine_a = hidden(t_a, gate(x_a, m_b))
    s_a = send_mine(mine_a)
    mine_b = hidden(t_b, gate(x_b, mine_a))
    s_b = send_mine(mine_b)

    s_a = gate(s_a, mine_b)
    f_a = send_on(*s_a)
    s_b = gate(s_b, s_a)
    f_b = send_on(*s_b)

    f_a = gate(f_a, s_b)
    in_a, in_a_other = input_part(mine_a, s_a[0], f_a[1], s_a[1], wi)
    in_a_got = shift(in_a_other, "core", 1)
    kept, *back = return_pieces("return_pieces", in_a, in_a_got, 4, (F32, BF16, BF16, BF16))
    back = [shift(a, "y", d) for d, a in zip((1, 2, 3), back)]

    f_b, back = gate((f_b, back), kept)
    in_b, in_b_other = input_part(mine_b, s_b[0], f_b[1], s_b[1], wi)
    in_b_got = shift(in_b_other, "core", 1)

    blocks = [(mine_a, s_a[0], *f_a, s_a[1]), (mine_b, s_b[0], *f_b, s_b[1])]
    blocks = gate(blocks, in_b_other)
    grads_other = weight_grads([tok_a, tok_b], [cot_a, cot_b], blocks, 1)
    got_other = to_core(grads_other)

    back_far = return_pieces("return_far", in_b, gate(in_b_got, grads_other), 4, (BF16,) * 4)
    got_other = gate(got_other, back_far)
    back_far = [
        lax.ppermute(a, ROWS, [(i, ((i // 2 + d) % 4) * 2 + (i + 1) % 2) for i in range(8)])
        for d, a in enumerate(back_far)
    ]
    w_in_grad, w_out_grad = weight_grads([tok_a, tok_b], [cot_a, cot_b], blocks, 0, got_other, place)

    total = kept
    for part in back + gate(back_far, w_in_grad, w_out_grad):
        total = total + part.astype(F32)
    input_grad = relative(total, 1).reshape(rows, feat).astype(BF16)
    return (input_grad, w_in_grad, w_out_grad)


def solution(mesh):
    fine = Mesh(mesh.devices.reshape(SIZES), AXES)
    return jax.shard_map(
        local,
        mesh=fine,
        in_specs=(P(ROWS, COLS), P(ROWS, COLS), P(COLS, ROWS), P(ROWS, COLS)),
        out_specs=(P(ROWS, COLS), P(COLS, ROWS), P(ROWS, COLS)),
        check_vma=False,
    )
```

```python
import jax
import jax.numpy as jnp
from jax import lax
from jax.experimental import pallas as pl
from jax.experimental.pallas import tpu as pltpu
from jax.sharding import Mesh
from jax.sharding import PartitionSpec as P

AXES = ("y", "xh", "xl", "z", "core")
SIZES = (4, 2, 2, 4, 2)
ROWS = ("y", "xh")
COLS = ("xl", "z", "core")
F32 = jnp.float32
BF16 = jnp.bfloat16
STEPS = 3


def gelu_parts(pre):
    cdf = 0.5 * (1.0 + lax.erf(pre * 0.7071067811865476))
    pdf = jnp.exp(-0.5 * pre * pre) * 0.3989422804014327
    return (cdf, pdf)


def shift(x, axis, by):
    n = SIZES[AXES.index(axis)]
    return lax.ppermute(x, axis, [(i, (i + by) % n) for i in range(n)])


def dot(a, b, da, db):
    return lax.dot_general(a, b, (((da,), (db,)), ((), ())), preferred_element_type=F32)


def gate(value, *after):
    return lax.optimization_barrier((value, after))[0]


COST = dict(pack=0.1, weights=0.1, join_a=0.1, join_b=0.1, products=0.1, ring_add=0.1, own_sum=0.1, hidden=0.1, pass_on=0.1, input_a=0.1, input_b=20, grads_a=0.1, grads_b=0.1, returns=0.1, place=5)


def kernel(name, body, grid, ins, outs, scratch=(), scalar=None):
    def spec(block, index):
        def at(i, *refs):
            return tuple(i if k == "i" else k(i, refs[0][0]) if callable(k) else k for k in index)

        return pl.BlockSpec(block, at)

    return pl.pallas_call(
        body,
        name=name,
        grid_spec=pltpu.PrefetchScalarGridSpec(
            num_scalar_prefetch=0 if scalar is None else 1,
            grid=(grid,),
            in_specs=[spec(block, index) for _, block, index in ins],
            out_specs=[spec(block, index) for _, _, block, index in outs],
            scratch_shapes=list(scratch),
        ),
        out_shape=[jax.ShapeDtypeStruct(shape, dtype) for shape, dtype, _, _ in outs],
        cost_estimate=pl.CostEstimate(flops=0, bytes_accessed=int(COST[name] * 3.69e6), transcendentals=0),
        compiler_params=pltpu.CompilerParams(vmem_limit_bytes=24 * 2**20),
    )(*([] if scalar is None else [scalar]), *[a for a, _, _ in ins])


def pack(w_in, w_out, core):
    feat = w_in.shape[0]
    half = w_out.shape[0] // feat // 2

    def body(_, wi, wo, out):
        out[0, 0] = wi[...]
        out[1, 0] = wo[...]

    block = (feat, feat)
    place = lambda i, c: (1 - c) * half + i
    return kernel(
        "pack",
        body,
        half,
        [(w_in, block, (0, place)), (w_out, block, (place, 0))],
        [((2, half, feat, feat), BF16, (2, 1, feat, feat), (0, "i", 0, 0))],
        scalar=core,
    )[0]


def weights(w_in, w_out, got, core):
    feat = w_in.shape[0]
    half = w_out.shape[0] // feat // 2

    def body(_, wi, wo, got, wi_out, wo_out):
        wi_out[:feat] = wi[...]
        wi_out[feat:] = got[0, 0]
        wo_out[:, :feat] = wo[...]
        wo_out[:, feat:] = got[1, 0]

    block = (feat, feat)
    place = lambda i, c: c * half + i
    return kernel(
        "weights",
        body,
        half,
        [(w_in, block, (0, place)), (w_out, block, (place, 0)), (got, (2, 1, feat, feat), (0, "i", 0, 0))],
        [
            ((2 * feat, half * feat), BF16, (2 * feat, feat), (0, "i")),
            ((half * feat, 2 * feat), BF16, (feat, 2 * feat), ("i", 0)),
        ],
        scalar=core,
    )


def join(name, pieces, others):
    zs, piece, width = pieces[0].shape
    count = len(pieces)
    per = count * piece

    def body(*refs):
        for out, side in zip(refs[-2:], (refs[:count], refs[count:])):
            for k in range(zs):
                for j in range(count):
                    out[pl.ds(k * per + j * piece, piece), :] = side[j][k]

    return kernel(
        name,
        body,
        1,
        [(a, (zs, piece, width), (0, 0, 0)) for a in (*pieces, *others)],
        [((zs * per, width), BF16, (zs * per, width), (0, 0))] * 2,
    )


def pass_on(above, below):
    _, per, hid = above.shape

    def body(above, below, act, grad):
        act[...] = above[0]
        grad[...] = below[0]

    return kernel(
        "pass_on",
        body,
        1,
        [(above, (1, per, hid), (0, 0, 0)), (below, (1, per, hid), (1, 0, 0))],
        [((per, hid), BF16, (per, hid), (0, 0))] * 2,
    )


def products(own, other, wi, wo):
    rows, width = own.shape
    feat, hid = wi.shape
    half, per, block = width // 2, rows // 4, hid // STEPS

    def body(own, other, wi, wo, pg, up, down, tok, cot):
        @pl.when(pl.program_id(0) == 0)
        def _():
            for side, ref in enumerate((own, other)):
                tok[:, side * half : (side + 1) * half] = ref[:, :half]
                cot[:, side * half : (side + 1) * half] = ref[:, half:]

        p = jnp.dot(tok[...], wi[...], preferred_element_type=F32)
        g = dot(cot[...], wo[...], 1, 1)
        pg[0] = p
        pg[1] = g
        up[...] = p[2 * per : 3 * per].astype(BF16)
        down[...] = g[2 * per : 3 * per].astype(BF16)

    whole = (rows, width)
    return kernel(
        "products",
        body,
        STEPS,
        [(own, whole, (0, 0)), (other, whole, (0, 0)), (wi, (feat, block), (0, "i")), (wo, (block, feat), ("i", 0))],
        [
            ((2, rows, hid), F32, (2, rows, block), (0, 0, "i")),
            ((per, hid), BF16, (per, block), (0, "i")),
            ((per, hid), BF16, (per, block), (0, "i")),
            ((rows, feat), BF16, (rows, feat), (0, 0)),
            ((rows, feat), BF16, (rows, feat), (0, 0)),
        ],
    )


def ring_add(pg, up, down):
    per, hid = up.shape
    block = hid // STEPS

    def body(one, three, up, down, up_out, down_out):
        up_out[0] = (one[0] + up[...].astype(F32)).astype(BF16)
        up_out[1] = one[1].astype(BF16)
        down_out[0] = three[0].astype(BF16)
        down_out[1] = (three[1] + down[...].astype(F32)).astype(BF16)

    part = (2, per, block)
    return kernel(
        "ring_add",
        body,
        STEPS,
        [(pg, part, (0, 1, "i")), (pg, part, (0, 3, "i")), (up, (per, block), (0, "i")), (down, (per, block), (0, "i"))],
        [((2, per, hid), BF16, part, (0, 0, "i"))] * 2,
    )


def own_sum(pg, up, down):
    _, per, hid = up.shape
    part = (2, per, hid // STEPS)

    def body(zero, up, down, out, sent):
        total = zero[...] + up[...].astype(F32) + down[...].astype(F32)
        out[...] = total
        sent[...] = total.astype(BF16)

    return kernel(
        "own_sum",
        body,
        STEPS,
        [(pg, part, (0, 0, "i")), (up, part, (0, 0, "i")), (down, part, (0, 0, "i"))],
        [((2, per, hid), F32, part, (0, 0, "i")), ((2, per, hid), BF16, part, (0, 0, "i"))],
    )


def hidden(total, other):
    _, per, hid = total.shape
    part = (2, per, hid // STEPS)

    def body(total, other, out):
        pre = total[0] + other[0].astype(F32)
        act_grad = total[1] + other[1].astype(F32)
        cdf, pdf = gelu_parts(pre)
        out[0] = (pre * cdf).astype(BF16)
        out[1] = (act_grad * (cdf + pre * pdf)).astype(BF16)

    return kernel(
        "hidden",
        body,
        STEPS,
        [(total, part, (0, 0, "i")), (other, part, (0, 0, "i"))],
        [((2, per, hid), BF16, part, (0, 0, "i"))],
    )[0]


def input_part(name, mine, above, grad2, below, wi):
    _, per, hid = mine.shape
    half = wi.shape[0] // 2

    def body(mine, above, grad2, below, wi, own, other):
        for step, out in enumerate((own, other)):

            @pl.when(pl.program_id(0) == step)
            def _():
                for k, grad in enumerate((mine.at[0], above.at[0], grad2, below.at[0])):
                    out[k * per : (k + 1) * per] = dot(grad[...], wi[...], 1, 1)

    second, whole = (1, per, hid), (4 * per, half)
    return kernel(
        name,
        body,
        2,
        [
            (mine, second, (1, 0, 0)),
            (above, second, (1, 0, 0)),
            (grad2, (per, hid), (0, 0)),
            (below, second, (1, 0, 0)),
            (wi, (half, hid), ("i", 0)),
        ],
        [(whole, F32, whole, (0, 0))] * 2,
    )


def returns(near, near_got, far, far_got, row):
    rows, feat = near.shape
    piece = rows // 16

    def body(row, near, near_got, far, far_got, out):
        here = row[0] % 2
        for at, mine, got in ((here, near, near_got), (1 - here, far, far_got)):
            out[at] = (mine[...] + got[...]).reshape(4 * piece, feat).astype(BF16)

    split = lambda a: a.reshape(4, 4, piece, feat)
    block = (4, 1, piece, feat)
    return kernel(
        "returns",
        body,
        4,
        [(split(a), block, (0, "i", 0, 0)) for a in (near, near_got, far, far_got)],
        [((8, 4 * piece, feat), BF16, (2, 4 * piece, feat), (lambda i, r: (r // 2 + i) % 4, 0, 0))],
        scalar=row,
    )[0]


def weight_grads(name, tok, cot, blocks, sums=None):
    rows, feat = tok.shape
    _, per, hid = blocks[0].shape
    half, block = feat // 2, hid // STEPS
    last = sums is not None

    def body(tok, cot, *refs):
        parts, refs = refs[:8], refs[8:]
        act, grad = refs[-2:]
        for k in range(4):
            for ref, out in zip(parts[2 * k : 2 * k + 2], (act, grad)):
                out[pl.ds(k * per, per), :] = ref[0] if len(ref.shape) == 3 else ref[...]
        wi = dot(tok[...], grad[...], 0, 0)
        wo = dot(act[...], cot[...], 0, 0)
        if not last:
            refs[0][...] = wi
            refs[1][...] = wo
        else:
            wi = (wi + refs[0][...]).astype(BF16)
            wo = (wo + refs[1][...]).astype(BF16)
            refs[2][...], refs[3][...] = wi[:half], wi[half:]
            refs[4][...], refs[5][...] = wo[:, :half], wo[:, half:]

    mine, above, act2, grad2, below = blocks
    ins = [(tok, (rows, feat), (0, 0)), (cot, (rows, feat), (0, 0))]
    for pair in (mine, above, (act2, grad2), below):
        if isinstance(pair, tuple):
            ins += [(a, (per, block), (0, "i")) for a in pair]
        else:
            ins += [(pair, (1, per, block), (k, 0, "i")) for k in (0, 1)]
    if last:
        ins += [(sums[0], (feat, block), (0, "i")), (sums[1], (block, feat), ("i", 0))]
        outs = [((half, hid), BF16, (half, block), (0, "i"))] * 2 + [((hid, half), BF16, (block, half), ("i", 0))] * 2
    else:
        outs = [((feat, hid), F32, (feat, block), (0, "i")), ((hid, feat), F32, (block, feat), ("i", 0))]
    return kernel(name, body, STEPS, ins, outs, [pltpu.VMEM((rows, block), BF16)] * 2)


def place(wi_own, wi_got, wo_own, wo_got, core):
    half, hid = wi_own.shape

    def body(core, wi_own, wi_got, wo_own, wo_got, wi, wo):
        mine = pl.program_id(0) // STEPS == core[0]

        @pl.when(mine)
        def _():
            wi[...] = wi_own[...]
            wo[...] = wo_own[...]

        @pl.when(jnp.logical_not(mine))
        def _():
            wi[...] = wi_got[...]
            wo[...] = wo_got[...]

    block = hid // STEPS
    at = lambda i, c: i % STEPS
    across, down = ((half, block), (0, at)), ((block, half), (at, 0))
    return kernel(
        "place",
        body,
        2 * STEPS,
        [(wi_own, *across), (wi_got, *across), (wo_own, *down), (wo_got, *down)],
        [((half, 2 * hid), BF16, (half, block), (0, "i")), ((2 * hid, half), BF16, (block, half), ("i", 0))],
        scalar=core,
    )


def local(tokens, cotangent, w_in, w_out):
    z, core = lax.axis_index("z"), lax.axis_index("core")
    rows, feat = tokens.shape
    hid = w_in.shape[1] // 2
    piece = rows // 4

    def relative(a, sign):
        return jnp.roll(a.reshape(4, piece, a.shape[-1]), sign * z, 0)

    def to_core(parts):
        return [shift(a, "core", 1) for a in parts]

    def up_down(up, down):
        return shift(up, "z", 1), shift(down, "z", -1)

    def send_mine(mine):
        return shift(mine, "z", -1), shift(mine, "z", 1)

    def send_on(above, below):
        act, grad = pass_on(above, below)
        return shift(act, "z", -1), shift(grad, "z", 1), act

    at_core = jnp.reshape(core, (1,)).astype(jnp.int32)
    at_row = jnp.reshape(lax.axis_index(ROWS), (1,)).astype(jnp.int32)
    own = relative(jnp.concatenate([tokens, cotangent], 1), -1)
    across = shift(own, "xh", 1)
    near = [shift(own, "y", -d) for d in (1, 2, 3)]
    packed = pack(*gate((w_in, w_out), own), at_core)
    got = shift(packed, "core", 1)
    across = gate(across, packed)
    far = [shift(across, "y", -d) for d in (1, 2, 3)]
    wi, wo = weights(w_in, w_out, gate(got, across), at_core)
    near = [own, *gate(near, wi)]
    near = join("join_a", near, to_core(near))

    pg_a, up_a, down_a, tok_a, cot_a = products(*near, wi, wo)
    r_a = up_down(up_a, down_a)

    far = gate([across, *far], up_a)
    far = join("join_b", far, to_core(far))
    pg_b, up_b, down_b, tok_b, cot_b = products(*far, wi, wo)
    r_b = up_down(up_b, down_b)

    m_a = ring_add(pg_a, *gate(r_a, up_b))
    r_a = up_down(*m_a)
    m_b = ring_add(pg_b, *gate(r_b, m_a))
    r_b = up_down(*m_b)

    t_a, m_a = own_sum(pg_a, *gate(r_a, m_b))
    x_a = shift(m_a, "xl", 1)
    t_b, m_b = own_sum(pg_b, *gate(r_b, m_a))
    x_b = shift(m_b, "xl", 1)

    mine_a = hidden(t_a, gate(x_a, m_b))
    s_a = send_mine(mine_a)
    mine_b = hidden(t_b, gate(x_b, mine_a))
    s_b = send_mine(mine_b)

    s_a = gate(s_a, mine_b)
    f_a = send_on(*s_a)[:2]
    s_b = gate(s_b, s_a)
    f_b = send_on(*s_b)

    f_a = gate(f_a, f_b[2])
    in_a, in_a_other = input_part("input_a", mine_a, s_a[0], f_a[1], s_a[1], wi)
    in_a_got = shift(in_a_other, "core", 1)
    sums = weight_grads("grads_a", tok_a, cot_a, gate((mine_a, s_a[0], *f_a, s_a[1]), in_a_other))

    f_b = gate(f_b[:2], sums)
    in_b, in_b_other = input_part("input_b", mine_b, s_b[0], f_b[1], s_b[1], wi)
    in_b_got = shift(in_b_other, "core", 1)
    blocks = gate((mine_b, s_b[0], *f_b, s_b[1]), in_b_other)
    wi_own, wi_other, wo_own, wo_other = weight_grads("grads_b", tok_b, cot_b, blocks, sums)
    wi_got, wo_got = to_core((wi_other, wo_other))

    in_a_got, in_b_got = gate((in_a_got, in_b_got), wi_own)
    back = returns(in_a, in_a_got, in_b, in_b_got, at_row)
    back = lax.all_to_all(back, ROWS, 0, 0, tiled=True)
    w_in_grad, w_out_grad = place(wi_own, gate(wi_got, back), wo_own, wo_got, at_core)
    input_grad = relative(jnp.sum(back.astype(F32), 0), 1).reshape(rows, feat).astype(BF16)
    return (input_grad, w_in_grad, w_out_grad)


def solution(mesh):
    fine = Mesh(mesh.devices.reshape(SIZES), AXES)
    return jax.shard_map(
        local,
        mesh=fine,
        in_specs=(P(ROWS, COLS), P(ROWS, COLS), P(COLS, ROWS), P(ROWS, COLS)),
        out_specs=(P(ROWS, COLS), P(COLS, ROWS), P(ROWS, COLS)),
        check_vma=False,
    )
```

```python
import jax
import jax.numpy as jnp
from jax import lax
from jax.experimental import pallas as pl
from jax.experimental.pallas import tpu as pltpu
from jax.sharding import Mesh
from jax.sharding import PartitionSpec as P

AXES = ("y", "xh", "xl", "z", "core")
SIZES = (4, 2, 2, 4, 2)
ROWS = ("y", "xh")
COLS = ("xl", "z", "core")
F32 = jnp.float32
BF16 = jnp.bfloat16
STEPS = 3


def gelu_parts(pre):
    cdf = 0.5 * (1.0 + lax.erf(pre * 0.7071067811865476))
    pdf = jnp.exp(-0.5 * pre * pre) * 0.3989422804014327
    return (cdf, pdf)


def shift(x, axis, by):
    n = SIZES[AXES.index(axis)]
    return lax.ppermute(x, axis, [(i, (i + by) % n) for i in range(n)])


def dot(a, b, da, db):
    return lax.dot_general(a, b, (((da,), (db,)), ((), ())), preferred_element_type=F32)


def gate(value, *after):
    return lax.optimization_barrier((value, after))[0]


COST = dict(pack=0.1, weights=0.1, join=0.1, products=0.1, ring_add=0.1, own_sum=0.1, hidden=0.1, pass_on=0.1, input_a=0.1, input_b=20, grads_a=0.1, grads_b=0.1, return_a=0.1, return_b=20, place=0.1)


def kernel(name, body, grid, ins, outs, scratch=(), scalar=None):
    def spec(block, index):
        def at(i, *refs):
            return tuple(i if k == "i" else k(i, *(r[0] for r in refs)) if callable(k) else k for k in index)

        return pl.BlockSpec(block, at)

    return pl.pallas_call(
        body,
        name=name,
        grid_spec=pltpu.PrefetchScalarGridSpec(
            num_scalar_prefetch=0 if scalar is None else 1,
            grid=(grid,),
            in_specs=[spec(block, index) for _, block, index in ins],
            out_specs=[spec(block, index) for _, _, block, index in outs],
            scratch_shapes=list(scratch),
        ),
        out_shape=[jax.ShapeDtypeStruct(shape, dtype) for shape, dtype, _, _ in outs],
        cost_estimate=pl.CostEstimate(flops=0, bytes_accessed=int(COST[name] * 3.69e6), transcendentals=0),
        compiler_params=pltpu.CompilerParams(vmem_limit_bytes=24 * 2**20),
    )(*([] if scalar is None else [scalar]), *[a for a, _, _ in ins])


def pack(w_in, w_out, core):
    feat = w_in.shape[0]
    half = w_out.shape[0] // feat // 2

    def body(_, wi, wo, out):
        out[0, 0] = wi[...]
        out[1, 0] = wo[...]

    block = (feat, feat)
    place = lambda i, c: (1 - c) * half + i
    return kernel(
        "pack",
        body,
        half,
        [(w_in, block, (0, place)), (w_out, block, (place, 0))],
        [((2, half, feat, feat), BF16, (2, 1, feat, feat), (0, "i", 0, 0))],
        scalar=core,
    )[0]


def weights(w_in, w_out, got, core):
    feat = w_in.shape[0]
    half = w_out.shape[0] // feat // 2

    def body(_, wi, wo, got, wi_out, wo_out):
        wi_out[:feat] = wi[...]
        wi_out[feat:] = got[0, 0]
        wo_out[:, :feat] = wo[...]
        wo_out[:, feat:] = got[1, 0]

    block = (feat, feat)
    place = lambda i, c: c * half + i
    return kernel(
        "weights",
        body,
        half,
        [(w_in, block, (0, place)), (w_out, block, (place, 0)), (got, (2, 1, feat, feat), (0, "i", 0, 0))],
        [
            ((2 * feat, half * feat), BF16, (2 * feat, feat), (0, "i")),
            ((half * feat, 2 * feat), BF16, (feat, 2 * feat), ("i", 0)),
        ],
        scalar=core,
    )


def pass_on(above, below):
    _, per, hid = above.shape

    def body(above, below, act, grad):
        act[...] = above[0]
        grad[...] = below[0]

    return kernel(
        "pass_on",
        body,
        1,
        [(above, (1, per, hid), (0, 0, 0)), (below, (1, per, hid), (1, 0, 0))],
        [((per, hid), BF16, (per, hid), (0, 0))] * 2,
    )


def products(own, other, wi, wo, row, side):
    count, per, width = own.shape
    feat, hid = wi.shape
    half, block, pieces = width // 2, hid // STEPS, count // 2
    piece, rows = per // 4, per * pieces

    def body(_, *refs):
        sides, (wi, wo, pg, up, down, tok, cot) = refs[: 2 * pieces], refs[2 * pieces :]

        @pl.when(pl.program_id(0) == 0)
        def _():
            for k in range(4):
                for j, ref in enumerate(sides):
                    at = pl.ds(k * per + j % pieces * piece, piece)
                    columns = slice(j // pieces * half, (j // pieces + 1) * half)
                    part = ref[0, k * piece : (k + 1) * piece, :]
                    tok[at, columns] = part[:, :half]
                    cot[at, columns] = part[:, half:]

        p = jnp.dot(tok[...], wi[...], preferred_element_type=F32)
        g = dot(cot[...], wo[...], 1, 1)
        pg[0] = p
        pg[1] = g
        up[...] = p[2 * per : 3 * per].astype(BF16)
        down[...] = g[2 * per : 3 * per].astype(BF16)

    def at(d):
        return lambda i, r: (r // 2 + d) % 4 * 2 + (r + side) % 2

    return kernel(
        "products",
        body,
        STEPS,
        [(a, (1, per, width), (at(d), 0, 0)) for a in (own, other) for d in range(pieces)]
        + [(wi, (feat, block), (0, "i")), (wo, (block, feat), ("i", 0))],
        [
            ((2, rows, hid), F32, (2, rows, block), (0, 0, "i")),
            ((per, hid), BF16, (per, block), (0, "i")),
            ((per, hid), BF16, (per, block), (0, "i")),
            ((rows, feat), BF16, (rows, feat), (0, 0)),
            ((rows, feat), BF16, (rows, feat), (0, 0)),
        ],
        scalar=row,
    )


def ring_add(pg, up, down):
    per, hid = up.shape
    block = hid // STEPS

    def body(one, three, up, down, up_out, down_out):
        up_out[0] = (one[0] + up[...].astype(F32)).astype(BF16)
        up_out[1] = one[1].astype(BF16)
        down_out[0] = three[0].astype(BF16)
        down_out[1] = (three[1] + down[...].astype(F32)).astype(BF16)

    part = (2, per, block)
    return kernel(
        "ring_add",
        body,
        STEPS,
        [(pg, part, (0, 1, "i")), (pg, part, (0, 3, "i")), (up, (per, block), (0, "i")), (down, (per, block), (0, "i"))],
        [((2, per, hid), BF16, part, (0, 0, "i"))] * 2,
    )


def own_sum(pg, up, down):
    _, per, hid = up.shape
    part = (2, per, hid // STEPS)

    def body(zero, up, down, out, sent):
        total = zero[...] + up[...].astype(F32) + down[...].astype(F32)
        out[...] = total
        sent[...] = total.astype(BF16)

    return kernel(
        "own_sum",
        body,
        STEPS,
        [(pg, part, (0, 0, "i")), (up, part, (0, 0, "i")), (down, part, (0, 0, "i"))],
        [((2, per, hid), F32, part, (0, 0, "i")), ((2, per, hid), BF16, part, (0, 0, "i"))],
    )


def hidden(total, other):
    _, per, hid = total.shape
    part = (2, per, hid // STEPS)

    def body(total, other, out):
        pre = total[0] + other[0].astype(F32)
        act_grad = total[1] + other[1].astype(F32)
        cdf, pdf = gelu_parts(pre)
        out[0] = (pre * cdf).astype(BF16)
        out[1] = (act_grad * (cdf + pre * pdf)).astype(BF16)

    return kernel(
        "hidden",
        body,
        STEPS,
        [(total, part, (0, 0, "i")), (other, part, (0, 0, "i"))],
        [((2, per, hid), BF16, part, (0, 0, "i"))],
    )[0]


def input_part(name, mine, above, grad2, below, wi, pieces):
    _, per, hid = mine.shape
    half = wi.shape[0] // 2
    width = half // pieces

    def body(mine, above, grad2, below, wi, own, *others):
        grads = (mine.at[0], above.at[0], grad2, below.at[0])

        @pl.when(pl.program_id(0) == 0)
        def _():
            for k, grad in enumerate(grads):
                part = dot(grad[...], wi[...], 1, 1)
                for j, other in enumerate(others):
                    other[k * per : (k + 1) * per] = part[:, j * width : (j + 1) * width]

        @pl.when(pl.program_id(0) == 1)
        def _():
            for k, grad in enumerate(grads):
                own[k * per : (k + 1) * per] = dot(grad[...], wi[...], 1, 1)

    second, whole, part = (1, per, hid), (4 * per, half), (4 * per, width)
    own, *others = kernel(
        name,
        body,
        2,
        [
            (mine, second, (1, 0, 0)),
            (above, second, (1, 0, 0)),
            (grad2, (per, hid), (0, 0)),
            (below, second, (1, 0, 0)),
            (wi, (half, hid), (lambda i: 1 - i, 0)),
        ],
        [(whole, F32, whole, (0, 0))] + [(part, F32, part, (0, 0))] * pieces,
    )
    return own, others


def return_pieces(name, mine, got, kinds):
    rows, feat = mine.shape
    width, pieces = got[0].shape[1], len(kinds)
    piece = rows // 4 // pieces

    def body(mine, *refs):
        for j, out in enumerate(refs[len(got) :]):
            for k in range(4):
                at = pl.ds((k * pieces + j) * piece, piece)
                for c, ref in enumerate(refs[: len(got)]):
                    columns = slice(c * width, (c + 1) * width)
                    out[k, :, columns] = (mine[at, columns] + ref[at, :]).astype(out.dtype)

    part = (4, piece, feat)
    return kernel(
        name,
        body,
        1,
        [(mine, (rows, feat), (0, 0))] + [(a, (rows, width), (0, 0)) for a in got],
        [(part, kind, part, (0, 0, 0)) for kind in kinds],
    )


def weight_grads(name, tok, cot, blocks, sums=None):
    rows, feat = tok.shape
    _, per, hid = blocks[0].shape
    half, block = feat // 2, hid // STEPS
    last = sums is not None

    def body(tok, cot, *refs):
        parts, refs = refs[:8], refs[8:]
        act, grad = refs[-2:]
        for k in range(4):
            for ref, out in zip(parts[2 * k : 2 * k + 2], (act, grad)):
                out[pl.ds(k * per, per), :] = ref[0] if len(ref.shape) == 3 else ref[...]
        wi = dot(tok[...], grad[...], 0, 0)
        wo = dot(act[...], cot[...], 0, 0)
        if not last:
            refs[0][...] = wi
            refs[1][...] = wo
        else:
            wi = (wi + refs[0][...]).astype(BF16)
            wo = (wo + refs[1][...]).astype(BF16)
            refs[2][...], refs[3][...] = wi[:half], wi[half:]
            refs[4][...], refs[5][...] = wo[:, :half], wo[:, half:]

    mine, above, act2, grad2, below = blocks
    ins = [(tok, (rows, feat), (0, 0)), (cot, (rows, feat), (0, 0))]
    for pair in (mine, above, (act2, grad2), below):
        if isinstance(pair, tuple):
            ins += [(a, (per, block), (0, "i")) for a in pair]
        else:
            ins += [(pair, (1, per, block), (k, 0, "i")) for k in (0, 1)]
    if last:
        ins += [(sums[0], (feat, block), (0, "i")), (sums[1], (block, feat), ("i", 0))]
        outs = [((half, hid), BF16, (half, block), (0, "i"))] * 2 + [((hid, half), BF16, (block, half), ("i", 0))] * 2
    else:
        outs = [((feat, hid), F32, (feat, block), (0, "i")), ((hid, feat), F32, (block, feat), ("i", 0))]
    return kernel(name, body, STEPS, ins, outs, [pltpu.VMEM((rows, block), BF16)] * 2)


def place(wi_own, wi_got, wo_own, wo_got, core):
    half, hid = wi_own.shape

    def body(core, wi_own, wi_got, wo_own, wo_got, wi, wo):
        mine = pl.program_id(0) // STEPS == core[0]

        @pl.when(mine)
        def _():
            wi[...] = wi_own[...]
            wo[...] = wo_own[...]

        @pl.when(jnp.logical_not(mine))
        def _():
            wi[...] = wi_got[...]
            wo[...] = wo_got[...]

    block = hid // STEPS
    at = lambda i, c: i % STEPS
    across, down = ((half, block), (0, at)), ((block, half), (at, 0))
    return kernel(
        "place",
        body,
        2 * STEPS,
        [(wi_own, *across), (wi_got, *across), (wo_own, *down), (wo_got, *down)],
        [((half, 2 * hid), BF16, (half, block), (0, "i")), ((2 * hid, half), BF16, (block, half), ("i", 0))],
        scalar=core,
    )


def local(tokens, cotangent, w_in, w_out):
    z, core = lax.axis_index("z"), lax.axis_index("core")
    rows, feat = tokens.shape
    hid = w_in.shape[1] // 2
    piece = rows // 4

    def relative(a, sign):
        return jnp.roll(a.reshape(4, piece, a.shape[-1]), sign * z, 0)

    def to_core(parts):
        return [shift(a, "core", 1) for a in parts]

    def up_down(up, down):
        return shift(up, "z", 1), shift(down, "z", -1)

    def send_mine(mine):
        return shift(mine, "z", -1), shift(mine, "z", 1)

    def send_on(above, below):
        act, grad = pass_on(above, below)
        return shift(act, "z", -1), shift(grad, "z", 1), act

    at_core = jnp.reshape(core, (1,)).astype(jnp.int32)
    at_row = jnp.reshape(lax.axis_index(ROWS), (1,)).astype(jnp.int32)
    own = relative(jnp.concatenate([tokens, cotangent], 1), -1).reshape(1, rows, 2 * feat)
    every = lax.all_to_all(jnp.broadcast_to(own, (8, rows, 2 * feat)), ROWS, 0, 0, tiled=True)
    packed = pack(w_in, w_out, at_core)
    wi, wo = weights(w_in, w_out, shift(packed, "core", 1), at_core)
    every = gate(every, wi)
    every_other = shift(every, "core", 1)

    pg_a, up_a, down_a, tok_a, cot_a = products(every, every_other, wi, wo, at_row, 0)
    r_a = up_down(up_a, down_a)
    every, every_other = gate((every, every_other), up_a)
    pg_b, up_b, down_b, tok_b, cot_b = products(every, every_other, wi, wo, at_row, 1)
    r_b = up_down(up_b, down_b)

    m_a = ring_add(pg_a, *gate(r_a, up_b))
    r_a = up_down(*m_a)
    m_b = ring_add(pg_b, *gate(r_b, m_a))
    r_b = up_down(*m_b)

    t_a, m_a = own_sum(pg_a, *gate(r_a, m_b))
    x_a = shift(m_a, "xl", 1)
    t_b, m_b = own_sum(pg_b, *gate(r_b, m_a))
    x_b = shift(m_b, "xl", 1)

    mine_a = hidden(t_a, gate(x_a, m_b))
    s_a = send_mine(mine_a)
    mine_b = hidden(t_b, gate(x_b, mine_a))
    s_b = send_mine(mine_b)

    s_a = gate(s_a, mine_b)
    f_a = send_on(*s_a)[:2]
    s_b = gate(s_b, s_a)
    f_b = send_on(*s_b)

    f_a = gate(f_a, f_b[2])
    in_a, others = input_part("input_a", mine_a, s_a[0], f_a[1], s_a[1], wi, 3)
    kept, *back = return_pieces("return_a", in_a, to_core(others), (F32, BF16, BF16, BF16))
    sums = weight_grads("grads_a", tok_a, cot_a, gate((mine_a, s_a[0], *f_a, s_a[1]), back), None)
    back = [shift(a, "y", d) for d, a in zip((1, 2, 3), back)]

    f_b, back = gate((f_b[:2], back), sums)
    in_b, others = input_part("input_b", mine_b, s_b[0], f_b[1], s_b[1], wi, 1)
    others_got = to_core(others)
    blocks = gate((mine_b, s_b[0], *f_b, s_b[1]), others)
    wi_own, wi_other, wo_own, wo_other = weight_grads("grads_b", tok_b, cot_b, blocks, sums)
    far = return_pieces("return_b", in_b, gate(others_got, wi_own), (BF16,) * 4)
    wi_got, wo_got = to_core(gate((wi_other, wo_other), far))
    far = [
        lax.ppermute(a, ROWS, [(i, ((i // 2 + d) % 4) * 2 + (i + 1) % 2) for i in range(8)])
        for d, a in enumerate(far)
    ]
    w_in_grad, w_out_grad = place(wi_own, wi_got, wo_own, wo_got, at_core)

    total = kept
    for part in back + gate(far, w_in_grad):
        total = total + part.astype(F32)
    input_grad = relative(total, 1).reshape(rows, feat).astype(BF16)
    return (input_grad, w_in_grad, w_out_grad)


def solution(mesh):
    fine = Mesh(mesh.devices.reshape(SIZES), AXES)
    return jax.shard_map(
        local,
        mesh=fine,
        in_specs=(P(ROWS, COLS), P(ROWS, COLS), P(COLS, ROWS), P(ROWS, COLS)),
        out_specs=(P(ROWS, COLS), P(COLS, ROWS), P(ROWS, COLS)),
        check_vma=False,
    )
```

```python
import jax
import jax.numpy as jnp
from jax import lax
from jax.experimental import pallas as pl
from jax.experimental.pallas import tpu as pltpu
from jax.sharding import Mesh
from jax.sharding import PartitionSpec as P

AXES = ("y", "xh", "xl", "z", "core")
SIZES = (4, 2, 2, 4, 2)
ROWS = ("y", "xh")
COLS = ("xl", "z", "core")
F32 = jnp.float32
BF16 = jnp.bfloat16
STEPS = 3


def gelu_parts(pre):
    cdf = 0.5 * (1.0 + lax.erf(pre * 0.7071067811865476))
    pdf = jnp.exp(-0.5 * pre * pre) * 0.3989422804014327
    return (cdf, pdf)


def shift(x, axis, by):
    n = SIZES[AXES.index(axis)]
    return lax.ppermute(x, axis, [(i, (i + by) % n) for i in range(n)])


def dot(a, b, da, db):
    return lax.dot_general(a, b, (((da,), (db,)), ((), ())), preferred_element_type=F32)


def gate(value, *after):
    return lax.optimization_barrier((value, after))[0]


COST = dict(pack=0.1, weights=20, join_a=100, join_b=0.1, products=0.1, ring_add=0.1, own_sum=0.1, hidden=0.1, pass_on=0.1, input_a=0.1, input_b=20, grads_a=0.1, grads_b=0.1, return_a=0.1, return_b=20, place=0.1)


def kernel(name, body, grid, ins, outs, scratch=(), scalar=None):
    def spec(block, index):
        def at(i, *refs):
            return tuple(i if k == "i" else k(i, *(r[0] for r in refs)) if callable(k) else k for k in index)

        return pl.BlockSpec(block, at)

    return pl.pallas_call(
        body,
        name=name,
        grid_spec=pltpu.PrefetchScalarGridSpec(
            num_scalar_prefetch=0 if scalar is None else 1,
            grid=(grid,),
            in_specs=[spec(block, index) for _, block, index in ins],
            out_specs=[spec(block, index) for _, _, block, index in outs],
            scratch_shapes=list(scratch),
        ),
        out_shape=[jax.ShapeDtypeStruct(shape, dtype) for shape, dtype, _, _ in outs],
        cost_estimate=pl.CostEstimate(flops=int(COST[name] * 1.15e9), bytes_accessed=int(COST[name] * 3.69e6), transcendentals=0),
        compiler_params=pltpu.CompilerParams(vmem_limit_bytes=24 * 2**20),
    )(*([] if scalar is None else [scalar]), *[a for a, _, _ in ins])


def pack(w_in, w_out, core):
    feat = w_in.shape[0]
    half = w_out.shape[0] // feat // 2

    def body(_, wi, wo, out):
        out[0, 0] = wi[...]
        out[1, 0] = wo[...]

    block = (feat, feat)
    place = lambda i, c: (1 - c) * half + i
    return kernel(
        "pack",
        body,
        half,
        [(w_in, block, (0, place)), (w_out, block, (place, 0))],
        [((2, half, feat, feat), BF16, (2, 1, feat, feat), (0, "i", 0, 0))],
        scalar=core,
    )[0]


def weights(w_in, w_out, got, core):
    feat = w_in.shape[0]
    half = w_out.shape[0] // feat // 2

    def body(_, wi, wo, got, wi_out, wo_out):
        wi_out[:feat] = wi[...]
        wi_out[feat:] = got[0, 0]
        wo_out[:, :feat] = wo[...]
        wo_out[:, feat:] = got[1, 0]

    block = (feat, feat)
    place = lambda i, c: c * half + i
    return kernel(
        "weights",
        body,
        half,
        [(w_in, block, (0, place)), (w_out, block, (place, 0)), (got, (2, 1, feat, feat), (0, "i", 0, 0))],
        [
            ((2 * feat, half * feat), BF16, (2 * feat, feat), (0, "i")),
            ((half * feat, 2 * feat), BF16, (feat, 2 * feat), ("i", 0)),
        ],
        scalar=core,
    )


def pass_on(above, below):
    _, per, hid = above.shape

    def body(above, below, act, grad):
        act[...] = above[0]
        grad[...] = below[0]

    return kernel(
        "pass_on",
        body,
        1,
        [(above, (1, per, hid), (0, 0, 0)), (below, (1, per, hid), (1, 0, 0))],
        [((per, hid), BF16, (per, hid), (0, 0))] * 2,
    )


def join(name, *sides):
    zs, piece, width = sides[0][0].shape
    count = len(sides[0])
    per = count * piece

    def body(*refs):
        for n, out in enumerate(refs[len(sides) * count :]):
            for k in range(zs):
                for j in range(count):
                    out[pl.ds(k * per + j * piece, piece), :] = refs[n * count + j][k]

    return kernel(
        name,
        body,
        1,
        [(a, (zs, piece, width), (0, 0, 0)) for side in sides for a in side],
        [((zs * per, width), BF16, (zs * per, width), (0, 0))] * len(sides),
    )


def products(own, other, wi, wo):
    rows, width = own.shape
    feat, hid = wi.shape
    half, per, block = width // 2, rows // 4, hid // STEPS

    def body(own, other, wi, wo, pg, up, down, tok, cot):
        @pl.when(pl.program_id(0) == 0)
        def _():
            for side, ref in enumerate((own, other)):
                tok[:, side * half : (side + 1) * half] = ref[:, :half]
                cot[:, side * half : (side + 1) * half] = ref[:, half:]

        p = jnp.dot(tok[...], wi[...], preferred_element_type=F32)
        g = dot(cot[...], wo[...], 1, 1)
        pg[0] = p
        pg[1] = g
        up[...] = p[2 * per : 3 * per].astype(BF16)
        down[...] = g[2 * per : 3 * per].astype(BF16)

    whole = (rows, width)
    return kernel(
        "products",
        body,
        STEPS,
        [(own, whole, (0, 0)), (other, whole, (0, 0)), (wi, (feat, block), (0, "i")), (wo, (block, feat), ("i", 0))],
        [
            ((2, rows, hid), F32, (2, rows, block), (0, 0, "i")),
            ((per, hid), BF16, (per, block), (0, "i")),
            ((per, hid), BF16, (per, block), (0, "i")),
            ((rows, feat), BF16, (rows, feat), (0, 0)),
            ((rows, feat), BF16, (rows, feat), (0, 0)),
        ],
    )


def ring_add(pg, up, down):
    per, hid = up.shape
    block = hid // STEPS

    def body(one, three, up, down, up_out, down_out):
        up_out[0] = (one[0] + up[...].astype(F32)).astype(BF16)
        up_out[1] = one[1].astype(BF16)
        down_out[0] = three[0].astype(BF16)
        down_out[1] = (three[1] + down[...].astype(F32)).astype(BF16)

    part = (2, per, block)
    return kernel(
        "ring_add",
        body,
        STEPS,
        [(pg, part, (0, 1, "i")), (pg, part, (0, 3, "i")), (up, (per, block), (0, "i")), (down, (per, block), (0, "i"))],
        [((2, per, hid), BF16, part, (0, 0, "i"))] * 2,
    )


def own_sum(pg, up, down):
    _, per, hid = up.shape
    part = (2, per, hid // STEPS)

    def body(zero, up, down, out, sent):
        total = zero[...] + up[...].astype(F32) + down[...].astype(F32)
        out[...] = total
        sent[...] = total.astype(BF16)

    return kernel(
        "own_sum",
        body,
        STEPS,
        [(pg, part, (0, 0, "i")), (up, part, (0, 0, "i")), (down, part, (0, 0, "i"))],
        [((2, per, hid), F32, part, (0, 0, "i")), ((2, per, hid), BF16, part, (0, 0, "i"))],
    )


def hidden(total, other):
    _, per, hid = total.shape
    part = (2, per, hid // STEPS)

    def body(total, other, out):
        pre = total[0] + other[0].astype(F32)
        act_grad = total[1] + other[1].astype(F32)
        cdf, pdf = gelu_parts(pre)
        out[0] = (pre * cdf).astype(BF16)
        out[1] = (act_grad * (cdf + pre * pdf)).astype(BF16)

    return kernel(
        "hidden",
        body,
        STEPS,
        [(total, part, (0, 0, "i")), (other, part, (0, 0, "i"))],
        [((2, per, hid), BF16, part, (0, 0, "i"))],
    )[0]


def input_part(name, mine, above, grad2, below, wi, pieces):
    _, per, hid = mine.shape
    half = wi.shape[0] // 2
    width = half // pieces

    def body(mine, above, grad2, below, wi, own, *others):
        grads = (mine.at[0], above.at[0], grad2, below.at[0])

        @pl.when(pl.program_id(0) == 0)
        def _():
            for k, grad in enumerate(grads):
                part = dot(grad[...], wi[...], 1, 1)
                for j, other in enumerate(others):
                    other[k * per : (k + 1) * per] = part[:, j * width : (j + 1) * width]

        @pl.when(pl.program_id(0) == 1)
        def _():
            for k, grad in enumerate(grads):
                own[k * per : (k + 1) * per] = dot(grad[...], wi[...], 1, 1)

    second, whole, part = (1, per, hid), (4 * per, half), (4 * per, width)
    own, *others = kernel(
        name,
        body,
        2,
        [
            (mine, second, (1, 0, 0)),
            (above, second, (1, 0, 0)),
            (grad2, (per, hid), (0, 0)),
            (below, second, (1, 0, 0)),
            (wi, (half, hid), (lambda i: 1 - i, 0)),
        ],
        [(whole, F32, whole, (0, 0))] + [(part, F32, part, (0, 0))] * pieces,
    )
    return own, others


def return_pieces(name, mine, got, kinds):
    rows, feat = mine.shape
    width, pieces = got[0].shape[1], len(kinds)
    piece = rows // 4 // pieces

    def body(mine, *refs):
        for j, out in enumerate(refs[len(got) :]):
            for k in range(4):
                at = pl.ds((k * pieces + j) * piece, piece)
                for c, ref in enumerate(refs[: len(got)]):
                    columns = slice(c * width, (c + 1) * width)
                    out[k, :, columns] = (mine[at, columns] + ref[at, :]).astype(out.dtype)

    part = (4, piece, feat)
    return kernel(
        name,
        body,
        1,
        [(mine, (rows, feat), (0, 0))] + [(a, (rows, width), (0, 0)) for a in got],
        [(part, kind, part, (0, 0, 0)) for kind in kinds],
    )


def weight_grads(name, tok, cot, blocks, sums=None):
    rows, feat = tok.shape
    _, per, hid = blocks[0].shape
    half, block = feat // 2, hid // STEPS
    last = sums is not None

    def body(tok, cot, *refs):
        parts, refs = refs[:8], refs[8:]
        act, grad = refs[-2:]
        for k in range(4):
            for ref, out in zip(parts[2 * k : 2 * k + 2], (act, grad)):
                out[pl.ds(k * per, per), :] = ref[0] if len(ref.shape) == 3 else ref[...]
        wi = dot(tok[...], grad[...], 0, 0)
        wo = dot(act[...], cot[...], 0, 0)
        if not last:
            refs[0][...] = wi
            refs[1][...] = wo
        else:
            wi = (wi + refs[0][...]).astype(BF16)
            wo = (wo + refs[1][...]).astype(BF16)
            refs[2][...], refs[3][...] = wi[:half], wi[half:]
            refs[4][...], refs[5][...] = wo[:, :half], wo[:, half:]

    mine, above, act2, grad2, below = blocks
    ins = [(tok, (rows, feat), (0, 0)), (cot, (rows, feat), (0, 0))]
    for pair in (mine, above, (act2, grad2), below):
        if isinstance(pair, tuple):
            ins += [(a, (per, block), (0, "i")) for a in pair]
        else:
            ins += [(pair, (1, per, block), (k, 0, "i")) for k in (0, 1)]
    if last:
        ins += [(sums[0], (feat, block), (0, "i")), (sums[1], (block, feat), ("i", 0))]
        outs = [((half, hid), BF16, (half, block), (0, "i"))] * 2 + [((hid, half), BF16, (block, half), ("i", 0))] * 2
    else:
        outs = [((feat, hid), F32, (feat, block), (0, "i")), ((hid, feat), F32, (block, feat), ("i", 0))]
    return kernel(name, body, STEPS, ins, outs, [pltpu.VMEM((rows, block), BF16)] * 2)


def place(wi_own, wi_got, wo_own, wo_got, core):
    half, hid = wi_own.shape

    def body(core, wi_own, wi_got, wo_own, wo_got, wi, wo):
        mine = pl.program_id(0) // STEPS == core[0]

        @pl.when(mine)
        def _():
            wi[...] = wi_own[...]
            wo[...] = wo_own[...]

        @pl.when(jnp.logical_not(mine))
        def _():
            wi[...] = wi_got[...]
            wo[...] = wo_got[...]

    block = hid // STEPS
    at = lambda i, c: i % STEPS
    across, down = ((half, block), (0, at)), ((block, half), (at, 0))
    return kernel(
        "place",
        body,
        2 * STEPS,
        [(wi_own, *across), (wi_got, *across), (wo_own, *down), (wo_got, *down)],
        [((half, 2 * hid), BF16, (half, block), (0, "i")), ((2 * hid, half), BF16, (block, half), ("i", 0))],
        scalar=core,
    )


def local(tokens, cotangent, w_in, w_out):
    z, core = lax.axis_index("z"), lax.axis_index("core")
    rows, feat = tokens.shape
    hid = w_in.shape[1] // 2
    piece = rows // 4

    def relative(a, sign):
        return jnp.roll(a.reshape(4, piece, a.shape[-1]), sign * z, 0)

    def to_core(parts):
        return [shift(a, "core", 1) for a in parts]

    def up_down(up, down):
        return shift(up, "z", 1), shift(down, "z", -1)

    def send_mine(mine):
        return shift(mine, "z", -1), shift(mine, "z", 1)

    def send_on(above, below):
        act, grad = pass_on(above, below)
        return shift(act, "z", -1), shift(grad, "z", 1), act

    at_core = jnp.reshape(core, (1,)).astype(jnp.int32)
    own = relative(jnp.concatenate([tokens, cotangent], 1), -1)
    near = [own] + [shift(own, "y", -d) for d in (1, 2, 3)]
    across = shift(own, "xh", 1)
    packed = pack(*gate((w_in, w_out), own), at_core)
    got = shift(packed, "core", 1)
    near = join("join_a", near)[0]
    near_other = shift(near, "core", 1)
    across = gate(across, near)
    far = [shift(across, "y", -d) for d in (1, 2, 3)]
    across_other = shift(across, "core", 1)
    wi, wo = weights(w_in, w_out, gate(got, across_other), at_core)

    pg_a, up_a, down_a, tok_a, cot_a = products(near, near_other, wi, wo)
    r_a = up_down(up_a, down_a)

    far = gate(far, up_a)
    far = join("join_b", [across, *far], [across_other, *to_core(far)])
    pg_b, up_b, down_b, tok_b, cot_b = products(*far, wi, wo)
    r_b = up_down(up_b, down_b)

    m_a = ring_add(pg_a, *gate(r_a, up_b))
    r_a = up_down(*m_a)
    m_b = ring_add(pg_b, *gate(r_b, m_a))
    r_b = up_down(*m_b)

    t_a, m_a = own_sum(pg_a, *gate(r_a, m_b))
    x_a = shift(m_a, "xl", 1)
    t_b, m_b = own_sum(pg_b, *gate(r_b, m_a))
    x_b = shift(m_b, "xl", 1)

    mine_a = hidden(t_a, gate(x_a, m_b))
    s_a = send_mine(mine_a)
    mine_b = hidden(t_b, gate(x_b, mine_a))
    s_b = send_mine(mine_b)

    s_a = gate(s_a, mine_b)
    f_a = send_on(*s_a)[:2]
    s_b = gate(s_b, s_a)
    f_b = send_on(*s_b)

    f_a = gate(f_a, f_b[2])
    in_a, others = input_part("input_a", mine_a, s_a[0], f_a[1], s_a[1], wi, 3)
    kept, *back = return_pieces("return_a", in_a, to_core(others), (F32, BF16, BF16, BF16))
    sums = weight_grads("grads_a", tok_a, cot_a, gate((mine_a, s_a[0], *f_a, s_a[1]), back), None)
    back = [shift(a, "y", d) for d, a in zip((1, 2, 3), back)]

    f_b, back = gate((f_b[:2], back), sums)
    in_b, others = input_part("input_b", mine_b, s_b[0], f_b[1], s_b[1], wi, 1)
    others_got = to_core(others)
    blocks = gate((mine_b, s_b[0], *f_b, s_b[1]), others)
    wi_own, wi_other, wo_own, wo_other = weight_grads("grads_b", tok_b, cot_b, blocks, sums)
    far = return_pieces("return_b", in_b, gate(others_got, wi_own), (BF16,) * 4)
    wi_got, wo_got = to_core(gate((wi_other, wo_other), far))
    far = [
        lax.ppermute(a, ROWS, [(i, ((i // 2 + d) % 4) * 2 + (i + 1) % 2) for i in range(8)])
        for d, a in enumerate(far)
    ]
    w_in_grad, w_out_grad = place(wi_own, wi_got, wo_own, wo_got, at_core)

    total = kept
    for part in back + gate(far, w_in_grad):
        total = total + part.astype(F32)
    input_grad = relative(total, 1).reshape(rows, feat).astype(BF16)
    return (input_grad, w_in_grad, w_out_grad)


def solution(mesh):
    fine = Mesh(mesh.devices.reshape(SIZES), AXES)
    return jax.shard_map(
        local,
        mesh=fine,
        in_specs=(P(ROWS, COLS), P(ROWS, COLS), P(COLS, ROWS), P(ROWS, COLS)),
        out_specs=(P(ROWS, COLS), P(COLS, ROWS), P(ROWS, COLS)),
        check_vma=False,
    )
```

```python
import jax
import jax.numpy as jnp
from jax import lax
from jax.experimental import pallas as pl
from jax.experimental.pallas import tpu as pltpu
from jax.sharding import Mesh
from jax.sharding import PartitionSpec as P

AXES = ("y", "xh", "xl", "z", "core")
SIZES = (4, 2, 2, 4, 2)
ROWS = ("y", "xh")
COLS = ("xl", "z", "core")
F32 = jnp.float32
BF16 = jnp.bfloat16
STEPS = 3


def gelu_parts(pre):
    cdf = 0.5 * (1.0 + lax.erf(pre * 0.7071067811865476))
    pdf = jnp.exp(-0.5 * pre * pre) * 0.3989422804014327
    return (cdf, pdf)


def shift(x, axis, by):
    n = SIZES[AXES.index(axis)]
    return lax.ppermute(x, axis, [(i, (i + by) % n) for i in range(n)])


def dot(a, b, da, db):
    return lax.dot_general(a, b, (((da,), (db,)), ((), ())), preferred_element_type=F32)


def gate(value, *after):
    return lax.optimization_barrier((value, after))[0]


COST = dict(pack=0.1, weights=20, join_a=100, join_b=0.1, products=0.1, ring_add=0.1, own_sum=0.1, hidden=0.1, pass_on=0.1, input_three=0.1, input_last=0.1, grads_a=0.1, grads_b=0.1, grads_last=0.1, return_a=0.1, return_b=20, place=0.1)


def kernel(name, body, grid, ins, outs, scratch=(), scalar=None, aliases=None):
    def spec(block, index):
        def at(i, *refs):
            return tuple(i if k == "i" else k(i, *(r[0] for r in refs)) if callable(k) else k for k in index)

        return pl.BlockSpec(memory_space=pl.ANY) if block is None else pl.BlockSpec(block, at)

    return pl.pallas_call(
        body,
        name=name,
        grid_spec=pltpu.PrefetchScalarGridSpec(
            num_scalar_prefetch=0 if scalar is None else 1,
            grid=(grid,),
            in_specs=[spec(block, index) for _, block, index in ins],
            out_specs=[spec(block, index) for _, _, block, index in outs],
            scratch_shapes=list(scratch),
        ),
        out_shape=[jax.ShapeDtypeStruct(shape, dtype) for shape, dtype, _, _ in outs],
        input_output_aliases=aliases or {},
        cost_estimate=pl.CostEstimate(flops=int(COST[name] * 1.15e9), bytes_accessed=int(COST[name] * 3.69e6), transcendentals=0),
        compiler_params=pltpu.CompilerParams(vmem_limit_bytes=24 * 2**20),
    )(*([] if scalar is None else [scalar]), *[a for a, _, _ in ins])


def pack(w_in, w_out, core):
    feat = w_in.shape[0]
    half = w_out.shape[0] // feat // 2

    def body(_, wi, wo, out):
        out[0, 0] = wi[...]
        out[1, 0] = wo[...]

    block = (feat, feat)
    place = lambda i, c: (1 - c) * half + i
    return kernel(
        "pack",
        body,
        half,
        [(w_in, block, (0, place)), (w_out, block, (place, 0))],
        [((2, half, feat, feat), BF16, (2, 1, feat, feat), (0, "i", 0, 0))],
        scalar=core,
    )[0]


def weights(w_in, w_out, got, core):
    feat = w_in.shape[0]
    half = w_out.shape[0] // feat // 2

    def body(_, wi, wo, got, wi_out, wo_out):
        wi_out[:feat] = wi[...]
        wi_out[feat:] = got[0, 0]
        wo_out[:, :feat] = wo[...]
        wo_out[:, feat:] = got[1, 0]

    block = (feat, feat)
    place = lambda i, c: c * half + i
    return kernel(
        "weights",
        body,
        half,
        [(w_in, block, (0, place)), (w_out, block, (place, 0)), (got, (2, 1, feat, feat), (0, "i", 0, 0))],
        [
            ((2 * feat, half * feat), BF16, (2 * feat, feat), (0, "i")),
            ((half * feat, 2 * feat), BF16, (feat, 2 * feat), ("i", 0)),
        ],
        scalar=core,
    )


def pass_on(above, below):
    _, per, hid = above.shape

    def body(above, below, act, grad):
        act[...] = above[0]
        grad[...] = below[0]

    return kernel(
        "pass_on",
        body,
        1,
        [(above, (1, per, hid), (0, 0, 0)), (below, (1, per, hid), (1, 0, 0))],
        [((per, hid), BF16, (per, hid), (0, 0))] * 2,
    )


def join(name, *sides):
    zs, piece, width = sides[0][0].shape
    count = len(sides[0])
    per = count * piece

    def body(*refs):
        for n, out in enumerate(refs[len(sides) * count :]):
            for k in range(zs):
                for j in range(count):
                    out[pl.ds(k * per + j * piece, piece), :] = refs[n * count + j][k]

    return kernel(
        name,
        body,
        1,
        [(a, (zs, piece, width), (0, 0, 0)) for side in sides for a in side],
        [((zs * per, width), BF16, (zs * per, width), (0, 0))] * len(sides),
    )


def products(own, other, wi, wo):
    rows, width = own.shape
    feat, hid = wi.shape
    half, per, block = width // 2, rows // 4, hid // STEPS

    def body(own, other, wi, wo, pg, up, down, tok, cot):
        @pl.when(pl.program_id(0) == 0)
        def _():
            for side, ref in enumerate((own, other)):
                tok[:, side * half : (side + 1) * half] = ref[:, :half]
                cot[:, side * half : (side + 1) * half] = ref[:, half:]

        p = jnp.dot(tok[...], wi[...], preferred_element_type=F32)
        g = dot(cot[...], wo[...], 1, 1)
        pg[0] = p
        pg[1] = g
        up[...] = p[2 * per : 3 * per].astype(BF16)
        down[...] = g[2 * per : 3 * per].astype(BF16)

    whole = (rows, width)
    return kernel(
        "products",
        body,
        STEPS,
        [(own, whole, (0, 0)), (other, whole, (0, 0)), (wi, (feat, block), (0, "i")), (wo, (block, feat), ("i", 0))],
        [
            ((2, rows, hid), F32, (2, rows, block), (0, 0, "i")),
            ((per, hid), BF16, (per, block), (0, "i")),
            ((per, hid), BF16, (per, block), (0, "i")),
            ((rows, feat), BF16, (rows, feat), (0, 0)),
            ((rows, feat), BF16, (rows, feat), (0, 0)),
        ],
    )


def ring_add(pg, up, down):
    per, hid = up.shape
    block = hid // STEPS

    def body(one, three, up, down, up_out, down_out):
        up_out[0] = (one[0] + up[...].astype(F32)).astype(BF16)
        up_out[1] = one[1].astype(BF16)
        down_out[0] = three[0].astype(BF16)
        down_out[1] = (three[1] + down[...].astype(F32)).astype(BF16)

    part = (2, per, block)
    return kernel(
        "ring_add",
        body,
        STEPS,
        [(pg, part, (0, 1, "i")), (pg, part, (0, 3, "i")), (up, (per, block), (0, "i")), (down, (per, block), (0, "i"))],
        [((2, per, hid), BF16, part, (0, 0, "i"))] * 2,
    )


def own_sum(pg, up, down):
    _, per, hid = up.shape
    part = (2, per, hid // STEPS)

    def body(zero, up, down, out, sent):
        total = zero[...] + up[...].astype(F32) + down[...].astype(F32)
        out[...] = total
        sent[...] = total.astype(BF16)

    return kernel(
        "own_sum",
        body,
        STEPS,
        [(pg, part, (0, 0, "i")), (up, part, (0, 0, "i")), (down, part, (0, 0, "i"))],
        [((2, per, hid), F32, part, (0, 0, "i")), ((2, per, hid), BF16, part, (0, 0, "i"))],
    )


def hidden(total, other):
    _, per, hid = total.shape
    part = (2, per, hid // STEPS)

    def body(total, other, out):
        pre = total[0] + other[0].astype(F32)
        act_grad = total[1] + other[1].astype(F32)
        cdf, pdf = gelu_parts(pre)
        out[0] = (pre * cdf).astype(BF16)
        out[1] = (act_grad * (cdf + pre * pdf)).astype(BF16)

    return kernel(
        "hidden",
        body,
        STEPS,
        [(total, part, (0, 0, "i")), (other, part, (0, 0, "i"))],
        [((2, per, hid), BF16, part, (0, 0, "i"))],
    )[0]


def input_three(mine, above, below, wi):
    _, per, hid = mine.shape
    half = wi.shape[0] // 2

    def body(mine, above, below, wi, own, other):
        for step, out in enumerate((own, other)):

            @pl.when(pl.program_id(0) == step)
            def _():
                for k, grad in enumerate((mine, above, below)):
                    out[k] = dot(grad[0], wi[...], 1, 1)

    second, whole = (1, per, hid), (3, per, half)
    return kernel(
        "input_three",
        body,
        2,
        [(a, second, (1, 0, 0)) for a in (mine, above, below)] + [(wi, (half, hid), ("i", 0))],
        [(whole, F32, whole, (0, 0, 0))] * 2,
    )


def input_last(three, grad2, wi, pieces):
    per, hid = grad2.shape
    half = wi.shape[0] // 2
    width = half // pieces

    def body(own3, other3, grad, wi, own, *others):
        for k, at in ((0, 0), (1, 1), (2, 3)):
            rows = pl.ds(at * per, per)
            own[rows, :] = own3[k]
            for j, other in enumerate(others):
                other[rows, :] = other3[k, :, j * width : (j + 1) * width]
        part = dot(grad[...], wi[...], 1, 1)
        rows = pl.ds(2 * per, per)
        own[rows, :] = part[:, :half]
        for j, other in enumerate(others):
            other[rows, :] = part[:, half + j * width : half + (j + 1) * width]

    whole, part = (4 * per, half), (4 * per, width)
    own, *others = kernel(
        "input_last",
        body,
        1,
        [(a, a.shape, (0, 0, 0)) for a in three] + [(a, a.shape, (0, 0)) for a in (grad2, wi)],
        [(whole, F32, whole, (0, 0))] + [(part, F32, part, (0, 0))] * pieces,
    )
    return own, others


def return_pieces(name, mine, got, kinds):
    rows, feat = mine.shape
    width, pieces = got[0].shape[1], len(kinds)
    piece = rows // 4 // pieces

    def body(mine, *refs):
        for j, out in enumerate(refs[len(got) :]):
            for k in range(4):
                at = pl.ds((k * pieces + j) * piece, piece)
                for c, ref in enumerate(refs[: len(got)]):
                    columns = slice(c * width, (c + 1) * width)
                    out[k, :, columns] = (mine[at, columns] + ref[at, :]).astype(out.dtype)

    part = (4, piece, feat)
    return kernel(
        name,
        body,
        1,
        [(mine, (rows, feat), (0, 0))] + [(a, (rows, width), (0, 0)) for a in got],
        [(part, kind, part, (0, 0, 0)) for kind in kinds],
    )


def weight_grads(name, terms, sums=None, core=None):
    per, hid = terms[0][3].shape[-2:]
    feat = terms[0][0].shape[1]
    half, block, count = feat // 2, hid // STEPS, len(terms)
    rows, last = count * per, core is not None

    def body(*refs):
        refs = refs[1:] if last else refs
        given, refs = [refs[k * count : (k + 1) * count] for k in range(4)], refs[4 * count :]
        both = refs[-4:]

        @pl.when(pl.program_id(0) == 0)
        def _():
            for parts, out in zip(given[:2], both[:2]):
                for k, ref in enumerate(parts):
                    out[k * per : (k + 1) * per] = ref[...]

        for parts, out in zip(given[2:], both[2:]):
            for k, ref in enumerate(parts):
                out[k * per : (k + 1) * per] = ref[0] if len(ref.shape) == 3 else ref[...]
        tok, cot, act, grad = both
        wi = dot(tok[...], grad[...], 0, 0)
        wo = dot(act[...], cot[...], 0, 0)
        if sums is not None:
            wi, wo, refs = wi + refs[0][...], wo + refs[1][...], refs[2:]
        if last:
            refs[0][...] = wi[:half].astype(BF16)
            refs[1][...] = wo[:, :half].astype(BF16)
            refs[2][...] = wi[half:].astype(BF16)
            refs[3][...] = wo[:, half:].astype(BF16)
        else:
            refs[0][...] = wi
            refs[1][...] = wo

    def hidden_part(a, which):
        return (a, (1, per, block), (which, 0, "i")) if len(a.shape) == 3 else (a, (per, block), (0, "i"))

    ins = [(term[n], (per, feat), (term[2], 0)) for n in (0, 1) for term in terms]
    ins += [hidden_part(term[3 + which], which) for which in (0, 1) for term in terms]
    if sums is not None:
        ins += [(sums[0], (feat, block), (0, "i")), (sums[1], (block, feat), ("i", 0))]
    if last:
        at = lambda i, c: c * STEPS + i
        outs = [((half, 2 * hid), BF16, (half, block), (0, at)), ((2 * hid, half), BF16, (block, half), (at, 0))]
        outs += [((half, hid), BF16, (half, block), (0, "i")), ((hid, half), BF16, (block, half), ("i", 0))]
    else:
        outs = [((feat, hid), F32, (feat, block), (0, "i")), ((hid, feat), F32, (block, feat), ("i", 0))]
    scratch = [pltpu.VMEM((rows, feat), BF16)] * 2 + [pltpu.VMEM((rows, block), BF16)] * 2
    return kernel(name, body, STEPS, ins, outs, scratch, core)


def place(wi, wo, wi_got, wo_got, core):
    half, hid = wi_got.shape
    block = hid // STEPS

    def body(core, wi, wo, wi_got, wo_got, wi_out, wo_out):
        wi_out[...] = wi_got[...]
        wo_out[...] = wo_got[...]

    at = lambda i, c: (1 - c) * STEPS + i
    return kernel(
        "place",
        body,
        STEPS,
        [(wi, None, None), (wo, None, None), (wi_got, (half, block), (0, "i")), (wo_got, (block, half), ("i", 0))],
        [(wi.shape, BF16, (half, block), (0, at)), (wo.shape, BF16, (block, half), (at, 0))],
        scalar=core,
        aliases={1: 0, 2: 1},
    )


def local(tokens, cotangent, w_in, w_out):
    z, core = lax.axis_index("z"), lax.axis_index("core")
    rows, feat = tokens.shape
    hid = w_in.shape[1] // 2
    piece = rows // 4

    def relative(a, sign):
        return jnp.roll(a.reshape(4, piece, a.shape[-1]), sign * z, 0)

    def to_core(parts):
        return [shift(a, "core", 1) for a in parts]

    def up_down(up, down):
        return shift(up, "z", 1), shift(down, "z", -1)

    def send_mine(mine):
        return shift(mine, "z", -1), shift(mine, "z", 1)

    def send_on(above, below):
        act, grad = pass_on(above, below)
        return shift(act, "z", -1), shift(grad, "z", 1), act

    at_core = jnp.reshape(core, (1,)).astype(jnp.int32)
    own = relative(jnp.concatenate([tokens, cotangent], 1), -1)
    near = [own] + [shift(own, "y", -d) for d in (1, 2, 3)]
    across = shift(own, "xh", 1)
    packed = pack(*gate((w_in, w_out), own), at_core)
    got = shift(packed, "core", 1)
    near = join("join_a", near)[0]
    near_other = shift(near, "core", 1)
    across = gate(across, near)
    far = [shift(across, "y", -d) for d in (1, 2, 3)]
    across_other = shift(across, "core", 1)
    wi, wo = weights(w_in, w_out, gate(got, across_other), at_core)

    pg_a, up_a, down_a, tok_a, cot_a = products(near, near_other, wi, wo)
    r_a = up_down(up_a, down_a)

    far = gate(far, up_a)
    far = join("join_b", [across, *far], [across_other, *to_core(far)])
    pg_b, up_b, down_b, tok_b, cot_b = products(*far, wi, wo)
    r_b = up_down(up_b, down_b)

    m_a = ring_add(pg_a, *gate(r_a, up_b))
    r_a = up_down(*m_a)
    m_b = ring_add(pg_b, *gate(r_b, m_a))
    r_b = up_down(*m_b)

    t_a, m_a = own_sum(pg_a, *gate(r_a, m_b))
    x_a = shift(m_a, "xl", 1)
    t_b, m_b = own_sum(pg_b, *gate(r_b, m_a))
    x_b = shift(m_b, "xl", 1)

    mine_a = hidden(t_a, gate(x_a, m_b))
    s_a = send_mine(mine_a)
    mine_b = hidden(t_b, gate(x_b, mine_a))
    s_b = send_mine(mine_b)

    s_a = gate(s_a, mine_b)
    *f_a, sent_a = send_on(*s_a)
    three_a = input_three(mine_a, *gate(s_a, sent_a), wi)
    terms = [(tok_a, cot_a, k, a, a) for k, a in zip((0, 1, 3), gate((mine_a, *s_a), three_a))]
    sums = weight_grads("grads_a", terms)

    s_b = gate(s_b, sums)
    *f_b, sent_b = send_on(*s_b)
    three_b = input_three(mine_b, *gate(s_b, sent_b), wi)
    terms = [(tok_b, cot_b, k, a, a) for k, a in zip((0, 1, 3), gate((mine_b, *s_b), three_b))]
    sums = weight_grads("grads_b", terms, sums)

    f_a = gate(f_a, sums)
    in_a, others = input_last(three_a, f_a[1], wi, 3)
    kept, *back = return_pieces("return_a", in_a, to_core(others), (F32, BF16, BF16, BF16))
    back = [shift(a, "y", d) for d, a in zip((1, 2, 3), back)]

    f_b = gate(f_b, kept)
    in_b, others = input_last(three_b, f_b[1], wi, 1)
    others_got = to_core(others)
    f_a, f_b = gate((f_a, f_b), others)
    terms = [(tok_a, cot_a, 2, *f_a), (tok_b, cot_b, 2, *f_b)]
    w_in_grad, w_out_grad, *others = weight_grads("grads_last", terms, sums, at_core)

    others_got, back = gate((others_got, back), others)
    far = return_pieces("return_b", in_b, others_got, (BF16,) * 4)
    got = to_core(gate(others, far))
    far = [
        lax.ppermute(a, ROWS, [(i, ((i // 2 + d) % 4) * 2 + (i + 1) % 2) for i in range(8)])
        for d, a in enumerate(far)
    ]
    w_in_grad, w_out_grad = place(w_in_grad, w_out_grad, *got, at_core)

    total = kept
    for part in back + gate(far, w_in_grad):
        total = total + part.astype(F32)
    input_grad = relative(total, 1).reshape(rows, feat).astype(BF16)
    return (input_grad, w_in_grad, w_out_grad)


def solution(mesh):
    fine = Mesh(mesh.devices.reshape(SIZES), AXES)
    return jax.shard_map(
        local,
        mesh=fine,
        in_specs=(P(ROWS, COLS), P(ROWS, COLS), P(COLS, ROWS), P(ROWS, COLS)),
        out_specs=(P(ROWS, COLS), P(COLS, ROWS), P(ROWS, COLS)),
        check_vma=False,
    )
```

```python
import jax
import jax.numpy as jnp
from jax import lax
from jax.experimental import pallas as pl
from jax.experimental.pallas import tpu as pltpu
from jax.sharding import Mesh
from jax.sharding import PartitionSpec as P

AXES = ("y", "xh", "xl", "z", "core")
SIZES = (4, 2, 2, 4, 2)
ROWS = ("y", "xh")
COLS = ("xl", "z", "core")
F32 = jnp.float32
BF16 = jnp.bfloat16
STEPS = 3


def gelu_parts(pre):
    cdf = 0.5 * (1.0 + lax.erf(pre * 0.7071067811865476))
    pdf = jnp.exp(-0.5 * pre * pre) * 0.3989422804014327
    return (cdf, pdf)


def shift(x, axis, by):
    n = SIZES[AXES.index(axis)]
    return lax.ppermute(x, axis, [(i, (i + by) % n) for i in range(n)])


def dot(a, b, da, db):
    return lax.dot_general(a, b, (((da,), (db,)), ((), ())), preferred_element_type=F32)


def gate(value, *after):
    return lax.optimization_barrier((value, after))[0]


COST = dict(pack=0.1, first_block=0.1, weights=7, join_a=100, join_b=0.1, products=0.1, ring_add=0.1, own_sum=0.1, hidden=0.1, pass_on=0.1, input_three=0.1, input_last=0.1, grads_a=0.1, grads_b=0.1, grads_last=0.1, return_a=0.1, return_b=20, place=0.1)


def kernel(name, body, grid, ins, outs, scratch=(), scalar=None, aliases=None):
    def spec(block, index):
        def at(i, *refs):
            return tuple(i if k == "i" else k(i, *(r[0] for r in refs)) if callable(k) else k for k in index)

        return pl.BlockSpec(memory_space=pltpu.HBM) if block is None else pl.BlockSpec(block, at)

    return pl.pallas_call(
        body,
        name=name,
        grid_spec=pltpu.PrefetchScalarGridSpec(
            num_scalar_prefetch=0 if scalar is None else 1,
            grid=(grid,),
            in_specs=[spec(block, index) for _, block, index in ins],
            out_specs=[spec(block, index) for _, _, block, index in outs],
            scratch_shapes=list(scratch),
        ),
        out_shape=[jax.ShapeDtypeStruct(shape, dtype) for shape, dtype, _, _ in outs],
        input_output_aliases=aliases or {},
        cost_estimate=pl.CostEstimate(flops=int(COST[name] * 1.15e9), bytes_accessed=int(COST[name] * 3.69e6), transcendentals=0),
        compiler_params=pltpu.CompilerParams(vmem_limit_bytes=24 * 2**20),
    )(*([] if scalar is None else [scalar]), *[a for a, _, _ in ins])


def pack(w_in, w_out, core):
    feat = w_in.shape[0]
    half = w_out.shape[0] // feat // 2

    def body(core, wi, wo, out, sems):
        copies = []
        for k in range(half):
            at = pl.ds(pl.multiple_of(((1 - core[0]) * half + k) * feat, feat), feat)
            copies.append(pltpu.make_async_copy(wi.at[:, at], out.at[0, k], sems.at[0, k]))
            copies.append(pltpu.make_async_copy(wo.at[at, :], out.at[1, k], sems.at[1, k]))
        for copy in copies:
            copy.start()
        for copy in copies:
            copy.wait()

    shape = (2, half, feat, feat)
    return kernel(
        "pack",
        body,
        1,
        [(w_in, None, None), (w_out, None, None)],
        [(shape, BF16, shape, (0, 0, 0, 0))],
        [pltpu.SemaphoreType.DMA((2, half))],
        scalar=core,
    )[0]


def weights(w_in, w_out, got, core):
    feat = w_in.shape[0]
    half = w_out.shape[0] // feat // 2

    def body(_, wi, wo, got, wi_out, wo_out):
        wi_out[:feat] = wi[...]
        wi_out[feat:] = got[0, 0]
        wo_out[:, :feat] = wo[...]
        wo_out[:, feat:] = got[1, 0]

    block = (feat, feat)
    place = lambda i, c: c * half + i
    return kernel(
        "weights",
        body,
        half,
        [(w_in, block, (0, place)), (w_out, block, (place, 0)), (got, (2, 1, feat, feat), (0, "i", 0, 0))],
        [
            ((2 * feat, half * feat), BF16, (2 * feat, feat), (0, "i")),
            ((half * feat, 2 * feat), BF16, (feat, 2 * feat), ("i", 0)),
        ],
        scalar=core,
    )


def pass_on(above, below):
    _, per, hid = above.shape

    def body(above, below, act, grad):
        act[...] = above[0]
        grad[...] = below[0]

    return kernel(
        "pass_on",
        body,
        1,
        [(above, (1, per, hid), (0, 0, 0)), (below, (1, per, hid), (1, 0, 0))],
        [((per, hid), BF16, (per, hid), (0, 0))] * 2,
    )


def join(name, *sides):
    zs, piece, width = sides[0][0].shape
    count = len(sides[0])
    per = count * piece

    def body(*refs):
        for n, out in enumerate(refs[len(sides) * count :]):
            for k in range(zs):
                for j in range(count):
                    out[pl.ds(k * per + j * piece, piece), :] = refs[n * count + j][k]

    return kernel(
        name,
        body,
        1,
        [(a, (zs, piece, width), (0, 0, 0)) for side in sides for a in side],
        [((zs * per, width), BF16, (zs * per, width), (0, 0))] * len(sides),
    )


def first_block(own, other, wi, wo):
    rows, width = own.shape
    feat, hid = wi.shape
    half, per, block = width // 2, rows // 4, hid // STEPS

    def body(own, other, wi, wo, up, down):
        tok = jnp.concatenate([own[:, :half], other[:, :half]], 1)
        cot = jnp.concatenate([own[:, half:], other[:, half:]], 1)
        up[...] = jnp.dot(tok, wi[...], preferred_element_type=F32).astype(BF16)
        down[...] = dot(cot, wo[...], 1, 1).astype(BF16)

    part = (per, width)
    return kernel(
        "first_block",
        body,
        STEPS,
        [(own, part, (2, 0)), (other, part, (2, 0)), (wi, (feat, block), (0, "i")), (wo, (block, feat), ("i", 0))],
        [((per, hid), BF16, (per, block), (0, "i"))] * 2,
    )


def products(own, other, wi, wo):
    rows, width = own.shape
    feat, hid = wi.shape
    half, per, block = width // 2, rows // 4, hid // STEPS

    def body(own, other, wi, wo, pg, up, down, tok, cot):
        @pl.when(pl.program_id(0) == 0)
        def _():
            for side, ref in enumerate((own, other)):
                tok[:, side * half : (side + 1) * half] = ref[:, :half]
                cot[:, side * half : (side + 1) * half] = ref[:, half:]

        p = jnp.dot(tok[...], wi[...], preferred_element_type=F32)
        g = dot(cot[...], wo[...], 1, 1)
        pg[0] = p
        pg[1] = g
        up[...] = p[2 * per : 3 * per].astype(BF16)
        down[...] = g[2 * per : 3 * per].astype(BF16)

    whole = (rows, width)
    return kernel(
        "products",
        body,
        STEPS,
        [(own, whole, (0, 0)), (other, whole, (0, 0)), (wi, (feat, block), (0, "i")), (wo, (block, feat), ("i", 0))],
        [
            ((2, rows, hid), F32, (2, rows, block), (0, 0, "i")),
            ((per, hid), BF16, (per, block), (0, "i")),
            ((per, hid), BF16, (per, block), (0, "i")),
            ((rows, feat), BF16, (rows, feat), (0, 0)),
            ((rows, feat), BF16, (rows, feat), (0, 0)),
        ],
    )


def ring_add(pg, up, down):
    per, hid = up.shape
    block = hid // STEPS

    def body(one, three, up, down, up_out, down_out):
        up_out[0] = (one[0] + up[...].astype(F32)).astype(BF16)
        up_out[1] = one[1].astype(BF16)
        down_out[0] = three[0].astype(BF16)
        down_out[1] = (three[1] + down[...].astype(F32)).astype(BF16)

    part = (2, per, block)
    return kernel(
        "ring_add",
        body,
        STEPS,
        [(pg, part, (0, 1, "i")), (pg, part, (0, 3, "i")), (up, (per, block), (0, "i")), (down, (per, block), (0, "i"))],
        [((2, per, hid), BF16, part, (0, 0, "i"))] * 2,
    )


def own_sum(pg, up, down):
    _, per, hid = up.shape
    part = (2, per, hid // STEPS)

    def body(zero, up, down, out, sent):
        total = zero[...] + up[...].astype(F32) + down[...].astype(F32)
        out[...] = total
        sent[...] = total.astype(BF16)

    return kernel(
        "own_sum",
        body,
        STEPS,
        [(pg, part, (0, 0, "i")), (up, part, (0, 0, "i")), (down, part, (0, 0, "i"))],
        [((2, per, hid), F32, part, (0, 0, "i")), ((2, per, hid), BF16, part, (0, 0, "i"))],
    )


def hidden(total, other):
    _, per, hid = total.shape
    part = (2, per, hid // STEPS)

    def body(total, other, out):
        pre = total[0] + other[0].astype(F32)
        act_grad = total[1] + other[1].astype(F32)
        cdf, pdf = gelu_parts(pre)
        out[0] = (pre * cdf).astype(BF16)
        out[1] = (act_grad * (cdf + pre * pdf)).astype(BF16)

    return kernel(
        "hidden",
        body,
        STEPS,
        [(total, part, (0, 0, "i")), (other, part, (0, 0, "i"))],
        [((2, per, hid), BF16, part, (0, 0, "i"))],
    )[0]


def input_three(mine, above, below, wi):
    _, per, hid = mine.shape
    half = wi.shape[0] // 2

    def body(mine, above, below, wi, own, other):
        for step, out in enumerate((own, other)):

            @pl.when(pl.program_id(0) == step)
            def _():
                for k, grad in enumerate((mine, above, below)):
                    out[k] = dot(grad[0], wi[...], 1, 1)

    second, whole = (1, per, hid), (3, per, half)
    return kernel(
        "input_three",
        body,
        2,
        [(a, second, (1, 0, 0)) for a in (mine, above, below)] + [(wi, (half, hid), ("i", 0))],
        [(whole, F32, whole, (0, 0, 0))] * 2,
    )


def input_last(three, grad2, wi, pieces):
    per, hid = grad2.shape
    half = wi.shape[0] // 2
    width = half // pieces

    def body(own3, other3, grad, wi, own, *others):
        for k, at in ((0, 0), (1, 1), (2, 3)):
            rows = pl.ds(at * per, per)
            own[rows, :] = own3[k]
            for j, other in enumerate(others):
                other[rows, :] = other3[k, :, j * width : (j + 1) * width]
        part = dot(grad[...], wi[...], 1, 1)
        rows = pl.ds(2 * per, per)
        own[rows, :] = part[:, :half]
        for j, other in enumerate(others):
            other[rows, :] = part[:, half + j * width : half + (j + 1) * width]

    whole, part = (4 * per, half), (4 * per, width)
    own, *others = kernel(
        "input_last",
        body,
        1,
        [(a, a.shape, (0, 0, 0)) for a in three] + [(a, a.shape, (0, 0)) for a in (grad2, wi)],
        [(whole, F32, whole, (0, 0))] + [(part, F32, part, (0, 0))] * pieces,
    )
    return own, others


def return_pieces(name, mine, got, kinds):
    rows, feat = mine.shape
    width, pieces = got[0].shape[1], len(kinds)
    piece = rows // 4 // pieces

    def body(mine, *refs):
        for j, out in enumerate(refs[len(got) :]):
            for k in range(4):
                at = pl.ds((k * pieces + j) * piece, piece)
                for c, ref in enumerate(refs[: len(got)]):
                    columns = slice(c * width, (c + 1) * width)
                    out[k, :, columns] = (mine[at, columns] + ref[at, :]).astype(out.dtype)

    part = (4, piece, feat)
    return kernel(
        name,
        body,
        1,
        [(mine, (rows, feat), (0, 0))] + [(a, (rows, width), (0, 0)) for a in got],
        [(part, kind, part, (0, 0, 0)) for kind in kinds],
    )


def weight_grads(name, terms, sums=None, core=None):
    per, hid = terms[0][3].shape[-2:]
    feat = terms[0][0].shape[1]
    half, block, count = feat // 2, hid // STEPS, len(terms)
    rows, last = count * per, core is not None

    def body(*refs):
        refs = refs[1:] if last else refs
        given, refs = [refs[k * count : (k + 1) * count] for k in range(4)], refs[4 * count :]
        both = refs[-4:]

        @pl.when(pl.program_id(0) == 0)
        def _():
            for parts, out in zip(given[:2], both[:2]):
                for k, ref in enumerate(parts):
                    out[k * per : (k + 1) * per] = ref[...]

        for parts, out in zip(given[2:], both[2:]):
            for k, ref in enumerate(parts):
                out[k * per : (k + 1) * per] = ref[0] if len(ref.shape) == 3 else ref[...]
        tok, cot, act, grad = both
        wi = dot(tok[...], grad[...], 0, 0)
        wo = dot(act[...], cot[...], 0, 0)
        if sums is not None:
            wi, wo, refs = wi + refs[0][...], wo + refs[1][...], refs[2:]
        if last:
            refs[0][...] = wi[:half].astype(BF16)
            refs[1][...] = wo[:, :half].astype(BF16)
            refs[2][...] = wi[half:].astype(BF16)
            refs[3][...] = wo[:, half:].astype(BF16)
        else:
            refs[0][...] = wi
            refs[1][...] = wo

    def hidden_part(a, which):
        return (a, (1, per, block), (which, 0, "i")) if len(a.shape) == 3 else (a, (per, block), (0, "i"))

    ins = [(term[n], (per, feat), (term[2], 0)) for n in (0, 1) for term in terms]
    ins += [hidden_part(term[3 + which], which) for which in (0, 1) for term in terms]
    if sums is not None:
        ins += [(sums[0], (feat, block), (0, "i")), (sums[1], (block, feat), ("i", 0))]
    if last:
        at = lambda i, c: c * STEPS + i
        outs = [((half, 2 * hid), BF16, (half, block), (0, at)), ((2 * hid, half), BF16, (block, half), (at, 0))]
        outs += [((half, hid), BF16, (half, block), (0, "i")), ((hid, half), BF16, (block, half), ("i", 0))]
    else:
        outs = [((feat, hid), F32, (feat, block), (0, "i")), ((hid, feat), F32, (block, feat), ("i", 0))]
    scratch = [pltpu.VMEM((rows, feat), BF16)] * 2 + [pltpu.VMEM((rows, block), BF16)] * 2
    return kernel(name, body, STEPS, ins, outs, scratch, core)


def place(wi, wo, wi_got, wo_got, core):
    half, hid = wi_got.shape
    block = hid // STEPS

    def body(core, wi, wo, wi_got, wo_got, wi_out, wo_out):
        wi_out[...] = wi_got[...]
        wo_out[...] = wo_got[...]

    at = lambda i, c: (1 - c) * STEPS + i
    return kernel(
        "place",
        body,
        STEPS,
        [(wi, None, None), (wo, None, None), (wi_got, (half, block), (0, "i")), (wo_got, (block, half), ("i", 0))],
        [(wi.shape, BF16, (half, block), (0, at)), (wo.shape, BF16, (block, half), (at, 0))],
        scalar=core,
        aliases={1: 0, 2: 1},
    )


def local(tokens, cotangent, w_in, w_out):
    z, core = lax.axis_index("z"), lax.axis_index("core")
    rows, feat = tokens.shape
    hid = w_in.shape[1] // 2
    piece = rows // 4

    def relative(a, sign):
        return jnp.roll(a.reshape(4, piece, a.shape[-1]), sign * z, 0)

    def to_core(parts):
        return [shift(a, "core", 1) for a in parts]

    def up_down(up, down):
        return shift(up, "z", 1), shift(down, "z", -1)

    def send_mine(mine):
        return shift(mine, "z", -1), shift(mine, "z", 1)

    def send_on(above, below):
        act, grad = pass_on(above, below)
        return shift(act, "z", -1), shift(grad, "z", 1), act

    at_core = jnp.reshape(core, (1,)).astype(jnp.int32)
    own = relative(jnp.concatenate([tokens, cotangent], 1), -1)
    near = [own] + [shift(own, "y", -d) for d in (1, 2, 3)]
    across = shift(own, "xh", 1)
    packed = pack(*gate((w_in, w_out), own), at_core)
    got = shift(packed, "core", 1)
    near = join("join_a", near)[0]
    near_other = shift(near, "core", 1)
    across = gate(across, near)
    far = [shift(across, "y", -d) for d in (1, 2, 3)]
    across_other = shift(across, "core", 1)
    wi, wo = weights(w_in, w_out, gate(got, across_other), at_core)

    up_a, down_a = first_block(near, near_other, wi, wo)
    r_a = up_down(up_a, down_a)
    near, near_other = gate((near, near_other), up_a)
    pg_a, _, _, tok_a, cot_a = products(near, near_other, wi, wo)

    far = gate(far, pg_a)
    far = join("join_b", [across, *far], [across_other, *to_core(far)])
    pg_b, up_b, down_b, tok_b, cot_b = products(*far, wi, wo)
    r_b = up_down(up_b, down_b)

    m_a = ring_add(pg_a, *gate(r_a, up_b))
    r_a = up_down(*m_a)
    m_b = ring_add(pg_b, *gate(r_b, m_a))
    r_b = up_down(*m_b)

    t_a, m_a = own_sum(pg_a, *gate(r_a, m_b))
    x_a = shift(m_a, "xl", 1)
    t_b, m_b = own_sum(pg_b, *gate(r_b, m_a))
    x_b = shift(m_b, "xl", 1)

    mine_a = hidden(t_a, gate(x_a, m_b))
    s_a = send_mine(mine_a)
    mine_b = hidden(t_b, gate(x_b, mine_a))
    s_b = send_mine(mine_b)

    s_a = gate(s_a, mine_b)
    *f_a, sent_a = send_on(*s_a)
    three_a = input_three(mine_a, *gate(s_a, sent_a), wi)
    terms = [(tok_a, cot_a, k, a, a) for k, a in zip((0, 1, 3), gate((mine_a, *s_a), three_a))]
    sums = weight_grads("grads_a", terms)

    s_b = gate(s_b, sums)
    *f_b, sent_b = send_on(*s_b)
    three_b = input_three(mine_b, *gate(s_b, sent_b), wi)
    terms = [(tok_b, cot_b, k, a, a) for k, a in zip((0, 1, 3), gate((mine_b, *s_b), three_b))]
    sums = weight_grads("grads_b", terms, sums)

    f_a = gate(f_a, sums)
    in_a, others = input_last(three_a, f_a[1], wi, 3)
    kept, *back = return_pieces("return_a", in_a, to_core(others), (F32, BF16, BF16, BF16))
    back = [shift(a, "y", d) for d, a in zip((1, 2, 3), back)]

    f_b = gate(f_b, kept)
    in_b, others = input_last(three_b, f_b[1], wi, 1)
    others_got = to_core(others)
    f_a, f_b = gate((f_a, f_b), others)
    terms = [(tok_a, cot_a, 2, *f_a), (tok_b, cot_b, 2, *f_b)]
    w_in_grad, w_out_grad, *others = weight_grads("grads_last", terms, sums, at_core)

    others_got, back = gate((others_got, back), others)
    far = return_pieces("return_b", in_b, others_got, (BF16,) * 4)
    got = to_core(gate(others, far))
    far = [
        lax.ppermute(a, ROWS, [(i, ((i // 2 + d) % 4) * 2 + (i + 1) % 2) for i in range(8)])
        for d, a in enumerate(far)
    ]
    w_in_grad, w_out_grad = place(w_in_grad, w_out_grad, *got, at_core)

    total = kept
    for part in back + gate(far, w_in_grad):
        total = total + part.astype(F32)
    input_grad = relative(total, 1).reshape(rows, feat).astype(BF16)
    return (input_grad, w_in_grad, w_out_grad)


def solution(mesh):
    fine = Mesh(mesh.devices.reshape(SIZES), AXES)
    return jax.shard_map(
        local,
        mesh=fine,
        in_specs=(P(ROWS, COLS), P(ROWS, COLS), P(COLS, ROWS), P(ROWS, COLS)),
        out_specs=(P(ROWS, COLS), P(COLS, ROWS), P(ROWS, COLS)),
        check_vma=False,
    )
```

```python
import jax
import jax.numpy as jnp
from jax import lax
from jax.experimental import pallas as pl
from jax.experimental.pallas import tpu as pltpu
from jax.sharding import Mesh
from jax.sharding import PartitionSpec as P

AXES = ("y", "xh", "xl", "z", "core")
SIZES = (4, 2, 2, 4, 2)
ROWS = ("y", "xh")
COLS = ("xl", "z", "core")
F32 = jnp.float32
BF16 = jnp.bfloat16
STEPS = 3


def gelu_parts(pre):
    cdf = 0.5 * (1.0 + lax.erf(pre * 0.7071067811865476))
    pdf = jnp.exp(-0.5 * pre * pre) * 0.3989422804014327
    return (cdf, pdf)


def shift(x, axis, by):
    n = SIZES[AXES.index(axis)]
    return lax.ppermute(x, axis, [(i, (i + by) % n) for i in range(n)])


def dot(a, b, da, db):
    return lax.dot_general(a, b, (((da,), (db,)), ((), ())), preferred_element_type=F32)


def gate(value, *after):
    return lax.optimization_barrier((value, after))[0]


COST = dict(pack=0.1, first_block=0.1, weights=7, join_a=100, join_b=0.1, products=0.1, ring_add=0.1, own_sum=0.1, hidden=0.1, pass_on=0.1, input_three=0.1, input_last=0.1, grads_a=0.1, grads_b=0.1, grads_last=0.1, return_a=0.1, return_b=20, place=0.1)


def kernel(name, body, grid, ins, outs, scratch=(), scalar=None, aliases=None, vmem=24):
    def spec(block, index):
        if block is None:
            return pl.BlockSpec(memory_space=pltpu.HBM if index == "hbm" else pl.ANY)

        def at(i, *refs):
            return tuple(i if k == "i" else k(i, *(r[0] for r in refs)) if callable(k) else k for k in index)

        return pl.BlockSpec(block, at)

    return pl.pallas_call(
        body,
        name=name,
        grid_spec=pltpu.PrefetchScalarGridSpec(
            num_scalar_prefetch=0 if scalar is None else 1,
            grid=(grid,),
            in_specs=[spec(block, index) for _, block, index in ins],
            out_specs=[spec(block, index) for _, _, block, index in outs],
            scratch_shapes=list(scratch),
        ),
        out_shape=[jax.ShapeDtypeStruct(shape, dtype) for shape, dtype, _, _ in outs],
        input_output_aliases=aliases or {},
        cost_estimate=pl.CostEstimate(flops=int(COST[name] * 1.15e9), bytes_accessed=int(COST[name] * 3.69e6), transcendentals=0),
        compiler_params=pltpu.CompilerParams(vmem_limit_bytes=vmem * 2**20),
    )(*([] if scalar is None else [scalar]), *[a for a, _, _ in ins])


def pack(w_in, w_out, core):
    feat = w_in.shape[0]
    half = w_out.shape[0] // feat // 2

    def body(core, wi, wo, out, sems):
        copies = []
        for k in range(half):
            at = pl.ds(pl.multiple_of(((1 - core[0]) * half + k) * feat, feat), feat)
            copies.append(pltpu.make_async_copy(wi.at[:, at], out.at[0, k], sems.at[0, k]))
            copies.append(pltpu.make_async_copy(wo.at[at, :], out.at[1, k], sems.at[1, k]))
        for copy in copies:
            copy.start()
        for copy in copies:
            copy.wait()

    shape = (2, half, feat, feat)
    return kernel(
        "pack",
        body,
        1,
        [(w_in, None, "hbm"), (w_out, None, "hbm")],
        [(shape, BF16, None, None)],
        [pltpu.SemaphoreType.DMA((2, half))],
        scalar=core,
        vmem=60,
    )[0]


def weights(w_in, w_out, got, core):
    feat = w_in.shape[0]
    half = w_out.shape[0] // feat // 2
    hid = half * feat

    def body(core, wi, wo, got, wi_out, wo_out, sems):
        mine = pl.ds(pl.multiple_of(core[0] * hid, hid), hid)
        copies = [
            pltpu.make_async_copy(wi.at[:, mine], wi_out.at[pl.ds(0, feat), :], sems.at[0, half]),
            pltpu.make_async_copy(wo.at[mine, :], wo_out.at[:, pl.ds(0, feat)], sems.at[1, half]),
        ]
        for k in range(half):
            at, other = pl.ds(k * feat, feat), pl.ds(feat, feat)
            copies.append(pltpu.make_async_copy(got.at[0, k], wi_out.at[other, at], sems.at[0, k]))
            copies.append(pltpu.make_async_copy(got.at[1, k], wo_out.at[at, other], sems.at[1, k]))
        for copy in copies:
            copy.start()
        for copy in copies:
            copy.wait()

    return kernel(
        "weights",
        body,
        1,
        [(w_in, None, "hbm"), (w_out, None, "hbm"), (got, None, None)],
        [((2 * feat, hid), BF16, None, None), ((hid, 2 * feat), BF16, None, None)],
        [pltpu.SemaphoreType.DMA((2, half + 1))],
        scalar=core,
    )


def pass_on(above, below):
    _, per, hid = above.shape

    def body(above, below, act, grad):
        act[...] = above[0]
        grad[...] = below[0]

    return kernel(
        "pass_on",
        body,
        1,
        [(above, (1, per, hid), (0, 0, 0)), (below, (1, per, hid), (1, 0, 0))],
        [((per, hid), BF16, (per, hid), (0, 0))] * 2,
    )


def join(name, *sides):
    zs, piece, width = sides[0][0].shape
    count = len(sides[0])
    per = count * piece

    def body(*refs):
        for n, out in enumerate(refs[len(sides) * count :]):
            for k in range(zs):
                for j in range(count):
                    out[pl.ds(k * per + j * piece, piece), :] = refs[n * count + j][k]

    return kernel(
        name,
        body,
        1,
        [(a, (zs, piece, width), (0, 0, 0)) for side in sides for a in side],
        [((zs * per, width), BF16, (zs * per, width), (0, 0))] * len(sides),
    )


def first_block(own, other, wi, wo):
    rows, width = own.shape
    feat, hid = wi.shape
    half, per, block = width // 2, rows // 4, hid // STEPS

    def body(own, other, wi, wo, up, down):
        tok = jnp.concatenate([own[:, :half], other[:, :half]], 1)
        cot = jnp.concatenate([own[:, half:], other[:, half:]], 1)
        up[...] = jnp.dot(tok, wi[...], preferred_element_type=F32).astype(BF16)
        down[...] = dot(cot, wo[...], 1, 1).astype(BF16)

    part = (per, width)
    return kernel(
        "first_block",
        body,
        STEPS,
        [(own, part, (2, 0)), (other, part, (2, 0)), (wi, (feat, block), (0, "i")), (wo, (block, feat), ("i", 0))],
        [((per, hid), BF16, (per, block), (0, "i"))] * 2,
    )


def products(own, other, wi, wo):
    rows, width = own.shape
    feat, hid = wi.shape
    half, block = width // 2, hid // STEPS

    def body(own, other, wi, wo, pg, tok, cot):
        @pl.when(pl.program_id(0) == 0)
        def _():
            for side, ref in enumerate((own, other)):
                tok[:, side * half : (side + 1) * half] = ref[:, :half]
                cot[:, side * half : (side + 1) * half] = ref[:, half:]

        p = jnp.dot(tok[...], wi[...], preferred_element_type=F32)
        g = dot(cot[...], wo[...], 1, 1)
        pg[0] = p
        pg[1] = g

    whole = (rows, width)
    return kernel(
        "products",
        body,
        STEPS,
        [(own, whole, (0, 0)), (other, whole, (0, 0)), (wi, (feat, block), (0, "i")), (wo, (block, feat), ("i", 0))],
        [
            ((2, rows, hid), F32, (2, rows, block), (0, 0, "i")),
            ((rows, feat), BF16, (rows, feat), (0, 0)),
            ((rows, feat), BF16, (rows, feat), (0, 0)),
        ],
    )


def ring_add(pg, up, down):
    per, hid = up.shape
    block = hid // STEPS

    def body(one, three, up, down, up_out, down_out):
        up_out[0] = (one[0] + up[...].astype(F32)).astype(BF16)
        up_out[1] = one[1].astype(BF16)
        down_out[0] = three[0].astype(BF16)
        down_out[1] = (three[1] + down[...].astype(F32)).astype(BF16)

    part = (2, per, block)
    return kernel(
        "ring_add",
        body,
        STEPS,
        [(pg, part, (0, 1, "i")), (pg, part, (0, 3, "i")), (up, (per, block), (0, "i")), (down, (per, block), (0, "i"))],
        [((2, per, hid), BF16, part, (0, 0, "i"))] * 2,
    )


def own_sum(pg, up, down):
    _, per, hid = up.shape
    part = (2, per, hid // STEPS)

    def body(zero, up, down, out, sent):
        total = zero[...] + up[...].astype(F32) + down[...].astype(F32)
        out[...] = total
        sent[...] = total.astype(BF16)

    return kernel(
        "own_sum",
        body,
        STEPS,
        [(pg, part, (0, 0, "i")), (up, part, (0, 0, "i")), (down, part, (0, 0, "i"))],
        [((2, per, hid), F32, part, (0, 0, "i")), ((2, per, hid), BF16, part, (0, 0, "i"))],
    )


def hidden(total, other):
    _, per, hid = total.shape
    part = (2, per, hid // STEPS)

    def body(total, other, out):
        pre = total[0] + other[0].astype(F32)
        act_grad = total[1] + other[1].astype(F32)
        cdf, pdf = gelu_parts(pre)
        out[0] = (pre * cdf).astype(BF16)
        out[1] = (act_grad * (cdf + pre * pdf)).astype(BF16)

    return kernel(
        "hidden",
        body,
        STEPS,
        [(total, part, (0, 0, "i")), (other, part, (0, 0, "i"))],
        [((2, per, hid), BF16, part, (0, 0, "i"))],
    )[0]


def input_three(mine, above, below, wi):
    _, per, hid = mine.shape
    half = wi.shape[0] // 2

    def body(mine, above, below, wi, own, other):
        for step, out in enumerate((own, other)):

            @pl.when(pl.program_id(0) == step)
            def _():
                for k, grad in enumerate((mine, above, below)):
                    out[k] = dot(grad[0], wi[...], 1, 1)

    second, whole = (1, per, hid), (3, per, half)
    return kernel(
        "input_three",
        body,
        2,
        [(a, second, (1, 0, 0)) for a in (mine, above, below)] + [(wi, (half, hid), ("i", 0))],
        [(whole, F32, whole, (0, 0, 0))] * 2,
    )


def input_last(three, grad2, wi, pieces):
    per, hid = grad2.shape
    half = wi.shape[0] // 2
    width = half // pieces

    def body(own3, other3, grad, wi, own, *others):
        for k, at in ((0, 0), (1, 1), (2, 3)):
            rows = pl.ds(at * per, per)
            own[rows, :] = own3[k]
            for j, other in enumerate(others):
                other[rows, :] = other3[k, :, j * width : (j + 1) * width]
        part = dot(grad[...], wi[...], 1, 1)
        rows = pl.ds(2 * per, per)
        own[rows, :] = part[:, :half]
        for j, other in enumerate(others):
            other[rows, :] = part[:, half + j * width : half + (j + 1) * width]

    whole, part = (4 * per, half), (4 * per, width)
    own, *others = kernel(
        "input_last",
        body,
        1,
        [(a, a.shape, (0, 0, 0)) for a in three] + [(a, a.shape, (0, 0)) for a in (grad2, wi)],
        [(whole, F32, whole, (0, 0))] + [(part, F32, part, (0, 0))] * pieces,
    )
    return own, others


def return_pieces(name, mine, got, kinds):
    rows, feat = mine.shape
    width, pieces = got[0].shape[1], len(kinds)
    piece = rows // 4 // pieces

    def body(mine, *refs):
        for j, out in enumerate(refs[len(got) :]):
            for k in range(4):
                at = pl.ds((k * pieces + j) * piece, piece)
                for c, ref in enumerate(refs[: len(got)]):
                    columns = slice(c * width, (c + 1) * width)
                    out[k, :, columns] = (mine[at, columns] + ref[at, :]).astype(out.dtype)

    part = (4, piece, feat)
    return kernel(
        name,
        body,
        1,
        [(mine, (rows, feat), (0, 0))] + [(a, (rows, width), (0, 0)) for a in got],
        [(part, kind, part, (0, 0, 0)) for kind in kinds],
    )


def weight_grads(name, terms, sums=None, core=None):
    per, hid = terms[0][3].shape[-2:]
    feat = terms[0][0].shape[1]
    half, block, count = feat // 2, hid // STEPS, len(terms)
    rows, last = count * per, core is not None

    def body(*refs):
        refs = refs[1:] if last else refs
        given, refs = [refs[k * count : (k + 1) * count] for k in range(4)], refs[4 * count :]
        both = refs[-4:]

        @pl.when(pl.program_id(0) == 0)
        def _():
            for parts, out in zip(given[:2], both[:2]):
                for k, ref in enumerate(parts):
                    out[k * per : (k + 1) * per] = ref[...]

        for parts, out in zip(given[2:], both[2:]):
            for k, ref in enumerate(parts):
                out[k * per : (k + 1) * per] = ref[0] if len(ref.shape) == 3 else ref[...]
        tok, cot, act, grad = both
        wi = dot(tok[...], grad[...], 0, 0)
        wo = dot(act[...], cot[...], 0, 0)
        if sums is not None:
            wi, wo, refs = wi + refs[0][...], wo + refs[1][...], refs[2:]
        if last:
            refs[0][...] = wi[:half].astype(BF16)
            refs[1][...] = wo[:, :half].astype(BF16)
            refs[2][...] = wi[half:].astype(BF16)
            refs[3][...] = wo[:, half:].astype(BF16)
        else:
            refs[0][...] = wi
            refs[1][...] = wo

    def hidden_part(a, which):
        return (a, (1, per, block), (which, 0, "i")) if len(a.shape) == 3 else (a, (per, block), (0, "i"))

    ins = [(term[n], (per, feat), (term[2], 0)) for n in (0, 1) for term in terms]
    ins += [hidden_part(term[3 + which], which) for which in (0, 1) for term in terms]
    if sums is not None:
        ins += [(sums[0], (feat, block), (0, "i")), (sums[1], (block, feat), ("i", 0))]
    if last:
        at = lambda i, c: c * STEPS + i
        outs = [((half, 2 * hid), BF16, (half, block), (0, at)), ((2 * hid, half), BF16, (block, half), (at, 0))]
        outs += [((half, hid), BF16, (half, block), (0, "i")), ((hid, half), BF16, (block, half), ("i", 0))]
    else:
        outs = [((feat, hid), F32, (feat, block), (0, "i")), ((hid, feat), F32, (block, feat), ("i", 0))]
    scratch = [pltpu.VMEM((rows, feat), BF16)] * 2 + [pltpu.VMEM((rows, block), BF16)] * 2
    return kernel(name, body, STEPS, ins, outs, scratch, core)


def place(wi, wo, wi_got, wo_got, core):
    half, hid = wi_got.shape
    block = hid // STEPS

    def body(core, wi, wo, wi_got, wo_got, wi_out, wo_out):
        wi_out[...] = wi_got[...]
        wo_out[...] = wo_got[...]

    at = lambda i, c: (1 - c) * STEPS + i
    return kernel(
        "place",
        body,
        STEPS,
        [(wi, None, None), (wo, None, None), (wi_got, (half, block), (0, "i")), (wo_got, (block, half), ("i", 0))],
        [(wi.shape, BF16, (half, block), (0, at)), (wo.shape, BF16, (block, half), (at, 0))],
        scalar=core,
        aliases={1: 0, 2: 1},
    )


def local(tokens, cotangent, w_in, w_out):
    z, core = lax.axis_index("z"), lax.axis_index("core")
    rows, feat = tokens.shape
    hid = w_in.shape[1] // 2
    piece = rows // 4

    def relative(a, sign):
        return jnp.roll(a.reshape(4, piece, a.shape[-1]), sign * z, 0)

    def to_core(parts):
        return [shift(a, "core", 1) for a in parts]

    def up_down(up, down):
        return shift(up, "z", 1), shift(down, "z", -1)

    def send_mine(mine):
        return shift(mine, "z", -1), shift(mine, "z", 1)

    def send_on(above, below):
        act, grad = pass_on(above, below)
        return shift(act, "z", -1), shift(grad, "z", 1), act

    at_core = jnp.reshape(core, (1,)).astype(jnp.int32)
    own = relative(jnp.concatenate([tokens, cotangent], 1), -1)
    near = [own] + [shift(own, "y", -d) for d in (1, 2, 3)]
    across = shift(own, "xh", 1)
    packed = pack(*gate((w_in, w_out), own), at_core)
    got = shift(packed, "core", 1)
    near = join("join_a", near)[0]
    near_other = shift(near, "core", 1)
    across = gate(across, near)
    far = [shift(across, "y", -d) for d in (1, 2, 3)]
    across_other = shift(across, "core", 1)
    wi, wo = weights(w_in, w_out, gate(got, across_other), at_core)

    up_a, down_a = first_block(near, near_other, wi, wo)
    r_a = up_down(up_a, down_a)
    far = gate(far, up_a)
    far = join("join_b", [across, *far], [across_other, *to_core(far)])
    up_b, down_b = first_block(*far, wi, wo)
    r_b = up_down(up_b, down_b)

    near, near_other = gate((near, near_other), up_b)
    pg_a, tok_a, cot_a = products(near, near_other, wi, wo)
    m_a = ring_add(pg_a, *gate(r_a, pg_a))
    r_a = up_down(*m_a)
    pg_b, tok_b, cot_b = products(*gate(far, m_a), wi, wo)
    m_b = ring_add(pg_b, *gate(r_b, pg_b))
    r_b = up_down(*m_b)

    t_a, m_a = own_sum(pg_a, *gate(r_a, m_b))
    x_a = shift(m_a, "xl", 1)
    t_b, m_b = own_sum(pg_b, *gate(r_b, m_a))
    x_b = shift(m_b, "xl", 1)

    mine_a = hidden(t_a, gate(x_a, m_b))
    s_a = send_mine(mine_a)
    mine_b = hidden(t_b, gate(x_b, mine_a))
    s_b = send_mine(mine_b)

    s_a = gate(s_a, mine_b)
    *f_a, sent_a = send_on(*s_a)
    three_a = input_three(mine_a, *gate(s_a, sent_a), wi)
    terms = [(tok_a, cot_a, k, a, a) for k, a in zip((0, 1, 3), gate((mine_a, *s_a), three_a))]
    sums = weight_grads("grads_a", terms)

    s_b = gate(s_b, sums)
    *f_b, sent_b = send_on(*s_b)
    three_b = input_three(mine_b, *gate(s_b, sent_b), wi)
    terms = [(tok_b, cot_b, k, a, a) for k, a in zip((0, 1, 3), gate((mine_b, *s_b), three_b))]
    sums = weight_grads("grads_b", terms, sums)

    f_a = gate(f_a, sums)
    in_a, others = input_last(three_a, f_a[1], wi, 3)
    kept, *back = return_pieces("return_a", in_a, to_core(others), (F32, BF16, BF16, BF16))
    back = [shift(a, "y", d) for d, a in zip((1, 2, 3), back)]

    f_b = gate(f_b, kept)
    in_b, others = input_last(three_b, f_b[1], wi, 1)
    others_got = to_core(others)
    f_a, f_b = gate((f_a, f_b), others)
    terms = [(tok_a, cot_a, 2, *f_a), (tok_b, cot_b, 2, *f_b)]
    w_in_grad, w_out_grad, *others = weight_grads("grads_last", terms, sums, at_core)

    others_got, back = gate((others_got, back), others)
    far = return_pieces("return_b", in_b, others_got, (BF16,) * 4)
    got = to_core(gate(others, far))
    far = [
        lax.ppermute(a, ROWS, [(i, ((i // 2 + d) % 4) * 2 + (i + 1) % 2) for i in range(8)])
        for d, a in enumerate(far)
    ]
    w_in_grad, w_out_grad = place(w_in_grad, w_out_grad, *got, at_core)

    total = kept
    for part in back + gate(far, w_in_grad):
        total = total + part.astype(F32)
    input_grad = relative(total, 1).reshape(rows, feat).astype(BF16)
    return (input_grad, w_in_grad, w_out_grad)


def solution(mesh):
    fine = Mesh(mesh.devices.reshape(SIZES), AXES)
    return jax.shard_map(
        local,
        mesh=fine,
        in_specs=(P(ROWS, COLS), P(ROWS, COLS), P(COLS, ROWS), P(ROWS, COLS)),
        out_specs=(P(ROWS, COLS), P(COLS, ROWS), P(ROWS, COLS)),
        check_vma=False,
    )
```

```python
import jax
import jax.numpy as jnp
from jax import lax
from jax.experimental import pallas as pl
from jax.experimental.pallas import tpu as pltpu
from jax.sharding import Mesh
from jax.sharding import PartitionSpec as P

AXES = ("y", "xh", "xl", "z", "core")
SIZES = (4, 2, 2, 4, 2)
ROWS = ("y", "xh")
COLS = ("xl", "z", "core")
F32 = jnp.float32
BF16 = jnp.bfloat16
STEPS = 3


def gelu_parts(pre):
    cdf = 0.5 * (1.0 + lax.erf(pre * 0.7071067811865476))
    pdf = jnp.exp(-0.5 * pre * pre) * 0.3989422804014327
    return (cdf, pdf)


def shift(x, axis, by):
    n = SIZES[AXES.index(axis)]
    return lax.ppermute(x, axis, [(i, (i + by) % n) for i in range(n)])


def dot(a, b, da, db):
    return lax.dot_general(a, b, (((da,), (db,)), ((), ())), preferred_element_type=F32)


def gate(value, *after):
    return lax.optimization_barrier((value, after))[0]


COST = dict(pack=0.1, first_block=0.1, weights=7, join_a=100, join_b=0.1, products=0.1, ring_add=0.1, own_sum=0.1, hidden=0.1, pass_on=0.1, input_three=0.1, input_last=0.1, grads_a=0.1, grads_b=0.1, grads_last=0.1, return_a=0.1, return_b=20, place=0.1)


def kernel(name, body, grid, ins, outs, scratch=(), scalar=None, aliases=None, vmem=24):
    def spec(block, index):
        if block is None:
            return pl.BlockSpec(memory_space=pltpu.HBM if index == "hbm" else pl.ANY)

        def at(i, *refs):
            return tuple(i if k == "i" else k(i, *(r[0] for r in refs)) if callable(k) else k for k in index)

        return pl.BlockSpec(block, at)

    return pl.pallas_call(
        body,
        name=name,
        grid_spec=pltpu.PrefetchScalarGridSpec(
            num_scalar_prefetch=0 if scalar is None else 1,
            grid=(grid,),
            in_specs=[spec(block, index) for _, block, index in ins],
            out_specs=[spec(block, index) for _, _, block, index in outs],
            scratch_shapes=list(scratch),
        ),
        out_shape=[jax.ShapeDtypeStruct(shape, dtype) for shape, dtype, _, _ in outs],
        input_output_aliases=aliases or {},
        cost_estimate=pl.CostEstimate(flops=int(COST[name] * 1.15e9), bytes_accessed=int(COST[name] * 3.69e6), transcendentals=0),
        compiler_params=pltpu.CompilerParams(vmem_limit_bytes=vmem * 2**20),
    )(*([] if scalar is None else [scalar]), *[a for a, _, _ in ins])


def pack(w_in, w_out, core):
    feat = w_in.shape[0]
    half = w_out.shape[0] // feat // 2

    def body(_, wi, wo, out):
        out[0, 0] = wi[...]
        out[1, 0] = wo[...]

    block = (feat, feat)
    place = lambda i, c: (1 - c) * half + i
    return kernel(
        "pack",
        body,
        half,
        [(w_in, block, (0, place)), (w_out, block, (place, 0))],
        [((2, half, feat, feat), BF16, (2, 1, feat, feat), (0, "i", 0, 0))],
        scalar=core,
        vmem=60,
    )[0]


def weights(w_in, w_out, got, core):
    feat = w_in.shape[0]
    half = w_out.shape[0] // feat // 2
    hid = half * feat

    def body(core, wi, wo, got, wi_out, wo_out, sems):
        mine = pl.ds(pl.multiple_of(core[0] * hid, hid), hid)
        copies = [
            pltpu.make_async_copy(wi.at[:, mine], wi_out.at[pl.ds(0, feat), :], sems.at[0, half]),
            pltpu.make_async_copy(wo.at[mine, :], wo_out.at[:, pl.ds(0, feat)], sems.at[1, half]),
        ]
        for k in range(half):
            at, other = pl.ds(k * feat, feat), pl.ds(feat, feat)
            copies.append(pltpu.make_async_copy(got.at[0, k], wi_out.at[other, at], sems.at[0, k]))
            copies.append(pltpu.make_async_copy(got.at[1, k], wo_out.at[at, other], sems.at[1, k]))
        for copy in copies:
            copy.start()
        for copy in copies:
            copy.wait()

    return kernel(
        "weights",
        body,
        1,
        [(w_in, None, "hbm"), (w_out, None, "hbm"), (got, None, None)],
        [((2 * feat, hid), BF16, None, None), ((hid, 2 * feat), BF16, None, None)],
        [pltpu.SemaphoreType.DMA((2, half + 1))],
        scalar=core,
    )


def pass_on(above, below):
    _, per, hid = above.shape

    def body(above, below, act, grad):
        act[...] = above[0]
        grad[...] = below[0]

    return kernel(
        "pass_on",
        body,
        1,
        [(above, (1, per, hid), (0, 0, 0)), (below, (1, per, hid), (1, 0, 0))],
        [((per, hid), BF16, (per, hid), (0, 0))] * 2,
    )


def join(name, *sides):
    zs, piece, width = sides[0][0].shape
    count = len(sides[0])
    per = count * piece

    def body(*refs):
        for n, out in enumerate(refs[len(sides) * count :]):
            for k in range(zs):
                for j in range(count):
                    out[pl.ds(k * per + j * piece, piece), :] = refs[n * count + j][k]

    return kernel(
        name,
        body,
        1,
        [(a, (zs, piece, width), (0, 0, 0)) for side in sides for a in side],
        [((zs * per, width), BF16, (zs * per, width), (0, 0))] * len(sides),
    )


def first_block(own, other, wi, wo):
    rows, width = own.shape
    feat, hid = wi.shape
    half, per, block = width // 2, rows // 4, hid // STEPS

    def body(own, other, wi, wo, up, down):
        tok = jnp.concatenate([own[:, :half], other[:, :half]], 1)
        cot = jnp.concatenate([own[:, half:], other[:, half:]], 1)
        up[...] = jnp.dot(tok, wi[...], preferred_element_type=F32).astype(BF16)
        down[...] = dot(cot, wo[...], 1, 1).astype(BF16)

    part = (per, width)
    return kernel(
        "first_block",
        body,
        STEPS,
        [(own, part, (2, 0)), (other, part, (2, 0)), (wi, (feat, block), (0, "i")), (wo, (block, feat), ("i", 0))],
        [((per, hid), BF16, (per, block), (0, "i"))] * 2,
    )


def products(own, other, wi, wo):
    rows, width = own.shape
    feat, hid = wi.shape
    half, block = width // 2, hid // STEPS

    def body(own, other, wi, wo, pg, tok, cot):
        @pl.when(pl.program_id(0) == 0)
        def _():
            for side, ref in enumerate((own, other)):
                tok[:, side * half : (side + 1) * half] = ref[:, :half]
                cot[:, side * half : (side + 1) * half] = ref[:, half:]

        p = jnp.dot(tok[...], wi[...], preferred_element_type=F32)
        g = dot(cot[...], wo[...], 1, 1)
        pg[0] = p
        pg[1] = g

    whole = (rows, width)
    return kernel(
        "products",
        body,
        STEPS,
        [(own, whole, (0, 0)), (other, whole, (0, 0)), (wi, (feat, block), (0, "i")), (wo, (block, feat), ("i", 0))],
        [
            ((2, rows, hid), F32, (2, rows, block), (0, 0, "i")),
            ((rows, feat), BF16, (rows, feat), (0, 0)),
            ((rows, feat), BF16, (rows, feat), (0, 0)),
        ],
    )


def ring_add(pg, up, down):
    per, hid = up.shape
    block = hid // STEPS

    def body(one, three, up, down, up_out, down_out):
        up_out[0] = (one[0] + up[...].astype(F32)).astype(BF16)
        up_out[1] = one[1].astype(BF16)
        down_out[0] = three[0].astype(BF16)
        down_out[1] = (three[1] + down[...].astype(F32)).astype(BF16)

    part = (2, per, block)
    return kernel(
        "ring_add",
        body,
        STEPS,
        [(pg, part, (0, 1, "i")), (pg, part, (0, 3, "i")), (up, (per, block), (0, "i")), (down, (per, block), (0, "i"))],
        [((2, per, hid), BF16, part, (0, 0, "i"))] * 2,
    )


def own_sum(pg, up, down):
    _, per, hid = up.shape
    part = (2, per, hid // STEPS)

    def body(zero, up, down, out, sent):
        total = zero[...] + up[...].astype(F32) + down[...].astype(F32)
        out[...] = total
        sent[...] = total.astype(BF16)

    return kernel(
        "own_sum",
        body,
        STEPS,
        [(pg, part, (0, 0, "i")), (up, part, (0, 0, "i")), (down, part, (0, 0, "i"))],
        [((2, per, hid), F32, part, (0, 0, "i")), ((2, per, hid), BF16, part, (0, 0, "i"))],
    )


def hidden(total, other):
    _, per, hid = total.shape
    part = (2, per, hid // STEPS)

    def body(total, other, out):
        pre = total[0] + other[0].astype(F32)
        act_grad = total[1] + other[1].astype(F32)
        cdf, pdf = gelu_parts(pre)
        out[0] = (pre * cdf).astype(BF16)
        out[1] = (act_grad * (cdf + pre * pdf)).astype(BF16)

    return kernel(
        "hidden",
        body,
        STEPS,
        [(total, part, (0, 0, "i")), (other, part, (0, 0, "i"))],
        [((2, per, hid), BF16, part, (0, 0, "i"))],
    )[0]


def input_three(mine, above, below, wi):
    _, per, hid = mine.shape
    half = wi.shape[0] // 2

    def body(mine, above, below, wi, own, other):
        for step, out in enumerate((own, other)):

            @pl.when(pl.program_id(0) == step)
            def _():
                for k, grad in enumerate((mine, above, below)):
                    out[k] = dot(grad[0], wi[...], 1, 1)

    second, whole = (1, per, hid), (3, per, half)
    return kernel(
        "input_three",
        body,
        2,
        [(a, second, (1, 0, 0)) for a in (mine, above, below)] + [(wi, (half, hid), ("i", 0))],
        [(whole, F32, whole, (0, 0, 0))] * 2,
    )


def input_last(three, grad2, wi, pieces):
    per, hid = grad2.shape
    half = wi.shape[0] // 2
    width = half // pieces

    def body(own3, other3, grad, wi, own, *others):
        for k, at in ((0, 0), (1, 1), (2, 3)):
            rows = pl.ds(at * per, per)
            own[rows, :] = own3[k]
            for j, other in enumerate(others):
                other[rows, :] = other3[k, :, j * width : (j + 1) * width]
        part = dot(grad[...], wi[...], 1, 1)
        rows = pl.ds(2 * per, per)
        own[rows, :] = part[:, :half]
        for j, other in enumerate(others):
            other[rows, :] = part[:, half + j * width : half + (j + 1) * width]

    whole, part = (4 * per, half), (4 * per, width)
    own, *others = kernel(
        "input_last",
        body,
        1,
        [(a, a.shape, (0, 0, 0)) for a in three] + [(a, a.shape, (0, 0)) for a in (grad2, wi)],
        [(whole, F32, whole, (0, 0))] + [(part, F32, part, (0, 0))] * pieces,
    )
    return own, others


def return_pieces(name, mine, got, kinds):
    rows, feat = mine.shape
    width, pieces = got[0].shape[1], len(kinds)
    piece = rows // 4 // pieces

    def body(mine, *refs):
        for j, out in enumerate(refs[len(got) :]):
            for k in range(4):
                at = pl.ds((k * pieces + j) * piece, piece)
                for c, ref in enumerate(refs[: len(got)]):
                    columns = slice(c * width, (c + 1) * width)
                    out[k, :, columns] = (mine[at, columns] + ref[at, :]).astype(out.dtype)

    part = (4, piece, feat)
    return kernel(
        name,
        body,
        1,
        [(mine, (rows, feat), (0, 0))] + [(a, (rows, width), (0, 0)) for a in got],
        [(part, kind, part, (0, 0, 0)) for kind in kinds],
    )


def weight_grads(name, terms, sums=None, core=None):
    per, hid = terms[0][3].shape[-2:]
    feat = terms[0][0].shape[1]
    half, block, count = feat // 2, hid // STEPS, len(terms)
    rows, last = count * per, core is not None

    def body(*refs):
        refs = refs[1:] if last else refs
        given, refs = [refs[k * count : (k + 1) * count] for k in range(4)], refs[4 * count :]
        both = refs[-4:]

        @pl.when(pl.program_id(0) == 0)
        def _():
            for parts, out in zip(given[:2], both[:2]):
                for k, ref in enumerate(parts):
                    out[k * per : (k + 1) * per] = ref[...]

        for parts, out in zip(given[2:], both[2:]):
            for k, ref in enumerate(parts):
                out[k * per : (k + 1) * per] = ref[0] if len(ref.shape) == 3 else ref[...]
        tok, cot, act, grad = both
        wi = dot(tok[...], grad[...], 0, 0)
        wo = dot(act[...], cot[...], 0, 0)
        if sums is not None:
            wi, wo, refs = wi + refs[0][...], wo + refs[1][...], refs[2:]
        if last:
            refs[0][...] = wi[:half].astype(BF16)
            refs[1][...] = wo[:, :half].astype(BF16)
            refs[2][...] = wi[half:].astype(BF16)
            refs[3][...] = wo[:, half:].astype(BF16)
        else:
            refs[0][...] = wi
            refs[1][...] = wo

    def hidden_part(a, which):
        return (a, (1, per, block), (which, 0, "i")) if len(a.shape) == 3 else (a, (per, block), (0, "i"))

    ins = [(term[n], (per, feat), (term[2], 0)) for n in (0, 1) for term in terms]
    ins += [hidden_part(term[3 + which], which) for which in (0, 1) for term in terms]
    if sums is not None:
        ins += [(sums[0], (feat, block), (0, "i")), (sums[1], (block, feat), ("i", 0))]
    if last:
        at = lambda i, c: c * STEPS + i
        outs = [((half, 2 * hid), BF16, (half, block), (0, at)), ((2 * hid, half), BF16, (block, half), (at, 0))]
        outs += [((half, hid), BF16, (half, block), (0, "i")), ((hid, half), BF16, (block, half), ("i", 0))]
    else:
        outs = [((feat, hid), F32, (feat, block), (0, "i")), ((hid, feat), F32, (block, feat), ("i", 0))]
    scratch = [pltpu.VMEM((rows, feat), BF16)] * 2 + [pltpu.VMEM((rows, block), BF16)] * 2
    return kernel(name, body, STEPS, ins, outs, scratch, core)


def place(wi, wo, wi_got, wo_got, core):
    half, hid = wi_got.shape
    block = hid // STEPS

    def body(core, wi, wo, wi_got, wo_got, wi_out, wo_out):
        wi_out[...] = wi_got[...]
        wo_out[...] = wo_got[...]

    at = lambda i, c: (1 - c) * STEPS + i
    return kernel(
        "place",
        body,
        STEPS,
        [(wi, None, None), (wo, None, None), (wi_got, (half, block), (0, "i")), (wo_got, (block, half), ("i", 0))],
        [(wi.shape, BF16, (half, block), (0, at)), (wo.shape, BF16, (block, half), (at, 0))],
        scalar=core,
        aliases={1: 0, 2: 1},
    )


def local(tokens, cotangent, w_in, w_out):
    z, core = lax.axis_index("z"), lax.axis_index("core")
    rows, feat = tokens.shape
    hid = w_in.shape[1] // 2
    piece = rows // 4

    def relative(a, sign):
        return jnp.roll(a.reshape(4, piece, a.shape[-1]), sign * z, 0)

    def to_core(parts):
        return [shift(a, "core", 1) for a in parts]

    def up_down(up, down):
        return shift(up, "z", 1), shift(down, "z", -1)

    def send_mine(mine):
        return shift(mine, "z", -1), shift(mine, "z", 1)

    def send_on(above, below):
        act, grad = pass_on(above, below)
        return shift(act, "z", -1), shift(grad, "z", 1), act

    at_core = jnp.reshape(core, (1,)).astype(jnp.int32)
    own = relative(jnp.concatenate([tokens, cotangent], 1), -1)
    near = [own] + [shift(own, "y", -d) for d in (1, 2, 3)]
    across = shift(own, "xh", 1)
    packed = pack(*gate((w_in, w_out), own), at_core)
    got = shift(packed, "core", 1)
    near = join("join_a", near)[0]
    near_other = shift(near, "core", 1)
    across = gate(across, near)
    far = [shift(across, "y", -d) for d in (1, 2, 3)]
    across_other = shift(across, "core", 1)
    wi, wo = weights(w_in, w_out, gate(got, across_other), at_core)

    up_a, down_a = first_block(near, near_other, wi, wo)
    r_a = up_down(up_a, down_a)
    far = gate(far, up_a)
    far = join("join_b", [across, *far], [across_other, *to_core(far)])
    up_b, down_b = first_block(*far, wi, wo)
    r_b = up_down(up_b, down_b)

    near, near_other = gate((near, near_other), up_b)
    pg_a, tok_a, cot_a = products(near, near_other, wi, wo)
    m_a = ring_add(pg_a, *gate(r_a, pg_a))
    r_a = up_down(*m_a)
    pg_b, tok_b, cot_b = products(*gate(far, m_a), wi, wo)
    m_b = ring_add(pg_b, *gate(r_b, pg_b))
    r_b = up_down(*m_b)

    t_a, m_a = own_sum(pg_a, *gate(r_a, m_b))
    x_a = shift(m_a, "xl", 1)
    t_b, m_b = own_sum(pg_b, *gate(r_b, m_a))
    x_b = shift(m_b, "xl", 1)

    mine_a = hidden(t_a, gate(x_a, m_b))
    s_a = send_mine(mine_a)
    mine_b = hidden(t_b, gate(x_b, mine_a))
    s_b = send_mine(mine_b)

    s_a = gate(s_a, mine_b)
    *f_a, sent_a = send_on(*s_a)
    three_a = input_three(mine_a, *gate(s_a, sent_a), wi)
    terms = [(tok_a, cot_a, k, a, a) for k, a in zip((0, 1, 3), gate((mine_a, *s_a), three_a))]
    sums = weight_grads("grads_a", terms)

    s_b = gate(s_b, sums)
    *f_b, sent_b = send_on(*s_b)
    three_b = input_three(mine_b, *gate(s_b, sent_b), wi)
    terms = [(tok_b, cot_b, k, a, a) for k, a in zip((0, 1, 3), gate((mine_b, *s_b), three_b))]
    sums = weight_grads("grads_b", terms, sums)

    f_a = gate(f_a, sums)
    in_a, others = input_last(three_a, f_a[1], wi, 3)
    kept, *back = return_pieces("return_a", in_a, to_core(others), (F32, BF16, BF16, BF16))
    back = [shift(a, "y", d) for d, a in zip((1, 2, 3), back)]

    f_b = gate(f_b, kept)
    in_b, others = input_last(three_b, f_b[1], wi, 1)
    others_got = to_core(others)
    f_a, f_b = gate((f_a, f_b), others)
    terms = [(tok_a, cot_a, 2, *f_a), (tok_b, cot_b, 2, *f_b)]
    w_in_grad, w_out_grad, *others = weight_grads("grads_last", terms, sums, at_core)

    others_got, back = gate((others_got, back), others)
    far = return_pieces("return_b", in_b, others_got, (BF16,) * 4)
    got = to_core(gate(others, far))
    far = [
        lax.ppermute(a, ROWS, [(i, ((i // 2 + d) % 4) * 2 + (i + 1) % 2) for i in range(8)])
        for d, a in enumerate(far)
    ]
    w_in_grad, w_out_grad = place(w_in_grad, w_out_grad, *got, at_core)

    total = kept
    for part in back + gate(far, w_in_grad):
        total = total + part.astype(F32)
    input_grad = relative(total, 1).reshape(rows, feat).astype(BF16)
    return (input_grad, w_in_grad, w_out_grad)


def solution(mesh):
    fine = Mesh(mesh.devices.reshape(SIZES), AXES)
    return jax.shard_map(
        local,
        mesh=fine,
        in_specs=(P(ROWS, COLS), P(ROWS, COLS), P(COLS, ROWS), P(ROWS, COLS)),
        out_specs=(P(ROWS, COLS), P(COLS, ROWS), P(ROWS, COLS)),
        check_vma=False,
    )
```

```python
import jax
import jax.numpy as jnp
from jax import lax
from jax.experimental import pallas as pl
from jax.experimental.pallas import tpu as pltpu
from jax.sharding import Mesh
from jax.sharding import PartitionSpec as P

AXES = ("y", "xh", "xl", "z", "core")
SIZES = (4, 2, 2, 4, 2)
ROWS = ("y", "xh")
COLS = ("xl", "z", "core")
F32 = jnp.float32
BF16 = jnp.bfloat16
STEPS = 2


def gelu_parts(pre):
    cdf = 0.5 * (1.0 + lax.erf(pre * 0.7071067811865476))
    pdf = jnp.exp(-0.5 * pre * pre) * 0.3989422804014327
    return (cdf, pdf)


def shift(x, axis, by):
    n = SIZES[AXES.index(axis)]
    return lax.ppermute(x, axis, [(i, (i + by) % n) for i in range(n)])


def dot(a, b, da, db):
    return lax.dot_general(a, b, (((da,), (db,)), ((), ())), preferred_element_type=F32)


def gate(value, *after):
    return lax.optimization_barrier((value, after))[0]


COST = dict(pack=0.1, first_block=0.1, weights=7, join_a=100, join_b=0.1, products=0.1, ring_add=0.1, own_sum=0.1, hidden=0.1, pass_on=0.1, input_three=0.1, input_last=0.1, grads_a=0.1, grads_b=0.1, grads_last=0.1, return_a=0.1, return_b=20, place=0.1)


def kernel(name, body, grid, ins, outs, scratch=(), scalar=None, aliases=None, vmem=24):
    def spec(block, index):
        if block is None:
            return pl.BlockSpec(memory_space=pltpu.HBM if index == "hbm" else pl.ANY)

        def at(i, *refs):
            return tuple(i if k == "i" else k(i, *(r[0] for r in refs)) if callable(k) else k for k in index)

        return pl.BlockSpec(block, at)

    return pl.pallas_call(
        body,
        name=name,
        grid_spec=pltpu.PrefetchScalarGridSpec(
            num_scalar_prefetch=0 if scalar is None else 1,
            grid=(grid,),
            in_specs=[spec(block, index) for _, block, index in ins],
            out_specs=[spec(block, index) for _, _, block, index in outs],
            scratch_shapes=list(scratch),
        ),
        out_shape=[jax.ShapeDtypeStruct(shape, dtype) for shape, dtype, _, _ in outs],
        input_output_aliases=aliases or {},
        cost_estimate=pl.CostEstimate(flops=int(COST[name] * 1.15e9), bytes_accessed=int(COST[name] * 3.69e6), transcendentals=0),
        compiler_params=pltpu.CompilerParams(vmem_limit_bytes=vmem * 2**20),
    )(*([] if scalar is None else [scalar]), *[a for a, _, _ in ins])


def pack(w_in, w_out, core):
    feat = w_in.shape[0]
    half = w_out.shape[0] // feat // 2

    def body(_, wi, wo, out):
        out[0, 0] = wi[...]
        out[1, 0] = wo[...]

    block = (feat, feat)
    place = lambda i, c: (1 - c) * half + i
    return kernel(
        "pack",
        body,
        half,
        [(w_in, block, (0, place)), (w_out, block, (place, 0))],
        [((2, half, feat, feat), BF16, (2, 1, feat, feat), (0, "i", 0, 0))],
        scalar=core,
        vmem=60,
    )[0]


def weights(w_in, w_out, got, core):
    feat = w_in.shape[0]
    half = w_out.shape[0] // feat // 2
    hid = half * feat

    def body(core, wi, wo, got, wi_out, wo_out, sems):
        mine = pl.ds(pl.multiple_of(core[0] * hid, hid), hid)
        copies = [
            pltpu.make_async_copy(wi.at[:, mine], wi_out.at[pl.ds(0, feat), :], sems.at[0, half]),
            pltpu.make_async_copy(wo.at[mine, :], wo_out.at[:, pl.ds(0, feat)], sems.at[1, half]),
        ]
        for k in range(half):
            at, other = pl.ds(k * feat, feat), pl.ds(feat, feat)
            copies.append(pltpu.make_async_copy(got.at[0, k], wi_out.at[other, at], sems.at[0, k]))
            copies.append(pltpu.make_async_copy(got.at[1, k], wo_out.at[at, other], sems.at[1, k]))
        for copy in copies:
            copy.start()
        for copy in copies:
            copy.wait()

    return kernel(
        "weights",
        body,
        1,
        [(w_in, None, "hbm"), (w_out, None, "hbm"), (got, None, None)],
        [((2 * feat, hid), BF16, None, None), ((hid, 2 * feat), BF16, None, None)],
        [pltpu.SemaphoreType.DMA((2, half + 1))],
        scalar=core,
    )


def pass_on(above, below):
    _, per, hid = above.shape

    def body(above, below, act, grad):
        act[...] = above[0]
        grad[...] = below[0]

    return kernel(
        "pass_on",
        body,
        1,
        [(above, (1, per, hid), (0, 0, 0)), (below, (1, per, hid), (1, 0, 0))],
        [((per, hid), BF16, (per, hid), (0, 0))] * 2,
    )


def join(name, *sides):
    zs, piece, width = sides[0][0].shape
    count = len(sides[0])
    per = count * piece

    def body(*refs):
        for n, out in enumerate(refs[len(sides) * count :]):
            for k in range(zs):
                for j in range(count):
                    out[pl.ds(k * per + j * piece, piece), :] = refs[n * count + j][k]

    return kernel(
        name,
        body,
        1,
        [(a, (zs, piece, width), (0, 0, 0)) for side in sides for a in side],
        [((zs * per, width), BF16, (zs * per, width), (0, 0))] * len(sides),
    )


def first_block(own, other, wi, wo):
    rows, width = own.shape
    feat, hid = wi.shape
    half, per, block = width // 2, rows // 4, hid // STEPS

    def body(own, other, wi, wo, up, down):
        tok = jnp.concatenate([own[:, :half], other[:, :half]], 1)
        cot = jnp.concatenate([own[:, half:], other[:, half:]], 1)
        up[...] = jnp.dot(tok, wi[...], preferred_element_type=F32).astype(BF16)
        down[...] = dot(cot, wo[...], 1, 1).astype(BF16)

    part = (per, width)
    return kernel(
        "first_block",
        body,
        STEPS,
        [(own, part, (2, 0)), (other, part, (2, 0)), (wi, (feat, block), (0, "i")), (wo, (block, feat), ("i", 0))],
        [((per, hid), BF16, (per, block), (0, "i"))] * 2,
    )


def products(own, other, wi, wo):
    rows, width = own.shape
    feat, hid = wi.shape
    half, block = width // 2, hid // STEPS

    def body(own, other, wi, wo, pg, tok, cot):
        @pl.when(pl.program_id(0) == 0)
        def _():
            for side, ref in enumerate((own, other)):
                tok[:, side * half : (side + 1) * half] = ref[:, :half]
                cot[:, side * half : (side + 1) * half] = ref[:, half:]

        p = jnp.dot(tok[...], wi[...], preferred_element_type=F32)
        g = dot(cot[...], wo[...], 1, 1)
        pg[0] = p
        pg[1] = g

    whole = (rows, width)
    return kernel(
        "products",
        body,
        STEPS,
        [(own, whole, (0, 0)), (other, whole, (0, 0)), (wi, (feat, block), (0, "i")), (wo, (block, feat), ("i", 0))],
        [
            ((2, rows, hid), F32, (2, rows, block), (0, 0, "i")),
            ((rows, feat), BF16, (rows, feat), (0, 0)),
            ((rows, feat), BF16, (rows, feat), (0, 0)),
        ],
    )


def ring_add(pg, up, down):
    per, hid = up.shape
    block = hid // STEPS

    def body(one, three, up, down, up_out, down_out):
        up_out[0] = (one[0] + up[...].astype(F32)).astype(BF16)
        up_out[1] = one[1].astype(BF16)
        down_out[0] = three[0].astype(BF16)
        down_out[1] = (three[1] + down[...].astype(F32)).astype(BF16)

    part = (2, per, block)
    return kernel(
        "ring_add",
        body,
        STEPS,
        [(pg, part, (0, 1, "i")), (pg, part, (0, 3, "i")), (up, (per, block), (0, "i")), (down, (per, block), (0, "i"))],
        [((2, per, hid), BF16, part, (0, 0, "i"))] * 2,
    )


def own_sum(pg, up, down):
    _, per, hid = up.shape
    part = (2, per, hid // STEPS)

    def body(zero, up, down, out, sent):
        total = zero[...] + up[...].astype(F32) + down[...].astype(F32)
        out[...] = total
        sent[...] = total.astype(BF16)

    return kernel(
        "own_sum",
        body,
        STEPS,
        [(pg, part, (0, 0, "i")), (up, part, (0, 0, "i")), (down, part, (0, 0, "i"))],
        [((2, per, hid), F32, part, (0, 0, "i")), ((2, per, hid), BF16, part, (0, 0, "i"))],
    )


def hidden(total, other):
    _, per, hid = total.shape
    part = (2, per, hid // STEPS)

    def body(total, other, out):
        pre = total[0] + other[0].astype(F32)
        act_grad = total[1] + other[1].astype(F32)
        cdf, pdf = gelu_parts(pre)
        out[0] = (pre * cdf).astype(BF16)
        out[1] = (act_grad * (cdf + pre * pdf)).astype(BF16)

    return kernel(
        "hidden",
        body,
        STEPS,
        [(total, part, (0, 0, "i")), (other, part, (0, 0, "i"))],
        [((2, per, hid), BF16, part, (0, 0, "i"))],
    )[0]


def input_three(mine, above, below, wi):
    _, per, hid = mine.shape
    half = wi.shape[0] // 2

    def body(mine, above, below, wi, own, other):
        for step, out in enumerate((own, other)):

            @pl.when(pl.program_id(0) == step)
            def _():
                for k, grad in enumerate((mine, above, below)):
                    out[k] = dot(grad[0], wi[...], 1, 1)

    second, whole = (1, per, hid), (3, per, half)
    return kernel(
        "input_three",
        body,
        2,
        [(a, second, (1, 0, 0)) for a in (mine, above, below)] + [(wi, (half, hid), ("i", 0))],
        [(whole, F32, whole, (0, 0, 0))] * 2,
    )


def input_last(three, grad2, wi, pieces):
    per, hid = grad2.shape
    half = wi.shape[0] // 2
    width = half // pieces

    def body(own3, other3, grad, wi, own, *others):
        for k, at in ((0, 0), (1, 1), (2, 3)):
            rows = pl.ds(at * per, per)
            own[rows, :] = own3[k]
            for j, other in enumerate(others):
                other[rows, :] = other3[k, :, j * width : (j + 1) * width]
        part = dot(grad[...], wi[...], 1, 1)
        rows = pl.ds(2 * per, per)
        own[rows, :] = part[:, :half]
        for j, other in enumerate(others):
            other[rows, :] = part[:, half + j * width : half + (j + 1) * width]

    whole, part = (4 * per, half), (4 * per, width)
    own, *others = kernel(
        "input_last",
        body,
        1,
        [(a, a.shape, (0, 0, 0)) for a in three] + [(a, a.shape, (0, 0)) for a in (grad2, wi)],
        [(whole, F32, whole, (0, 0))] + [(part, F32, part, (0, 0))] * pieces,
    )
    return own, others


def return_pieces(name, mine, got, kinds):
    rows, feat = mine.shape
    width, pieces = got[0].shape[1], len(kinds)
    piece = rows // 4 // pieces

    def body(mine, *refs):
        for j, out in enumerate(refs[len(got) :]):
            for k in range(4):
                at = pl.ds((k * pieces + j) * piece, piece)
                for c, ref in enumerate(refs[: len(got)]):
                    columns = slice(c * width, (c + 1) * width)
                    out[k, :, columns] = (mine[at, columns] + ref[at, :]).astype(out.dtype)

    part = (4, piece, feat)
    return kernel(
        name,
        body,
        1,
        [(mine, (rows, feat), (0, 0))] + [(a, (rows, width), (0, 0)) for a in got],
        [(part, kind, part, (0, 0, 0)) for kind in kinds],
    )


def weight_grads(name, terms, sums=None, core=None):
    per, hid = terms[0][3].shape[-2:]
    feat = terms[0][0].shape[1]
    half, block, count = feat // 2, hid // STEPS, len(terms)
    rows, last = count * per, core is not None

    def body(*refs):
        refs = refs[1:] if last else refs
        given, refs = [refs[k * count : (k + 1) * count] for k in range(4)], refs[4 * count :]
        both = refs[-4:]

        @pl.when(pl.program_id(0) == 0)
        def _():
            for parts, out in zip(given[:2], both[:2]):
                for k, ref in enumerate(parts):
                    out[k * per : (k + 1) * per] = ref[...]

        for parts, out in zip(given[2:], both[2:]):
            for k, ref in enumerate(parts):
                out[k * per : (k + 1) * per] = ref[0] if len(ref.shape) == 3 else ref[...]
        tok, cot, act, grad = both
        wi = dot(tok[...], grad[...], 0, 0)
        wo = dot(act[...], cot[...], 0, 0)
        if sums is not None:
            wi, wo, refs = wi + refs[0][...], wo + refs[1][...], refs[2:]
        if last:
            refs[0][...] = wi[:half].astype(BF16)
            refs[1][...] = wo[:, :half].astype(BF16)
            refs[2][...] = wi[half:].astype(BF16)
            refs[3][...] = wo[:, half:].astype(BF16)
        else:
            refs[0][...] = wi
            refs[1][...] = wo

    def hidden_part(a, which):
        return (a, (1, per, block), (which, 0, "i")) if len(a.shape) == 3 else (a, (per, block), (0, "i"))

    ins = [(term[n], (per, feat), (term[2], 0)) for n in (0, 1) for term in terms]
    ins += [hidden_part(term[3 + which], which) for which in (0, 1) for term in terms]
    if sums is not None:
        ins += [(sums[0], (feat, block), (0, "i")), (sums[1], (block, feat), ("i", 0))]
    if last:
        at = lambda i, c: c * STEPS + i
        outs = [((half, 2 * hid), BF16, (half, block), (0, at)), ((2 * hid, half), BF16, (block, half), (at, 0))]
        outs += [((half, hid), BF16, (half, block), (0, "i")), ((hid, half), BF16, (block, half), ("i", 0))]
    else:
        outs = [((feat, hid), F32, (feat, block), (0, "i")), ((hid, feat), F32, (block, feat), ("i", 0))]
    scratch = [pltpu.VMEM((rows, feat), BF16)] * 2 + [pltpu.VMEM((rows, block), BF16)] * 2
    return kernel(name, body, STEPS, ins, outs, scratch, core)


def place(wi, wo, wi_got, wo_got, core):
    half, hid = wi_got.shape
    block = hid // STEPS

    def body(core, wi, wo, wi_got, wo_got, wi_out, wo_out):
        wi_out[...] = wi_got[...]
        wo_out[...] = wo_got[...]

    at = lambda i, c: (1 - c) * STEPS + i
    return kernel(
        "place",
        body,
        STEPS,
        [(wi, None, None), (wo, None, None), (wi_got, (half, block), (0, "i")), (wo_got, (block, half), ("i", 0))],
        [(wi.shape, BF16, (half, block), (0, at)), (wo.shape, BF16, (block, half), (at, 0))],
        scalar=core,
        aliases={1: 0, 2: 1},
    )


def local(tokens, cotangent, w_in, w_out):
    z, core = lax.axis_index("z"), lax.axis_index("core")
    rows, feat = tokens.shape
    hid = w_in.shape[1] // 2
    piece = rows // 4

    def relative(a, sign):
        return jnp.roll(a.reshape(4, piece, a.shape[-1]), sign * z, 0)

    def to_core(parts):
        return [shift(a, "core", 1) for a in parts]

    def up_down(up, down):
        return shift(up, "z", 1), shift(down, "z", -1)

    def send_mine(mine):
        return shift(mine, "z", -1), shift(mine, "z", 1)

    def send_on(above, below):
        act, grad = pass_on(above, below)
        return shift(act, "z", -1), shift(grad, "z", 1), act

    at_core = jnp.reshape(core, (1,)).astype(jnp.int32)
    own = relative(jnp.concatenate([tokens, cotangent], 1), -1)
    near = [own] + [shift(own, "y", -d) for d in (1, 2, 3)]
    across = shift(own, "xh", 1)
    packed = pack(*gate((w_in, w_out), own), at_core)
    got = shift(packed, "core", 1)
    near = join("join_a", near)[0]
    near_other = shift(near, "core", 1)
    across = gate(across, near)
    far = [shift(across, "y", -d) for d in (1, 2, 3)]
    across_other = shift(across, "core", 1)
    wi, wo = weights(w_in, w_out, gate(got, across_other), at_core)

    up_a, down_a = first_block(near, near_other, wi, wo)
    r_a = up_down(up_a, down_a)
    far = gate(far, up_a)
    far = join("join_b", [across, *far], [across_other, *to_core(far)])
    up_b, down_b = first_block(*far, wi, wo)
    r_b = up_down(up_b, down_b)

    near, near_other = gate((near, near_other), up_b)
    pg_a, tok_a, cot_a = products(near, near_other, wi, wo)
    m_a = ring_add(pg_a, *gate(r_a, pg_a))
    r_a = up_down(*m_a)
    pg_b, tok_b, cot_b = products(*gate(far, m_a), wi, wo)
    m_b = ring_add(pg_b, *gate(r_b, pg_b))
    r_b = up_down(*m_b)

    t_a, m_a = own_sum(pg_a, *gate(r_a, m_b))
    x_a = shift(m_a, "xl", 1)
    t_b, m_b = own_sum(pg_b, *gate(r_b, m_a))
    x_b = shift(m_b, "xl", 1)

    mine_a = hidden(t_a, gate(x_a, m_b))
    s_a = send_mine(mine_a)
    mine_b = hidden(t_b, gate(x_b, mine_a))
    s_b = send_mine(mine_b)

    s_a = gate(s_a, mine_b)
    *f_a, sent_a = send_on(*s_a)
    three_a = input_three(mine_a, *gate(s_a, sent_a), wi)
    terms = [(tok_a, cot_a, k, a, a) for k, a in zip((0, 1, 3), gate((mine_a, *s_a), three_a))]
    sums = weight_grads("grads_a", terms)

    s_b = gate(s_b, sums)
    *f_b, sent_b = send_on(*s_b)
    three_b = input_three(mine_b, *gate(s_b, sent_b), wi)
    terms = [(tok_b, cot_b, k, a, a) for k, a in zip((0, 1, 3), gate((mine_b, *s_b), three_b))]
    sums = weight_grads("grads_b", terms, sums)

    f_a = gate(f_a, sums)
    in_a, others = input_last(three_a, f_a[1], wi, 3)
    kept, *back = return_pieces("return_a", in_a, to_core(others), (F32, BF16, BF16, BF16))
    back = [shift(a, "y", d) for d, a in zip((1, 2, 3), back)]

    f_b = gate(f_b, kept)
    in_b, others = input_last(three_b, f_b[1], wi, 1)
    others_got = to_core(others)
    f_a, f_b = gate((f_a, f_b), others)
    terms = [(tok_a, cot_a, 2, *f_a), (tok_b, cot_b, 2, *f_b)]
    w_in_grad, w_out_grad, *others = weight_grads("grads_last", terms, sums, at_core)

    others_got, back = gate((others_got, back), others)
    far = return_pieces("return_b", in_b, others_got, (BF16,) * 4)
    got = to_core(gate(others, far))
    far = [
        lax.ppermute(a, ROWS, [(i, ((i // 2 + d) % 4) * 2 + (i + 1) % 2) for i in range(8)])
        for d, a in enumerate(far)
    ]
    w_in_grad, w_out_grad = place(w_in_grad, w_out_grad, *got, at_core)

    total = kept
    for part in back + gate(far, w_in_grad):
        total = total + part.astype(F32)
    input_grad = relative(total, 1).reshape(rows, feat).astype(BF16)
    return (input_grad, w_in_grad, w_out_grad)


def solution(mesh):
    fine = Mesh(mesh.devices.reshape(SIZES), AXES)
    return jax.shard_map(
        local,
        mesh=fine,
        in_specs=(P(ROWS, COLS), P(ROWS, COLS), P(COLS, ROWS), P(ROWS, COLS)),
        out_specs=(P(ROWS, COLS), P(COLS, ROWS), P(ROWS, COLS)),
        check_vma=False,
    )
```

```python
import jax
import jax.numpy as jnp
from jax import lax
from jax.experimental import pallas as pl
from jax.experimental.pallas import tpu as pltpu
from jax.sharding import Mesh
from jax.sharding import PartitionSpec as P

AXES = ("y", "xh", "xl", "z", "core")
SIZES = (4, 2, 2, 4, 2)
ROWS = ("y", "xh")
COLS = ("xl", "z", "core")
F32 = jnp.float32
BF16 = jnp.bfloat16
STEPS = 2


def gelu_parts(pre):
    cdf = 0.5 * (1.0 + lax.erf(pre * 0.7071067811865476))
    pdf = jnp.exp(-0.5 * pre * pre) * 0.3989422804014327
    return (cdf, pdf)


def shift(x, axis, by):
    n = SIZES[AXES.index(axis)]
    return lax.ppermute(x, axis, [(i, (i + by) % n) for i in range(n)])


def dot(a, b, da, db):
    return lax.dot_general(a, b, (((da,), (db,)), ((), ())), preferred_element_type=F32)


def gate(value, *after):
    return lax.optimization_barrier((value, after))[0]


COST = dict(pack=0.1, first_block=0.1, weights=7, join_a=100, join_b=0.1, products=0.1, ring_add=0.1, own_sum=0.1, hidden=0.1, pass_on=0.1, input_three=0.1, input_last=0.1, grads_a=0.1, grads_b=0.1, grads_last=0.1, return_a=0.1, return_b=20, place=0.1, finish=0.1)


def kernel(name, body, grid, ins, outs, scratch=(), scalar=None, aliases=None, vmem=24):
    def spec(block, index):
        if block is None:
            return pl.BlockSpec(memory_space=pltpu.HBM if index == "hbm" else pl.ANY)

        def at(i, *refs):
            return tuple(i if k == "i" else k(i, *(r[0] for r in refs)) if callable(k) else k for k in index)

        return pl.BlockSpec(block, at)

    return pl.pallas_call(
        body,
        name=name,
        grid_spec=pltpu.PrefetchScalarGridSpec(
            num_scalar_prefetch=0 if scalar is None else 1,
            grid=(grid,),
            in_specs=[spec(block, index) for _, block, index in ins],
            out_specs=[spec(block, index) for _, _, block, index in outs],
            scratch_shapes=list(scratch),
        ),
        out_shape=[jax.ShapeDtypeStruct(shape, dtype) for shape, dtype, _, _ in outs],
        input_output_aliases=aliases or {},
        cost_estimate=pl.CostEstimate(flops=int(COST[name] * 1.15e9), bytes_accessed=int(COST[name] * 3.69e6), transcendentals=0),
        compiler_params=pltpu.CompilerParams(vmem_limit_bytes=vmem * 2**20),
    )(*([] if scalar is None else [scalar]), *[a for a, _, _ in ins])


def pack(w_in, w_out, core):
    feat = w_in.shape[0]
    half = w_out.shape[0] // feat // 2
    steps = 2
    width = half // steps

    def body(_, wi, wo, out):
        for k in range(width):
            at = slice(k * feat, (k + 1) * feat)
            out[0, k] = wi[:, at]
            out[1, k] = wo[at, :]

    place = lambda i, c: (1 - c) * steps + i
    return kernel(
        "pack",
        body,
        steps,
        [(w_in, (feat, width * feat), (0, place)), (w_out, (width * feat, feat), (place, 0))],
        [((2, half, feat, feat), BF16, (2, width, feat, feat), (0, "i", 0, 0))],
        scalar=core,
        vmem=60,
    )[0]


def weights(w_in, w_out, got, core):
    feat = w_in.shape[0]
    half = w_out.shape[0] // feat // 2
    hid = half * feat

    def body(core, wi, wo, got, wi_out, wo_out, sems):
        mine = pl.ds(pl.multiple_of(core[0] * hid, hid), hid)
        copies = [
            pltpu.make_async_copy(wi.at[:, mine], wi_out.at[pl.ds(0, feat), :], sems.at[0, half]),
            pltpu.make_async_copy(wo.at[mine, :], wo_out.at[:, pl.ds(0, feat)], sems.at[1, half]),
        ]
        for k in range(half):
            at, other = pl.ds(k * feat, feat), pl.ds(feat, feat)
            copies.append(pltpu.make_async_copy(got.at[0, k], wi_out.at[other, at], sems.at[0, k]))
            copies.append(pltpu.make_async_copy(got.at[1, k], wo_out.at[at, other], sems.at[1, k]))
        for copy in copies:
            copy.start()
        for copy in copies:
            copy.wait()

    return kernel(
        "weights",
        body,
        1,
        [(w_in, None, "hbm"), (w_out, None, "hbm"), (got, None, None)],
        [((2 * feat, hid), BF16, None, None), ((hid, 2 * feat), BF16, None, None)],
        [pltpu.SemaphoreType.DMA((2, half + 1))],
        scalar=core,
    )


def pass_on(above, below):
    _, per, hid = above.shape

    def body(above, below, act, grad):
        act[...] = above[0]
        grad[...] = below[0]

    return kernel(
        "pass_on",
        body,
        1,
        [(above, (1, per, hid), (0, 0, 0)), (below, (1, per, hid), (1, 0, 0))],
        [((per, hid), BF16, (per, hid), (0, 0))] * 2,
    )


def join(name, *sides):
    zs, piece, width = sides[0][0].shape
    count = len(sides[0])
    per = count * piece

    def body(*refs):
        for n, out in enumerate(refs[len(sides) * count :]):
            for k in range(zs):
                for j in range(count):
                    out[pl.ds(k * per + j * piece, piece), :] = refs[n * count + j][k]

    return kernel(
        name,
        body,
        1,
        [(a, (zs, piece, width), (0, 0, 0)) for side in sides for a in side],
        [((zs * per, width), BF16, (zs * per, width), (0, 0))] * len(sides),
    )


def first_block(own, other, wi, wo):
    rows, width = own.shape
    feat, hid = wi.shape
    half, per, block = width // 2, rows // 4, hid // STEPS

    def body(own, other, wi, wo, up, down):
        tok = jnp.concatenate([own[:, :half], other[:, :half]], 1)
        cot = jnp.concatenate([own[:, half:], other[:, half:]], 1)
        up[...] = jnp.dot(tok, wi[...], preferred_element_type=F32).astype(BF16)
        down[...] = dot(cot, wo[...], 1, 1).astype(BF16)

    part = (per, width)
    return kernel(
        "first_block",
        body,
        STEPS,
        [(own, part, (2, 0)), (other, part, (2, 0)), (wi, (feat, block), (0, "i")), (wo, (block, feat), ("i", 0))],
        [((per, hid), BF16, (per, block), (0, "i"))] * 2,
    )


def products(own, other, wi, wo):
    rows, width = own.shape
    feat, hid = wi.shape
    half, block = width // 2, hid // STEPS

    def body(own, other, wi, wo, pg, tok, cot):
        @pl.when(pl.program_id(0) == 0)
        def _():
            for side, ref in enumerate((own, other)):
                tok[:, side * half : (side + 1) * half] = ref[:, :half]
                cot[:, side * half : (side + 1) * half] = ref[:, half:]

        p = jnp.dot(tok[...], wi[...], preferred_element_type=F32)
        g = dot(cot[...], wo[...], 1, 1)
        pg[0] = p
        pg[1] = g

    whole = (rows, width)
    return kernel(
        "products",
        body,
        STEPS,
        [(own, whole, (0, 0)), (other, whole, (0, 0)), (wi, (feat, block), (0, "i")), (wo, (block, feat), ("i", 0))],
        [
            ((2, rows, hid), F32, (2, rows, block), (0, 0, "i")),
            ((rows, feat), BF16, (rows, feat), (0, 0)),
            ((rows, feat), BF16, (rows, feat), (0, 0)),
        ],
    )


def ring_add(pg, up, down):
    per, hid = up.shape
    block = hid // STEPS

    def body(one, three, up, down, up_out, down_out):
        up_out[0] = (one[0] + up[...].astype(F32)).astype(BF16)
        up_out[1] = one[1].astype(BF16)
        down_out[0] = three[0].astype(BF16)
        down_out[1] = (three[1] + down[...].astype(F32)).astype(BF16)

    part = (2, per, block)
    return kernel(
        "ring_add",
        body,
        STEPS,
        [(pg, part, (0, 1, "i")), (pg, part, (0, 3, "i")), (up, (per, block), (0, "i")), (down, (per, block), (0, "i"))],
        [((2, per, hid), BF16, part, (0, 0, "i"))] * 2,
    )


def own_sum(pg, up, down):
    _, per, hid = up.shape
    part = (2, per, hid // STEPS)

    def body(zero, up, down, out, sent):
        total = zero[...] + up[...].astype(F32) + down[...].astype(F32)
        out[...] = total
        sent[...] = total.astype(BF16)

    return kernel(
        "own_sum",
        body,
        STEPS,
        [(pg, part, (0, 0, "i")), (up, part, (0, 0, "i")), (down, part, (0, 0, "i"))],
        [((2, per, hid), F32, part, (0, 0, "i")), ((2, per, hid), BF16, part, (0, 0, "i"))],
    )


def hidden(total, other):
    _, per, hid = total.shape
    part = (2, per, hid // STEPS)

    def body(total, other, out):
        pre = total[0] + other[0].astype(F32)
        act_grad = total[1] + other[1].astype(F32)
        cdf, pdf = gelu_parts(pre)
        out[0] = (pre * cdf).astype(BF16)
        out[1] = (act_grad * (cdf + pre * pdf)).astype(BF16)

    return kernel(
        "hidden",
        body,
        STEPS,
        [(total, part, (0, 0, "i")), (other, part, (0, 0, "i"))],
        [((2, per, hid), BF16, part, (0, 0, "i"))],
    )[0]


def input_three(mine, above, below, wi):
    _, per, hid = mine.shape
    half = wi.shape[0] // 2

    def body(mine, above, below, wi, own, other):
        for step, out in enumerate((own, other)):

            @pl.when(pl.program_id(0) == step)
            def _():
                for k, grad in enumerate((mine, above, below)):
                    out[k] = dot(grad[0], wi[...], 1, 1)

    second, whole = (1, per, hid), (3, per, half)
    return kernel(
        "input_three",
        body,
        2,
        [(a, second, (1, 0, 0)) for a in (mine, above, below)] + [(wi, (half, hid), ("i", 0))],
        [(whole, F32, whole, (0, 0, 0))] * 2,
    )


def input_last(three, grad2, wi, pieces):
    per, hid = grad2.shape
    half = wi.shape[0] // 2
    width = half // pieces

    def body(own3, other3, grad, wi, own, *others):
        for k, at in ((0, 0), (1, 1), (2, 3)):
            rows = pl.ds(at * per, per)
            own[rows, :] = own3[k]
            for j, other in enumerate(others):
                other[rows, :] = other3[k, :, j * width : (j + 1) * width]
        part = dot(grad[...], wi[...], 1, 1)
        rows = pl.ds(2 * per, per)
        own[rows, :] = part[:, :half]
        for j, other in enumerate(others):
            other[rows, :] = part[:, half + j * width : half + (j + 1) * width]

    whole, part = (4 * per, half), (4 * per, width)
    own, *others = kernel(
        "input_last",
        body,
        1,
        [(a, a.shape, (0, 0, 0)) for a in three] + [(a, a.shape, (0, 0)) for a in (grad2, wi)],
        [(whole, F32, whole, (0, 0))] + [(part, F32, part, (0, 0))] * pieces,
    )
    return own, others


def return_pieces(name, mine, got, kinds):
    rows, feat = mine.shape
    width, pieces = got[0].shape[1], len(kinds)
    piece = rows // 4 // pieces

    def body(mine, *refs):
        for j, out in enumerate(refs[len(got) :]):
            for k in range(4):
                at = pl.ds((k * pieces + j) * piece, piece)
                for c, ref in enumerate(refs[: len(got)]):
                    columns = slice(c * width, (c + 1) * width)
                    out[k, :, columns] = (mine[at, columns] + ref[at, :]).astype(out.dtype)

    part = (4, piece, feat)
    return kernel(
        name,
        body,
        1,
        [(mine, (rows, feat), (0, 0))] + [(a, (rows, width), (0, 0)) for a in got],
        [(part, kind, part, (0, 0, 0)) for kind in kinds],
    )


def weight_grads(name, terms, sums=None, core=None):
    per, hid = terms[0][3].shape[-2:]
    feat = terms[0][0].shape[1]
    half, block, count = feat // 2, hid // STEPS, len(terms)
    rows, last = count * per, core is not None

    def body(*refs):
        refs = refs[1:] if last else refs
        given, refs = [refs[k * count : (k + 1) * count] for k in range(4)], refs[4 * count :]
        both = refs[-4:]

        @pl.when(pl.program_id(0) == 0)
        def _():
            for parts, out in zip(given[:2], both[:2]):
                for k, ref in enumerate(parts):
                    out[k * per : (k + 1) * per] = ref[...]

        for parts, out in zip(given[2:], both[2:]):
            for k, ref in enumerate(parts):
                out[k * per : (k + 1) * per] = ref[0] if len(ref.shape) == 3 else ref[...]
        tok, cot, act, grad = both
        wi = dot(tok[...], grad[...], 0, 0)
        wo = dot(act[...], cot[...], 0, 0)
        if sums is not None:
            wi, wo, refs = wi + refs[0][...], wo + refs[1][...], refs[2:]
        if last:
            refs[0][...] = wi[:half].astype(BF16)
            refs[1][...] = wo[:, :half].astype(BF16)
            refs[2][...] = wi[half:].astype(BF16)
            refs[3][...] = wo[:, half:].astype(BF16)
        else:
            refs[0][...] = wi
            refs[1][...] = wo

    def hidden_part(a, which):
        return (a, (1, per, block), (which, 0, "i")) if len(a.shape) == 3 else (a, (per, block), (0, "i"))

    ins = [(term[n], (per, feat), (term[2], 0)) for n in (0, 1) for term in terms]
    ins += [hidden_part(term[3 + which], which) for which in (0, 1) for term in terms]
    if sums is not None:
        ins += [(sums[0], (feat, block), (0, "i")), (sums[1], (block, feat), ("i", 0))]
    if last:
        at = lambda i, c: c * STEPS + i
        outs = [((half, 2 * hid), BF16, (half, block), (0, at)), ((2 * hid, half), BF16, (block, half), (at, 0))]
        outs += [((half, hid), BF16, (half, block), (0, "i")), ((hid, half), BF16, (block, half), ("i", 0))]
    else:
        outs = [((feat, hid), F32, (feat, block), (0, "i")), ((hid, feat), F32, (block, feat), ("i", 0))]
    scratch = [pltpu.VMEM((rows, feat), BF16)] * 2 + [pltpu.VMEM((rows, block), BF16)] * 2
    return kernel(name, body, STEPS, ins, outs, scratch, core)


def place(wi, wo, wi_got, wo_got, core):
    half, hid = wi_got.shape
    block = hid // STEPS

    def body(core, wi, wo, wi_got, wo_got, wi_out, wo_out):
        wi_out[...] = wi_got[...]
        wo_out[...] = wo_got[...]

    at = lambda i, c: (1 - c) * STEPS + i
    return kernel(
        "place",
        body,
        STEPS,
        [(wi, None, None), (wo, None, None), (wi_got, (half, block), (0, "i")), (wo_got, (block, half), ("i", 0))],
        [(wi.shape, BF16, (half, block), (0, at)), (wo.shape, BF16, (block, half), (at, 0))],
        scalar=core,
        aliases={1: 0, 2: 1},
    )


def finish(parts, z):
    shape = parts[0].shape

    def body(z, *refs):
        for k in range(shape[0]):
            at = (k + shape[0] - z[0]) % shape[0]
            total = refs[0][at]
            for ref in refs[1:-1]:
                total = total + ref[at].astype(F32)
            refs[-1][k] = total.astype(BF16)

    ins = [(a, shape, (0, 0, 0)) for a in parts]
    return kernel("finish", body, 1, ins, [(shape, BF16, shape, (0, 0, 0))], scalar=z)[0]


def local(tokens, cotangent, w_in, w_out):
    z, core = lax.axis_index("z"), lax.axis_index("core")
    rows, feat = tokens.shape
    hid = w_in.shape[1] // 2
    piece = rows // 4

    def relative(a, sign):
        return jnp.roll(a.reshape(4, piece, a.shape[-1]), sign * z, 0)

    def to_core(parts):
        return [shift(a, "core", 1) for a in parts]

    def up_down(up, down):
        return shift(up, "z", 1), shift(down, "z", -1)

    def send_mine(mine):
        return shift(mine, "z", -1), shift(mine, "z", 1)

    def send_on(above, below):
        act, grad = pass_on(above, below)
        return shift(act, "z", -1), shift(grad, "z", 1), act

    at_core = jnp.reshape(core, (1,)).astype(jnp.int32)
    own = relative(jnp.concatenate([tokens, cotangent], 1), -1)
    near = [own] + [shift(own, "y", -d) for d in (1, 2, 3)]
    across = shift(own, "xh", 1)
    packed = pack(*gate((w_in, w_out), own), at_core)
    got = shift(packed, "core", 1)
    near = join("join_a", near)[0]
    near_other = shift(near, "core", 1)
    across = gate(across, near)
    far = [shift(across, "y", -d) for d in (1, 2, 3)]
    across_other = shift(across, "core", 1)
    wi, wo = weights(w_in, w_out, gate(got, across_other), at_core)

    up_a, down_a = first_block(near, near_other, wi, wo)
    r_a = up_down(up_a, down_a)
    far = gate(far, up_a)
    far = join("join_b", [across, *far], [across_other, *to_core(far)])
    up_b, down_b = first_block(*far, wi, wo)
    r_b = up_down(up_b, down_b)

    near, near_other = gate((near, near_other), up_b)
    pg_a, tok_a, cot_a = products(near, near_other, wi, wo)
    m_a = ring_add(pg_a, *gate(r_a, pg_a))
    r_a = up_down(*m_a)
    pg_b, tok_b, cot_b = products(*gate(far, m_a), wi, wo)
    m_b = ring_add(pg_b, *gate(r_b, pg_b))
    r_b = up_down(*m_b)

    t_a, m_a = own_sum(pg_a, *gate(r_a, m_b))
    x_a = shift(m_a, "xl", 1)
    t_b, m_b = own_sum(pg_b, *gate(r_b, m_a))
    x_b = shift(m_b, "xl", 1)

    mine_a = hidden(t_a, gate(x_a, m_b))
    s_a = send_mine(mine_a)
    mine_b = hidden(t_b, gate(x_b, mine_a))
    s_b = send_mine(mine_b)

    s_a = gate(s_a, mine_b)
    *f_a, sent_a = send_on(*s_a)
    three_a = input_three(mine_a, *gate(s_a, sent_a), wi)
    terms = [(tok_a, cot_a, k, a, a) for k, a in zip((0, 1, 3), gate((mine_a, *s_a), three_a))]
    sums = weight_grads("grads_a", terms)

    s_b = gate(s_b, sums)
    *f_b, sent_b = send_on(*s_b)
    three_b = input_three(mine_b, *gate(s_b, sent_b), wi)
    terms = [(tok_b, cot_b, k, a, a) for k, a in zip((0, 1, 3), gate((mine_b, *s_b), three_b))]
    sums = weight_grads("grads_b", terms, sums)

    f_a = gate(f_a, sums)
    in_a, others = input_last(three_a, f_a[1], wi, 3)
    kept, *back = return_pieces("return_a", in_a, to_core(others), (F32, BF16, BF16, BF16))
    back = [shift(a, "y", d) for d, a in zip((1, 2, 3), back)]

    f_b = gate(f_b, kept)
    in_b, others = input_last(three_b, f_b[1], wi, 1)
    others_got = to_core(others)
    f_a, f_b = gate((f_a, f_b), others)
    terms = [(tok_a, cot_a, 2, *f_a), (tok_b, cot_b, 2, *f_b)]
    w_in_grad, w_out_grad, *others = weight_grads("grads_last", terms, sums, at_core)

    others_got, back = gate((others_got, back), others)
    far = return_pieces("return_b", in_b, others_got, (BF16,) * 4)
    got = to_core(gate(others, far))
    far = [
        lax.ppermute(a, ROWS, [(i, ((i // 2 + d) % 4) * 2 + (i + 1) % 2) for i in range(8)])
        for d, a in enumerate(far)
    ]
    w_in_grad, w_out_grad = place(w_in_grad, w_out_grad, *got, at_core)

    parts = [kept, *back, *gate(far, w_in_grad)]
    input_grad = finish(parts, jnp.reshape(z, (1,)).astype(jnp.int32)).reshape(rows, feat)
    return (input_grad, w_in_grad, w_out_grad)


def solution(mesh):
    fine = Mesh(mesh.devices.reshape(SIZES), AXES)
    return jax.shard_map(
        local,
        mesh=fine,
        in_specs=(P(ROWS, COLS), P(ROWS, COLS), P(COLS, ROWS), P(ROWS, COLS)),
        out_specs=(P(ROWS, COLS), P(COLS, ROWS), P(ROWS, COLS)),
        check_vma=False,
    )
```

```python
import jax
import jax.numpy as jnp
from jax import lax
from jax.experimental import pallas as pl
from jax.experimental.pallas import tpu as pltpu
from jax.sharding import Mesh
from jax.sharding import PartitionSpec as P

AXES = ("y", "xh", "xl", "z", "core")
SIZES = (4, 2, 2, 4, 2)
ROWS = ("y", "xh")
COLS = ("xl", "z", "core")
F32 = jnp.float32
BF16 = jnp.bfloat16
STEPS = 2


def gelu_parts(pre):
    cdf = 0.5 * (1.0 + lax.erf(pre * 0.7071067811865476))
    pdf = jnp.exp(-0.5 * pre * pre) * 0.3989422804014327
    return (cdf, pdf)


def shift(x, axis, by):
    n = SIZES[AXES.index(axis)]
    return lax.ppermute(x, axis, [(i, (i + by) % n) for i in range(n)])


def dot(a, b, da, db):
    return lax.dot_general(a, b, (((da,), (db,)), ((), ())), preferred_element_type=F32)


def gate(value, *after):
    return lax.optimization_barrier((value, after))[0]


COST = dict(pack=0.1, first_block=0.1, weights=7, join_a=100, join_b=0.1, products=0.1, ring_add=0.1, own_sum=0.1, hidden=0.1, pass_on=0.1, input_three=0.1, input_last=0.1, grads_a=0.1, grads_b=0.1, grads_last=0.1, return_a=0.1, return_b=20, place=0.1, finish=0.1)


def kernel(name, body, grid, ins, outs, scratch=(), scalar=None, aliases=None, vmem=24):
    def spec(block, index):
        if block is None:
            return pl.BlockSpec(memory_space=pltpu.HBM if index == "hbm" else pl.ANY)

        def at(i, *refs):
            return tuple(i if k == "i" else k(i, *(r[0] for r in refs)) if callable(k) else k for k in index)

        return pl.BlockSpec(block, at)

    return pl.pallas_call(
        body,
        name=name,
        grid_spec=pltpu.PrefetchScalarGridSpec(
            num_scalar_prefetch=0 if scalar is None else 1,
            grid=(grid,),
            in_specs=[spec(block, index) for _, block, index in ins],
            out_specs=[spec(block, index) for _, _, block, index in outs],
            scratch_shapes=list(scratch),
        ),
        out_shape=[jax.ShapeDtypeStruct(shape, dtype) for shape, dtype, _, _ in outs],
        input_output_aliases=aliases or {},
        cost_estimate=pl.CostEstimate(flops=int(COST[name] * 1.15e9), bytes_accessed=int(COST[name] * 3.69e6), transcendentals=0),
        compiler_params=pltpu.CompilerParams(vmem_limit_bytes=vmem * 2**20),
    )(*([] if scalar is None else [scalar]), *[a for a, _, _ in ins])


def pack(w_in, w_out, core):
    feat = w_in.shape[0]
    half = w_out.shape[0] // feat // 2
    steps = 2
    width = half // steps

    def body(_, wi, wo, out):
        for k in range(width):
            at = slice(k * feat, (k + 1) * feat)
            out[0, k] = wi[:, at]
            out[1, k] = wo[at, :]

    place = lambda i, c: (1 - c) * steps + i
    return kernel(
        "pack",
        body,
        steps,
        [(w_in, (feat, width * feat), (0, place)), (w_out, (width * feat, feat), (place, 0))],
        [((2, half, feat, feat), BF16, (2, width, feat, feat), (0, "i", 0, 0))],
        scalar=core,
        vmem=60,
    )[0]


def weights(w_in, w_out, got, core):
    feat = w_in.shape[0]
    half = w_out.shape[0] // feat // 2
    hid = half * feat

    def body(core, wi, wo, got, wi_out, wo_out, sems):
        mine = pl.ds(pl.multiple_of(core[0] * hid, hid), hid)
        copies = [
            pltpu.make_async_copy(wi.at[:, mine], wi_out.at[pl.ds(0, feat), :], sems.at[0, half]),
            pltpu.make_async_copy(wo.at[mine, :], wo_out.at[:, pl.ds(0, feat)], sems.at[1, half]),
        ]
        for k in range(half):
            at, other = pl.ds(k * feat, feat), pl.ds(feat, feat)
            copies.append(pltpu.make_async_copy(got.at[0, k], wi_out.at[other, at], sems.at[0, k]))
            copies.append(pltpu.make_async_copy(got.at[1, k], wo_out.at[at, other], sems.at[1, k]))
        for copy in copies:
            copy.start()
        for copy in copies:
            copy.wait()

    return kernel(
        "weights",
        body,
        1,
        [(w_in, None, "hbm"), (w_out, None, "hbm"), (got, None, None)],
        [((2 * feat, hid), BF16, None, None), ((hid, 2 * feat), BF16, None, None)],
        [pltpu.SemaphoreType.DMA((2, half + 1))],
        scalar=core,
    )


def pass_on(above, below):
    _, per, hid = above.shape

    def body(above, below, act, grad):
        act[...] = above[0]
        grad[...] = below[0]

    return kernel(
        "pass_on",
        body,
        1,
        [(above, (1, per, hid), (0, 0, 0)), (below, (1, per, hid), (1, 0, 0))],
        [((per, hid), BF16, (per, hid), (0, 0))] * 2,
    )


def join(name, *sides):
    zs, piece, width = sides[0][0].shape
    count = len(sides[0])
    per = count * piece

    def body(*refs):
        for n, out in enumerate(refs[len(sides) * count :]):
            for k in range(zs):
                for j in range(count):
                    out[pl.ds(k * per + j * piece, piece), :] = refs[n * count + j][k]

    return kernel(
        name,
        body,
        1,
        [(a, (zs, piece, width), (0, 0, 0)) for side in sides for a in side],
        [((zs * per, width), BF16, (zs * per, width), (0, 0))] * len(sides),
    )


def first_block(own, other, wi, wo):
    rows, width = own.shape
    feat, hid = wi.shape
    half, per, block = width // 2, rows // 4, hid // STEPS

    def body(own, other, wi, wo, up, down):
        tok = jnp.concatenate([own[:, :half], other[:, :half]], 1)
        cot = jnp.concatenate([own[:, half:], other[:, half:]], 1)
        up[...] = jnp.dot(tok, wi[...], preferred_element_type=F32).astype(BF16)
        down[...] = dot(cot, wo[...], 1, 1).astype(BF16)

    part = (per, width)
    return kernel(
        "first_block",
        body,
        STEPS,
        [(own, part, (2, 0)), (other, part, (2, 0)), (wi, (feat, block), (0, "i")), (wo, (block, feat), ("i", 0))],
        [((per, hid), BF16, (per, block), (0, "i"))] * 2,
    )


def products(own, other, wi, wo):
    rows, width = own.shape
    feat, hid = wi.shape
    half, block = width // 2, hid // STEPS

    def body(own, other, wi, wo, pg, tok, cot):
        @pl.when(pl.program_id(0) == 0)
        def _():
            for side, ref in enumerate((own, other)):
                tok[:, side * half : (side + 1) * half] = ref[:, :half]
                cot[:, side * half : (side + 1) * half] = ref[:, half:]

        p = jnp.dot(tok[...], wi[...], preferred_element_type=F32)
        g = dot(cot[...], wo[...], 1, 1)
        pg[0] = p
        pg[1] = g

    whole = (rows, width)
    return kernel(
        "products",
        body,
        STEPS,
        [(own, whole, (0, 0)), (other, whole, (0, 0)), (wi, (feat, block), (0, "i")), (wo, (block, feat), ("i", 0))],
        [
            ((2, rows, hid), F32, (2, rows, block), (0, 0, "i")),
            ((rows, feat), BF16, (rows, feat), (0, 0)),
            ((rows, feat), BF16, (rows, feat), (0, 0)),
        ],
    )


def ring_add(pg, up, down):
    per, hid = up.shape
    block = hid // STEPS

    def body(one, three, up, down, up_out, down_out):
        up_out[0] = (one[0] + up[...].astype(F32)).astype(BF16)
        up_out[1] = one[1].astype(BF16)
        down_out[0] = three[0].astype(BF16)
        down_out[1] = (three[1] + down[...].astype(F32)).astype(BF16)

    part = (2, per, block)
    return kernel(
        "ring_add",
        body,
        STEPS,
        [(pg, part, (0, 1, "i")), (pg, part, (0, 3, "i")), (up, (per, block), (0, "i")), (down, (per, block), (0, "i"))],
        [((2, per, hid), BF16, part, (0, 0, "i"))] * 2,
    )


def own_sum(pg, up, down):
    _, per, hid = up.shape
    part = (2, per, hid // STEPS)

    def body(zero, up, down, out, sent):
        total = zero[...] + up[...].astype(F32) + down[...].astype(F32)
        out[...] = total
        sent[...] = total.astype(BF16)

    return kernel(
        "own_sum",
        body,
        STEPS,
        [(pg, part, (0, 0, "i")), (up, part, (0, 0, "i")), (down, part, (0, 0, "i"))],
        [((2, per, hid), F32, part, (0, 0, "i")), ((2, per, hid), BF16, part, (0, 0, "i"))],
    )


def hidden(total, other):
    _, per, hid = total.shape
    part = (2, per, hid // STEPS)

    def body(total, other, out):
        pre = total[0] + other[0].astype(F32)
        act_grad = total[1] + other[1].astype(F32)
        cdf, pdf = gelu_parts(pre)
        out[0] = (pre * cdf).astype(BF16)
        out[1] = (act_grad * (cdf + pre * pdf)).astype(BF16)

    return kernel(
        "hidden",
        body,
        STEPS,
        [(total, part, (0, 0, "i")), (other, part, (0, 0, "i"))],
        [((2, per, hid), BF16, part, (0, 0, "i"))],
    )[0]


def input_three(mine, above, below, wi):
    _, per, hid = mine.shape
    half = wi.shape[0] // 2

    def body(mine, above, below, wi, own, other):
        for step, out in enumerate((own, other)):

            @pl.when(pl.program_id(0) == step)
            def _():
                for k, grad in enumerate((mine, above, below)):
                    out[k] = dot(grad[0], wi[...], 1, 1)

    second, whole = (1, per, hid), (3, per, half)
    return kernel(
        "input_three",
        body,
        2,
        [(a, second, (1, 0, 0)) for a in (mine, above, below)] + [(wi, (half, hid), ("i", 0))],
        [(whole, F32, whole, (0, 0, 0))] * 2,
    )


def input_last(three, grad2, wi, pieces):
    per, hid = grad2.shape
    half = wi.shape[0] // 2
    width = half // pieces

    def body(own3, other3, grad, wi, own, *others):
        for k, at in ((0, 0), (1, 1), (2, 3)):
            rows = pl.ds(at * per, per)
            own[rows, :] = own3[k]
            for j, other in enumerate(others):
                other[rows, :] = other3[k, :, j * width : (j + 1) * width]
        part = dot(grad[...], wi[...], 1, 1)
        rows = pl.ds(2 * per, per)
        own[rows, :] = part[:, :half]
        for j, other in enumerate(others):
            other[rows, :] = part[:, half + j * width : half + (j + 1) * width]

    whole, part = (4 * per, half), (4 * per, width)
    own, *others = kernel(
        "input_last",
        body,
        1,
        [(a, a.shape, (0, 0, 0)) for a in three] + [(a, a.shape, (0, 0)) for a in (grad2, wi)],
        [(whole, F32, whole, (0, 0))] + [(part, F32, part, (0, 0))] * pieces,
    )
    return own, others


def return_pieces(name, mine, got, kinds):
    rows, feat = mine.shape
    width, pieces = got[0].shape[1], len(kinds)
    piece = rows // 4 // pieces

    def body(mine, *refs):
        for j, out in enumerate(refs[len(got) :]):
            for k in range(4):
                at = pl.ds((k * pieces + j) * piece, piece)
                for c, ref in enumerate(refs[: len(got)]):
                    columns = slice(c * width, (c + 1) * width)
                    out[k, :, columns] = (mine[at, columns] + ref[at, :]).astype(out.dtype)

    part = (4, piece, feat)
    return kernel(
        name,
        body,
        1,
        [(mine, (rows, feat), (0, 0))] + [(a, (rows, width), (0, 0)) for a in got],
        [(part, kind, part, (0, 0, 0)) for kind in kinds],
    )


def weight_grads(name, terms, sums=None, core=None):
    per, hid = terms[0][3].shape[-2:]
    feat = terms[0][0].shape[1]
    half, block, count = feat // 2, hid // STEPS, len(terms)
    rows, last = count * per, core is not None

    def body(*refs):
        refs = refs[1:] if last else refs
        given, refs = [refs[k * count : (k + 1) * count] for k in range(4)], refs[4 * count :]
        both = refs[-4:]

        @pl.when(pl.program_id(0) == 0)
        def _():
            for parts, out in zip(given[:2], both[:2]):
                for k, ref in enumerate(parts):
                    out[k * per : (k + 1) * per] = ref[...]

        for parts, out in zip(given[2:], both[2:]):
            for k, ref in enumerate(parts):
                out[k * per : (k + 1) * per] = ref[0] if len(ref.shape) == 3 else ref[...]
        tok, cot, act, grad = both
        wi = dot(tok[...], grad[...], 0, 0)
        wo = dot(act[...], cot[...], 0, 0)
        if sums is not None:
            wi, wo, refs = wi + refs[0][...], wo + refs[1][...], refs[2:]
        if last:
            refs[0][...] = wi[:half].astype(BF16)
            refs[1][...] = wo[:, :half].astype(BF16)
            refs[2][...] = wi[half:].astype(BF16)
            refs[3][...] = wo[:, half:].astype(BF16)
        else:
            refs[0][...] = wi
            refs[1][...] = wo

    def hidden_part(a, which):
        return (a, (1, per, block), (which, 0, "i")) if len(a.shape) == 3 else (a, (per, block), (0, "i"))

    ins = [(term[n], (per, feat), (term[2], 0)) for n in (0, 1) for term in terms]
    ins += [hidden_part(term[3 + which], which) for which in (0, 1) for term in terms]
    if sums is not None:
        ins += [(sums[0], (feat, block), (0, "i")), (sums[1], (block, feat), ("i", 0))]
    if last:
        at = lambda i, c: c * STEPS + i
        outs = [((half, 2 * hid), BF16, (half, block), (0, at)), ((2 * hid, half), BF16, (block, half), (at, 0))]
        outs += [((half, hid), BF16, (half, block), (0, "i")), ((hid, half), BF16, (block, half), ("i", 0))]
    else:
        outs = [((feat, hid), F32, (feat, block), (0, "i")), ((hid, feat), F32, (block, feat), ("i", 0))]
    scratch = [pltpu.VMEM((rows, feat), BF16)] * 2 + [pltpu.VMEM((rows, block), BF16)] * 2
    return kernel(name, body, STEPS, ins, outs, scratch, core)


def place(wi, wo, wi_got, wo_got, core):
    half, hid = wi_got.shape
    block = hid // STEPS

    def body(core, wi, wo, wi_got, wo_got, wi_out, wo_out):
        wi_out[...] = wi_got[...]
        wo_out[...] = wo_got[...]

    at = lambda i, c: (1 - c) * STEPS + i
    return kernel(
        "place",
        body,
        STEPS,
        [(wi, None, None), (wo, None, None), (wi_got, (half, block), (0, "i")), (wo_got, (block, half), ("i", 0))],
        [(wi.shape, BF16, (half, block), (0, at)), (wo.shape, BF16, (block, half), (at, 0))],
        scalar=core,
        aliases={1: 0, 2: 1},
    )


def finish(parts, z):
    shape = parts[0].shape

    def body(z, *refs):
        for k in range(shape[0]):
            at = (k + shape[0] - z[0]) % shape[0]
            total = refs[0][at]
            for ref in refs[1:-1]:
                total = total + ref[at].astype(F32)
            refs[-1][k] = total.astype(BF16)

    ins = [(a, shape, (0, 0, 0)) for a in parts]
    return kernel("finish", body, 1, ins, [(shape, BF16, shape, (0, 0, 0))], scalar=z)[0]


def local(tokens, cotangent, w_in, w_out):
    z, core = lax.axis_index("z"), lax.axis_index("core")
    rows, feat = tokens.shape
    hid = w_in.shape[1] // 2
    piece = rows // 4

    def relative(a, sign):
        return jnp.roll(a.reshape(4, piece, a.shape[-1]), sign * z, 0)

    def to_core(parts):
        return [shift(a, "core", 1) for a in parts]

    def up_down(up, down):
        return shift(up, "z", 1), shift(down, "z", -1)

    def send_mine(mine):
        return shift(mine, "z", -1), shift(mine, "z", 1)

    def send_on(above, below):
        act, grad = pass_on(above, below)
        return shift(act, "z", -1), shift(grad, "z", 1), act

    at_core = jnp.reshape(core, (1,)).astype(jnp.int32)
    own = relative(jnp.concatenate([tokens, cotangent], 1), -1)
    near = [own] + [shift(own, "y", -d) for d in (1, 2, 3)]
    across = shift(own, "xh", 1)
    packed = pack(*gate((w_in, w_out), own), at_core)
    got = shift(packed, "core", 1)
    near = join("join_a", near)[0]
    near_other = shift(near, "core", 1)
    across = gate(across, near)
    far = [shift(across, "y", -d) for d in (1, 2, 3)]
    across_other = shift(across, "core", 1)
    wi, wo = weights(w_in, w_out, gate(got, across_other), at_core)

    up_a, down_a = first_block(near, near_other, wi, wo)
    r_a = up_down(up_a, down_a)
    far = gate(far, up_a)
    far = join("join_b", [across, *far], [across_other, *to_core(far)])
    up_b, down_b = first_block(*far, wi, wo)
    r_b = up_down(up_b, down_b)

    near, near_other = gate((near, near_other), up_b)
    pg_a, tok_a, cot_a = products(near, near_other, wi, wo)
    m_a = ring_add(pg_a, *gate(r_a, pg_a))
    r_a = up_down(*m_a)
    pg_b, tok_b, cot_b = products(*gate(far, m_a), wi, wo)
    m_b = ring_add(pg_b, *gate(r_b, pg_b))
    r_b = up_down(*m_b)

    t_a, m_a = own_sum(pg_a, *gate(r_a, m_b))
    x_a = shift(m_a, "xl", 1)
    t_b, m_b = own_sum(pg_b, *gate(r_b, m_a))
    x_b = shift(m_b, "xl", 1)

    mine_a = hidden(t_a, gate(x_a, m_b))
    s_a = send_mine(mine_a)
    mine_b = hidden(t_b, gate(x_b, mine_a))
    s_b = send_mine(mine_b)

    s_a = gate(s_a, mine_b)
    *f_a, sent_a = send_on(*s_a)
    three_a = input_three(mine_a, *gate(s_a, sent_a), wi)
    terms = [(tok_a, cot_a, k, a, a) for k, a in zip((0, 1, 3), gate((mine_a, *s_a), three_a))]
    sums = weight_grads("grads_a", terms)

    s_b = gate(s_b, sums)
    *f_b, sent_b = send_on(*s_b)
    three_b = input_three(mine_b, *gate(s_b, sent_b), wi)
    terms = [(tok_b, cot_b, k, a, a) for k, a in zip((0, 1, 3), gate((mine_b, *s_b), three_b))]
    sums = weight_grads("grads_b", terms, sums)

    f_a = gate(f_a, sums)
    in_a, others = input_last(three_a, f_a[1], wi, 3)
    kept, *back = return_pieces("return_a", in_a, to_core(others), (F32, BF16, BF16, BF16))
    back = [shift(a, "y", d) for d, a in zip((1, 2, 3), back)]

    f_b = gate(f_b, kept)
    in_b, others = input_last(three_b, f_b[1], wi, 1)
    others_got = to_core(others)
    f_a, f_b = gate((f_a, f_b), others)
    terms = [(tok_a, cot_a, 2, *f_a), (tok_b, cot_b, 2, *f_b)]
    w_in_grad, w_out_grad, *others = weight_grads("grads_last", terms, sums, at_core)

    others_got, back = gate((others_got, back), others)
    far = return_pieces("return_b", in_b, others_got, (BF16,) * 4)
    got = to_core(gate(others, far))
    far = [
        lax.ppermute(a, ROWS, [(i, ((i // 2 + d) % 4) * 2 + (i + 1) % 2) for i in range(8)])
        for d, a in sorted(enumerate(far), key=lambda pair: (2, 1, 3, 0).index(pair[0]))
    ]
    w_in_grad, w_out_grad = place(w_in_grad, w_out_grad, *got, at_core)

    parts = [kept, *back, *gate(far, w_in_grad)]
    input_grad = finish(parts, jnp.reshape(z, (1,)).astype(jnp.int32)).reshape(rows, feat)
    return (input_grad, w_in_grad, w_out_grad)


def solution(mesh):
    fine = Mesh(mesh.devices.reshape(SIZES), AXES)
    return jax.shard_map(
        local,
        mesh=fine,
        in_specs=(P(ROWS, COLS), P(ROWS, COLS), P(COLS, ROWS), P(ROWS, COLS)),
        out_specs=(P(ROWS, COLS), P(COLS, ROWS), P(ROWS, COLS)),
        check_vma=False,
    )
```
